512 devices in a mesh: tm: 16 (over y, core), space: 32 (over z, x).
Axes of the slice: x: 4, y: 8, z: 8, core: 2. Of those that a mesh axis runs over, the one named last changes fastest.
Arguments:
- right_side: float32 [128, 256, 1024], P('tm', 'space'), may hold values from -50 to 50
- kappa: float32 [256, 1024], P('space'), may hold values from 0.05 to 1
- velocity: int32 [2, 256, 1024], P(None, 'space'), may hold values from -2 to 2
Outputs:
- solution: float32 [128, 256, 1024], P('tm', 'space')
- residual: float32 [128, 256, 1024], P('tm', 'space')
The draws below stay inside these ranges and needn't reach their ends.
All inputs are finite; a program needn't handle non-finite values.
Results may differ from the reference program's by a relative error of at most 0.013.
Values sent between devices are 32-bit elements; how exact they have to be, the bound alone decides.
No kernel may reach another device: no remote copies, remote signals or barrier semaphores. Data moves between devices by JAX's collectives and lax.ppermute only.
A program may use at most 64 MiB of HBM per device.

```python
import math
import jax
import jax.numpy as jnp
from jax import lax

CHEB = 4
ITERS = 2
NT = 128
NX = 256
NY = 1024


def draw_right_side(key, part):
    key = jax.random.fold_in(key, 11)
    time_pos = jnp.arange(NT, dtype=jnp.float32) / NT
    row_pos = jnp.arange(NX, dtype=jnp.float32) / NX
    base = jax.random.truncated_normal(key, -4.0, 4.0, (NT, NX, NY), jnp.float32)
    power = 0.5
    scale = 10.0 ** (power * (time_pos[:, None, None] + row_pos[None, :, None]))
    return (base * scale).astype(jnp.float32)


def with_ends(entries, key, low, largest):
    spot = [jax.random.randint(jax.random.fold_in(key, axis), (), 0, length) for axis, length in enumerate(entries.shape)]
    main_axis = entries.shape.index(max(entries.shape))
    neighbour = spot[:main_axis] + [(spot[main_axis] + 1) % entries.shape[main_axis]] + spot[main_axis + 1:]
    return entries.at[tuple(spot)].set(low).at[tuple(neighbour)].set(largest)


def shard_levels(rng, extent, split, least, largest):
    level = 1.0
    for dim, blocks in split:
        steps = jax.random.uniform(jax.random.fold_in(jax.random.fold_in(rng, 6), dim), (blocks,), jnp.float32, least / len(split), largest / len(split))
        level = level * jnp.repeat(jnp.exp(steps), extent[dim] // blocks).reshape((-1,) + (1,) * (len(extent) - 1 - dim))
    return level


def setup_inputs(seed: int = 0) -> dict:
    keys = jax.random.split(jax.random.key(seed), 4)
    right_side = draw_right_side(jax.random.fold_in(keys[3], 71), 0)
    kappa = jnp.clip(jnp.exp(math.log(1.0) - 2.9957323 * jax.random.uniform(keys[1], (NX, NY), jnp.float32) ** shard_levels(keys[1], (NX, NY), ((0, 32),), -0.2, 0.2)), 0.05, 1.0)
    velocity = with_ends(jax.random.randint(keys[2], (2, NX, NY), -2, 3), jax.random.fold_in(keys[2], 1), -2, 2).astype(jnp.int32)
    return {"right_side": right_side, "kappa": kappa, "velocity": velocity}


time_coupling = 2.0
kappa_low = 0.05
kappa_high = 1.0
stencil_reach = 16.0

def hartley_table(length):
    index = jnp.arange(length, dtype=jnp.int32)
    product = index[:, None] * index[None, :] % length
    angle = product.astype(jnp.float32) * (2.0 * math.pi / length)
    return (jnp.cos(angle) + jnp.sin(angle)) / math.sqrt(length)

def spectral_shift(length):
    index = jnp.arange(length, dtype=jnp.int32)
    angle = index.astype(jnp.float32) * (2.0 * math.pi / length)
    return (time_coupling * (2.0 - 2.0 * jnp.cos(angle))).reshape(length, 1, 1)

def transform(cas_table, field):
    return jnp.einsum('kt,txy->kxy', cas_table, field, precision=lax.Precision.HIGHEST)

def chebyshev(source, freq_shift, apply_space):
    half_width = 0.5 * (kappa_high + stencil_reach - kappa_low)
    middle = 0.5 * (kappa_low + kappa_high + stencil_reach) + freq_shift
    spread_ratio = middle / half_width
    damping = 1.0 / spread_ratio
    step_dir = source / middle
    solved = jnp.zeros_like(source)
    remain = source
    for _ in range(CHEB):
        solved = solved + step_dir
        remain = remain - (apply_space(step_dir) + freq_shift * step_dir)
        damp_next = 1.0 / (2.0 * spread_ratio - damping)
        step_dir = damp_next * damping * step_dir + 2.0 * damp_next / half_width * remain
        damping = damp_next
    return solved + step_dir

def edge_weights(kappa, velocity):
    squares = velocity.astype(jnp.float32) ** 2
    east_edge = 1.0 + 0.125 * (squares[0] + jnp.roll(squares[0], -1, 0))
    west_edge = jnp.roll(east_edge, 1, 0)
    north_edge = 1.0 + 0.125 * (squares[1] + jnp.roll(squares[1], -1, 1))
    south_edge = jnp.roll(north_edge, 1, 1)
    centre = kappa + east_edge + west_edge + north_edge + south_edge
    return (centre, east_edge, west_edge, north_edge, south_edge)

def reference(right_side, kappa, velocity):
    centre, east_edge, west_edge, north_edge, south_edge = edge_weights(kappa, velocity)

    def apply_space(field):
        return centre * field - east_edge * jnp.roll(field, -1, 1) - west_edge * jnp.roll(field, 1, 1) - north_edge * jnp.roll(field, -1, 2) - south_edge * jnp.roll(field, 1, 2)

    def apply_full(field):
        return apply_space(field) + time_coupling * (2.0 * field - jnp.roll(field, -1, 0) - jnp.roll(field, 1, 0))
    cas_table = hartley_table(NT)
    freq_shift = spectral_shift(NT)

    def precondition(field):
        return transform(cas_table, chebyshev(transform(cas_table, field), freq_shift, apply_space))
    solution = jnp.zeros_like(right_side)
    residual = right_side
    search = precondition(residual)
    direction = search
    gamma = jnp.sum(residual * search)
    for iteration in range(ITERS):
        curved = apply_full(direction)
        step_len = gamma / jnp.sum(direction * curved)
        solution = solution + step_len * direction
        residual = residual - step_len * curved
        if iteration + 1 < ITERS:
            search = precondition(residual)
            gamma_next = jnp.sum(residual * search)
            direction = search + gamma_next / gamma * direction
            gamma = gamma_next
    return (solution, residual)
```

```python
import functools
import math

import jax
import jax.numpy as jnp
import numpy as np
from jax import lax
from jax.experimental import pallas as pl
from jax.experimental.pallas import tpu as pltpu
from jax.sharding import PartitionSpec as P

CHEB = 4
COUPLING = 2.0
KAPPA_LOW = 0.05
KAPPA_HIGH = 1.0
REACH = 16.0

LANES = 128
HALO = CHEB + 1
PARAMS = pltpu.CompilerParams(vmem_limit_bytes=24 * 1024 * 1024)


def hartley_table(length):
    index = np.arange(length)
    angle = (index[:, None] * index[None, :] % length) * (2.0 * math.pi / length)
    return ((np.cos(angle) + np.sin(angle)) / math.sqrt(length)).astype(np.float32)


def chebyshev_table(length):
    shift = COUPLING * (2.0 - 2.0 * np.cos(2.0 * math.pi * np.arange(length) / length))
    half = 0.5 * (KAPPA_HIGH + REACH - KAPPA_LOW)
    mid = 0.5 * (KAPPA_LOW + KAPPA_HIGH + REACH) + shift
    ratio = mid / half
    damp = 1.0 / ratio
    columns = [shift, 1.0 / mid]
    for _ in range(CHEB):
        damp_next = 1.0 / (2.0 * ratio - damp)
        columns += [damp_next * damp, 2.0 * damp_next / half]
        damp = damp_next
    table = np.zeros((length, LANES), np.float32)
    table[:, : len(columns)] = np.stack(columns, 1)
    return table


def lane_index(shape):
    return lax.broadcasted_iota(jnp.int32, shape, len(shape) - 1)


def exact_dot(left, right):
    return lax.dot_general(
        left,
        right,
        (((1,), (0,)), ((), ())),
        precision=lax.Precision.HIGHEST,
        preferred_element_type=jnp.float32,
    )


def window_kernel(rows, times, tiles, source_ref, out_ref, scratch_ref):
    quarter = LANES // 4
    width = source_ref.shape[1]
    for part in range(width // LANES):
        scratch_ref[part] = source_ref[:, part * LANES : (part + 1) * LANES]
    for row in range(rows):
        place = pl.ds(row, times, stride=rows)
        field = jnp.concatenate(
            [scratch_ref[part, place, :] for part in range(width // LANES)], axis=1
        )
        even = pltpu.roll(field, quarter, 1)
        odd = pltpu.roll(field, width - quarter, 1)
        for tile in range(tiles):
            picked = even if tile % 2 == 0 else odd
            start = tile // 2 * LANES
            out_ref[tile, row * times : (row + 1) * times, :] = picked[:, start : start + LANES]


def forward_kernel(rows, times, length, cas_ref, field_ref, weight_ref, out_ref, low_ref, high_ref):
    for row in range(rows):
        block = field_ref[:, row * times : (row + 1) * times, :].reshape(length, LANES)
        freq = exact_dot(cas_ref[...], block)
        out_ref[row * length : (row + 1) * length, :] = freq
        if row < HALO:
            low_ref[row * length : (row + 1) * length, :] = freq
        if row >= rows - HALO:
            place = row - (rows - HALO)
            high_ref[place * length : (place + 1) * length, :] = freq
    low_ref[HALO * length :, :] = weight_ref[...]
    high_ref[HALO * length :, :] = weight_ref[...]


def passes(source, weights, coef, rows):
    shift, scale = coef[0], coef[1]
    total = rows + 2 * HALO
    step = [scale * field for field in source]
    remain = list(source)
    solved = [None] * total
    for turn in range(CHEB + 1):
        first, last = turn + 1, total - turn - 1
        flux = None
        new_step = [None] * total
        for row in range(first - 1, last):
            here = step[row]
            ahead = weights(1, row) * (here - step[row + 1])
            if row >= first:
                side = weights(2, row) * (here - pltpu.roll(here, LANES - 1, 1))
                applied = (
                    (weights(0, row) + shift) * here
                    + (ahead - flux)
                    + (side - pltpu.roll(side, 1, 1))
                )
                remain[row] = remain[row] - applied
                if HALO <= row < rows + HALO:
                    solved[row] = here if turn == 0 else solved[row] + here
                if turn < CHEB:
                    new_step[row] = coef[2 + 2 * turn] * here + coef[3 + 2 * turn] * remain[row]
            flux = ahead
        step = new_step
    inside = range(HALO, rows + HALO)
    return [solved[row] for row in inside], [source[row] - remain[row] for row in inside]


def read_coef(coef_ref, block):
    return [
        jnp.broadcast_to(coef_ref[block, index : index + 1], (8, LANES))
        for index in range(2 + 2 * CHEB)
    ]


def own(field):
    lane = lane_index(field.shape)
    return jnp.where((lane >= LANES // 4) & (lane < 3 * LANES // 4), field, 0.0)


def first_kernel(
    rows, length, field_ref, top_ref, bottom_ref, weight_ref, coef_ref,
    solved_ref, applied_ref, low_ref, high_ref, wide_ref, sums_ref,
):
    edge = HALO * length
    planes = []
    for plane in range(3):
        start = plane * rows
        planes.append(
            jnp.concatenate(
                [
                    top_ref[edge + start + rows - HALO : edge + start + rows, :],
                    weight_ref[start : start + rows, :],
                    bottom_ref[edge + start : edge + start + HALO, :],
                ],
                axis=0,
            )
        )
    east = 1.0 + 0.125 * (planes[1][:-1] + planes[1][1:])
    north = 1.0 + 0.125 * (planes[2] + pltpu.roll(planes[2], LANES - 1, 1))
    total = rows + 2 * HALO
    for plane, weight in enumerate((planes[0], east, north)):
        for row in range(weight.shape[0]):
            wide_ref[plane * total + row] = jnp.broadcast_to(weight[row : row + 1], (8, LANES))

    def weights(plane, row):
        return wide_ref[plane * total + row]

    def block_step(index, sums):
        gamma, curved = sums
        start = pl.multiple_of(index * 8, 8)
        source = (
            [top_ref[pl.ds(row * length + start, 8), :] for row in range(HALO)]
            + [field_ref[pl.ds(row * length + start, 8), :] for row in range(rows)]
            + [bottom_ref[pl.ds(row * length + start, 8), :] for row in range(HALO)]
        )
        coef = read_coef(coef_ref, pl.ds(start, 8))
        solved, applied = passes(source, weights, coef, rows)
        for row in range(rows):
            place = pl.ds(row * length + start, 8)
            solved_ref[place, :] = solved[row]
            applied_ref[place, :] = applied[row]
            if row < HALO:
                low_ref[place, :] = applied[row]
            if row >= rows - HALO:
                high_ref[pl.ds((row - rows + HALO) * length + start, 8), :] = applied[row]
            gamma = gamma + source[row + HALO] * solved[row]
            curved = curved + solved[row] * applied[row]
        return gamma, curved

    zero = jnp.zeros((8, LANES), jnp.float32)
    gamma, curved = lax.fori_loop(0, length // 8, block_step, (zero, zero))
    sums_ref[0] = gamma
    sums_ref[1] = curved


def second_kernel(
    rows, times, length, field_ref, top_ref, bottom_ref, earlier_ref, wide_ref, coef_ref, cas_ref,
    early_ref, out_ref, sums_ref, packed_ref,
):
    total = rows + 2 * HALO
    quarter = LANES // 4

    def weights(plane, row):
        return wide_ref[plane * total + row]

    def pack(left, right):
        return jnp.where(
            lane_index(left.shape) < LANES // 2,
            pltpu.roll(left, LANES - quarter, 1),
            pltpu.roll(right, quarter, 1),
        )

    def block_step(index, sums):
        cross, curved = sums
        start = pl.multiple_of(index * 8, 8)
        source = (
            [top_ref[pl.ds(row * length + start, 8), :] for row in range(HALO)]
            + [field_ref[pl.ds(row * length + start, 8), :] for row in range(rows)]
            + [bottom_ref[pl.ds(row * length + start, 8), :] for row in range(HALO)]
        )
        coef = read_coef(coef_ref, pl.ds(start, 8))
        solved, applied = passes(source, weights, coef, rows)
        for row in range(rows):
            place = pl.ds(row * length + start, 8)
            here = source[row + HALO]
            packed_ref[pl.ds(start, 8), row * LANES : (row + 1) * LANES] = pack(
                earlier_ref[place, :], solved[row]
            )
            packed_ref[pl.ds(start, 8), (rows + row) * LANES : (rows + row + 1) * LANES] = pack(
                here, applied[row]
            )
            cross = cross + here * solved[row]
            curved = curved + solved[row] * applied[row]
        return cross, curved

    zero = jnp.zeros((8, LANES), jnp.float32)
    cross, curved = lax.fori_loop(0, length // 8, block_step, (zero, zero))
    values = [jnp.sum(own(field)) for field in (early_ref[0], early_ref[1], cross, curved)]
    lane = lane_index((1, LANES))
    line = jnp.zeros((1, LANES), jnp.float32)
    for index, value in enumerate(values):
        line = jnp.where(lane == index, value, line)
    sums_ref[...] = jnp.broadcast_to(line[None], sums_ref.shape)
    for place in range(rows):
        wide = slice(place * 2 * LANES, (place + 1) * 2 * LANES)
        back = exact_dot(cas_ref[...], packed_ref[:, wide])
        for part in range(2):
            piece = back[:, part * LANES : (part + 1) * LANES].reshape(length // times, times, LANES)
            start = (2 * place + part) * times
            out_ref[:, start : start + times, :] = piece


def final_kernel(rows, times, tiles, source_ref, field_ref, sums_ref, solution_ref, residual_ref):
    line = jnp.sum(sums_ref[...].reshape(tiles, LANES), axis=0, keepdims=True)
    gamma, curved, cross, last = (
        jnp.broadcast_to(line[:, index : index + 1], (times, LANES)) for index in range(4)
    )
    step = gamma / curved
    gamma_next = step * step * cross - gamma
    turn = gamma_next / gamma
    grown = 1.0 + turn
    next_curved = grown * grown * curved - 2.0 * step * grown * cross + step * step * last
    next_step = gamma_next / next_curved
    low = lane_index((times, LANES)) < LANES // 2
    scale = jnp.where(low, step + next_step * grown, -next_step * step)
    for time in range(times):
        place = slice(time * rows, (time + 1) * rows)
        for pair in range(tiles // 2):
            columns = slice(pair * LANES, (pair + 1) * LANES)
            merged = []
            for part in range(2):
                taken = pl.ds(part * rows * times + time, rows, stride=times)
                left = scale * source_ref[2 * pair, taken, :]
                right = scale * source_ref[2 * pair + 1, taken, :]
                left = left + pltpu.roll(left, LANES // 2, 1)
                right = right + pltpu.roll(right, LANES // 2, 1)
                merged.append(jnp.where(low, left, right))
            solution_ref[place, columns] = merged[0]
            residual_ref[place, columns] = field_ref[place, columns] - merged[1]


def call(kernel, out_shape, scratch=()):
    shapes = [jax.ShapeDtypeStruct(shape, jnp.float32) for shape in out_shape]
    return pl.pallas_call(
        kernel,
        out_shape=shapes[0] if len(shapes) == 1 else shapes,
        scratch_shapes=[pltpu.VMEM(shape, jnp.float32) for shape in scratch],
        compiler_params=PARAMS,
    )


def shards(right_side, kappa, velocity):
    tiles = lax.axis_size("tm")
    spaces = lax.axis_size("space")
    times, rows, width = right_side.shape
    length = times * tiles
    tile = width // tiles
    quarter = LANES // 4
    cas_table = jnp.asarray(hartley_table(length))
    coef_table = jnp.asarray(chebyshev_table(length))
    up = [(i, (i + 1) % spaces) for i in range(spaces)]
    down = [(i, (i - 1) % spaces) for i in range(spaces)]

    field = right_side.reshape(times * rows, width)
    windows = call(
        functools.partial(window_kernel, rows, times, tiles),
        [(tiles, rows * times, LANES)],
        [(width // LANES, times * rows, LANES)],
    )(field)
    gathered = lax.all_to_all(windows, "tm", 0, 0)

    squares = velocity.astype(jnp.float32) ** 2
    planes = jnp.concatenate([kappa, squares[0], squares[1]], axis=0)
    planes = jnp.concatenate([planes[:, -quarter:], planes, planes[:, :quarter]], axis=1)
    local = lax.dynamic_slice_in_dim(planes, lax.axis_index("tm") * tile, LANES, 1)

    halo_shape = (HALO * length + 3 * rows, LANES)
    freq, low, high = call(
        functools.partial(forward_kernel, rows, times, length),
        [(rows * length, LANES), halo_shape, halo_shape],
    )(cas_table, gathered, local)
    top = lax.ppermute(high, "space", up)
    bottom = lax.ppermute(low, "space", down)

    total = rows + 2 * HALO
    halo_shape = (HALO * length, LANES)
    solved, applied, low, high, wide, early = call(
        functools.partial(first_kernel, rows, length),
        [
            (rows * length, LANES),
            (rows * length, LANES),
            halo_shape,
            halo_shape,
            (3 * total, 8, LANES),
            (2, 8, LANES),
        ],
    )(freq, top, bottom, local, coef_table)
    top = lax.ppermute(high, "space", up)
    bottom = lax.ppermute(low, "space", down)

    packed, sums = call(
        functools.partial(second_kernel, rows, times, length),
        [(tiles, 2 * rows * times, LANES), (spaces, 1, LANES)],
        [(length, 2 * rows * LANES)],
    )(applied, top, bottom, solved, wide, coef_table, cas_table, early)
    returned = lax.all_to_all(packed, "tm", 0, 0)
    sums = jnp.sum(lax.all_to_all(sums, "space", 0, 0), axis=0)
    sums = lax.all_to_all(jnp.broadcast_to(sums[None], (tiles, 1, LANES)), "tm", 0, 0)

    solution, residual = call(
        functools.partial(final_kernel, rows, times, tiles),
        [(times * rows, width), (times * rows, width)],
    )(returned, field, sums)
    shape = right_side.shape
    return solution.reshape(shape), residual.reshape(shape)


def solution(mesh):
    placed = (P("tm", "space", None), P("space", None), P(None, "space", None))
    return jax.shard_map(
        shards,
        mesh=mesh,
        in_specs=placed,
        out_specs=(P("tm", "space", None), P("tm", "space", None)),
        check_vma=False,
    )
```

```python
import functools
import math

import jax
import jax.numpy as jnp
import numpy as np
from jax import lax
from jax.experimental import pallas as pl
from jax.experimental.pallas import tpu as pltpu
from jax.sharding import PartitionSpec as P

CHEB = 4
COUPLING = 2.0
KAPPA_LOW = 0.05
KAPPA_HIGH = 1.0
REACH = 16.0

LANES = 128
SUB = 8
HALO = CHEB + 1
SIDE = 16
BLOCK = 11
WINDOW = SUB * BLOCK
PARAMS = pltpu.CompilerParams(vmem_limit_bytes=24 * 1024 * 1024)


def hartley_table(length):
    index = np.arange(length)
    angle = (index[:, None] * index[None, :] % length) * (2.0 * math.pi / length)
    return ((np.cos(angle) + np.sin(angle)) / math.sqrt(length)).astype(np.float32)


def chebyshev_table(length):
    shift = COUPLING * (2.0 - 2.0 * np.cos(2.0 * math.pi * np.arange(length) / length))
    half = 0.5 * (KAPPA_HIGH + REACH - KAPPA_LOW)
    mid = 0.5 * (KAPPA_LOW + KAPPA_HIGH + REACH) + shift
    ratio = mid / half
    damp = 1.0 / ratio
    lines = [shift, 1.0 / mid]
    for _ in range(CHEB):
        damp_next = 1.0 / (2.0 * ratio - damp)
        lines += [damp_next * damp, 2.0 * damp_next / half]
        damp = damp_next
    return np.repeat(np.stack(lines).astype(np.float32)[:, None], SUB, 1)


def lane_index(shape):
    return lax.broadcasted_iota(jnp.int32, shape, len(shape) - 1)


def exact_dot(left, right, left_dim, right_dim):
    return lax.dot_general(
        left,
        right,
        (((left_dim,), (right_dim,)), ((), ())),
        precision=lax.Precision.HIGHEST,
        preferred_element_type=jnp.float32,
    )


def window_kernel(rows, times, tiles, source_ref, out_ref, scratch_ref):
    half = LANES // 2
    parts = source_ref.shape[1] // LANES
    for part in range(parts):
        scratch_ref[part] = source_ref[:, part * LANES : (part + 1) * LANES]
    lane = lane_index((times, LANES))
    fields = [
        [scratch_ref[part, pl.ds(row, times, stride=rows), :] for part in range(parts)]
        for row in range(rows)
    ]
    for pair in range(rows // 2):
        for part in range(parts):
            one, two = fields[2 * pair][part], fields[2 * pair + 1][part]
            place = slice(pair * times, (pair + 1) * times)
            out_ref[2 * part, place, :] = jnp.where(lane < half, one, pltpu.roll(two, half, 1))
            out_ref[2 * part + 1, place, :] = jnp.where(lane < half, pltpu.roll(one, half, 1), two)
    spread = 2 * SIDE
    group = LANES // spread
    for quad in range(rows // group):
        even = [None] * parts
        odd = [None] * parts
        for index in range(group):
            row = quad * group + index
            wide = jnp.concatenate(fields[row], axis=1)
            near = pltpu.roll(wide, spread * index + SIDE, 1)
            away = pltpu.roll(wide, (spread * index - half + SIDE) % wide.shape[1], 1)
            left = (lane >= spread * index) & (lane < spread * index + SIDE)
            right = (lane >= spread * index + SIDE) & (lane < spread * (index + 1))
            for part in range(parts):
                here = slice(part * LANES, (part + 1) * LANES)
                then = (part + 1) % parts
                then = slice(then * LANES, (then + 1) * LANES)
                if index == 0:
                    even[part] = jnp.where(left, near[:, here], away[:, here])
                    odd[part] = jnp.where(left, away[:, here], near[:, then])
                else:
                    even[part] = jnp.where(
                        left, near[:, here], jnp.where(right, away[:, here], even[part])
                    )
                    odd[part] = jnp.where(
                        left, away[:, here], jnp.where(right, near[:, then], odd[part])
                    )
        start = (rows // 2 + quad) * times
        for part in range(parts):
            out_ref[2 * part, start : start + times, :] = even[part]
            out_ref[2 * part + 1, start : start + times, :] = odd[part]


def forward_kernel(rows, times, length, cas_ref, field_ref, out_ref, low_ref, high_ref, line_ref):
    half = LANES // 2
    span = half + 2 * SIDE
    pieces = field_ref.shape[1] // times
    group = LANES // (2 * SIDE)
    for piece in range(pieces):
        block = field_ref[:, piece * times : (piece + 1) * times, :].reshape(length, LANES)
        freq = exact_dot(block, cas_ref[...], 0, 0)
        if piece < rows // 2:
            for part in range(2):
                start = (2 * piece + part) * span + SIDE
                line_ref[start : start + half, :] = freq[part * half : (part + 1) * half]
        else:
            for index in range(group):
                start = ((piece - rows // 2) * group + index) * span
                place = 2 * SIDE * index
                line_ref[start : start + SIDE, :] = freq[place : place + SIDE]
                line_ref[start + SIDE + half : start + span, :] = freq[
                    place + SIDE : place + 2 * SIDE
                ]
    skip = (span - WINDOW) // 2
    for row in range(rows):
        for column in range(BLOCK):
            value = line_ref[pl.ds(row * span + skip + column, SUB, stride=BLOCK), :]
            out_ref[row, column] = value
            if row < HALO:
                low_ref[row, column] = value
            if row >= rows - HALO:
                high_ref[row - (rows - HALO), column] = value


def weight_kernel(rows, local_ref, top_ref, bottom_ref, wide_ref, scratch_ref):
    planes = []
    for plane in range(3):
        start = plane * rows
        planes.append(
            jnp.concatenate(
                [
                    top_ref[start + rows - HALO : start + rows, :],
                    local_ref[start : start + rows, :],
                    bottom_ref[start : start + HALO, :],
                ],
                axis=0,
            )
        )
    east = 1.0 + 0.125 * (planes[1] + jnp.concatenate([planes[1][1:], planes[1][:1]], axis=0))
    north = 1.0 + 0.125 * (planes[2] + pltpu.roll(planes[2], LANES - 1, 1))
    total = rows + 2 * HALO
    zero = jnp.zeros((LANES - 3 * total, LANES), jnp.float32)
    scratch_ref[...] = jnp.transpose(jnp.concatenate([planes[0], east, north, zero], axis=0))
    skip = (LANES - WINDOW) // 2
    for column in range(BLOCK):
        lines = scratch_ref[pl.ds(skip + column, SUB, stride=BLOCK), :]
        for row in range(total):
            for plane in range(3):
                index = plane * total + row
                wide_ref[row, plane * BLOCK + column] = jnp.broadcast_to(
                    lines[:, index : index + 1], (SUB, LANES)
                )


def own_columns(column):
    place = lax.broadcasted_iota(jnp.int32, (SUB, LANES), 0) * BLOCK + column
    first = (WINDOW - LANES // 2) // 2
    return (place >= first) & (place < first + LANES // 2)


def passes(
    rows, top_ref, field_ref, bottom_ref, wide_ref, coef_ref, step_ref, remain_ref, solved_ref, emit
):
    total = rows + 2 * HALO
    columns = range(BLOCK)

    def begin(source_ref, offset, count):
        scale = coef_ref[1]

        @pl.loop(0, count)
        def _(row):
            for column in columns:
                value = source_ref[row, column]
                remain_ref[offset + row, column] = value
                step_ref[offset + row, column] = scale * value

    begin(top_ref, 0, HALO)
    begin(field_ref, HALO, rows)
    begin(bottom_ref, HALO + rows, HALO)

    for turn in range(CHEB + 1):
        first, last = turn + 1, total - turn - 1
        shift = coef_ref[0]

        def row_step(row, carry, *, turn=turn, inside=False, shift=shift):
            here, flux = carry[:BLOCK], carry[BLOCK:]
            after = [step_ref[row + 1, column] for column in columns]
            ahead = [wide_ref[row, BLOCK + column] * (here[column] - after[column]) for column in columns]
            beside = list(here[1:]) + [pltpu.roll(here[0], SUB - 1, 0)]
            side = [wide_ref[row, 2 * BLOCK + column] * (here[column] - beside[column]) for column in columns]
            behind = [pltpu.roll(side[-1], 1, 0)] + side[:-1]
            for column in columns:
                applied = (
                    (wide_ref[row, column] + shift) * here[column]
                    + (ahead[column] - flux[column])
                    + (side[column] - behind[column])
                )
                left = remain_ref[row, column] - applied
                if turn < CHEB:
                    remain_ref[row, column] = left
                    step_ref[row, column] = (
                        coef_ref[2 + 2 * turn] * here[column] + coef_ref[3 + 2 * turn] * left
                    )
                if inside:
                    own = row - HALO
                    if turn == 0:
                        solved_ref[own, column] = here[column]
                    elif turn < CHEB:
                        solved_ref[own, column] = solved_ref[own, column] + here[column]
                    else:
                        source = field_ref[own, column]
                        emit(own, column, source, solved_ref[own, column] + here[column], source - left)
            return (*after, *ahead)

        here = [step_ref[first, column] for column in columns]
        flux = [
            wide_ref[first - 1, BLOCK + column] * (step_ref[first - 1, column] - here[column])
            for column in columns
        ]
        carry = (*here, *flux)
        if first < HALO:
            carry = lax.fori_loop(first, HALO, row_step, carry)
        carry = lax.fori_loop(HALO, HALO + rows, functools.partial(row_step, inside=True), carry)
        if HALO + rows < last:
            lax.fori_loop(HALO + rows, last, row_step, carry)


def first_kernel(
    rows, top_ref, field_ref, bottom_ref, wide_ref, coef_ref,
    solved_ref, applied_ref, low_ref, high_ref, sums_ref, step_ref, remain_ref, part_ref,
):
    sums_ref[...] = jnp.zeros_like(sums_ref)

    def emit(row, column, source, solved, applied):
        solved_ref[row, column] = solved
        applied_ref[row, column] = applied
        inside = jnp.where(own_columns(column), solved, 0.0)
        sums_ref[0] = sums_ref[0] + source * inside
        sums_ref[1] = sums_ref[1] + applied * inside

    passes(
        rows, top_ref, field_ref, bottom_ref, wide_ref, coef_ref, step_ref, remain_ref, part_ref, emit
    )
    for row in range(HALO):
        for column in range(BLOCK):
            low_ref[row, column] = applied_ref[row, column]
            high_ref[row, column] = applied_ref[rows - HALO + row, column]


def second_kernel(
    rows, top_ref, field_ref, bottom_ref, wide_ref, coef_ref, early_ref,
    solved_ref, applied_ref, sums_ref, step_ref, remain_ref, part_ref, late_ref,
):
    late_ref[...] = jnp.zeros_like(late_ref)

    def emit(row, column, source, solved, applied):
        solved_ref[row, column] = solved
        applied_ref[row, column] = applied
        inside = jnp.where(own_columns(column), solved, 0.0)
        late_ref[0] = late_ref[0] + source * inside
        late_ref[1] = late_ref[1] + applied * inside

    passes(
        rows, top_ref, field_ref, bottom_ref, wide_ref, coef_ref, step_ref, remain_ref, part_ref, emit
    )
    values = [jnp.sum(ref[index]) for ref in (early_ref, late_ref) for index in range(2)]
    lane = lane_index((1, LANES))
    line = jnp.zeros((1, LANES), jnp.float32)
    for index, value in enumerate(values):
        line = jnp.where(lane == index, value, line)
    sums_ref[...] = jnp.broadcast_to(line[None], sums_ref.shape)


def inverse_kernel(rows, times, length, cas_ref, one_ref, two_ref, three_ref, four_ref, out_ref, line_ref):
    half = LANES // 2
    span = half + 2 * SIDE
    skip = (span - WINDOW) // 2
    refs = (one_ref, two_ref, three_ref, four_ref)
    for row in range(rows):
        for index, ref in enumerate(refs):
            for column in range(BLOCK):
                start = (row * len(refs) + index) * span + skip + column
                line_ref[pl.ds(start, SUB, stride=BLOCK), :] = ref[row, column]
    for row in range(rows):
        for pair in range(2):
            start = (row * len(refs) + 2 * pair) * span + SIDE
            points = jnp.concatenate(
                [line_ref[start : start + half, :], line_ref[start + span : start + span + half, :]],
                axis=0,
            )
            back = exact_dot(cas_ref[...], points, 1, 1).reshape(length // times, times, LANES)
            place = (pair * rows + row) * times
            out_ref[:, place : place + times, :] = back


def final_kernel(rows, times, tiles, source_ref, field_ref, sums_ref, solution_ref, residual_ref):
    line = sums_ref[...]
    gamma, curved, cross, last = (
        jnp.broadcast_to(line[:, index : index + 1], (times, LANES)) for index in range(4)
    )
    step = gamma / curved
    gamma_next = step * step * cross - gamma
    turn = gamma_next / gamma
    grown = 1.0 + turn
    next_curved = grown * grown * curved - 2.0 * step * grown * cross + step * step * last
    next_step = gamma_next / next_curved
    low = lane_index((times, LANES)) < LANES // 2
    scale = jnp.where(low, step + next_step * grown, -next_step * step)
    for time in range(times):
        place = slice(time * rows, (time + 1) * rows)
        for pair in range(tiles // 2):
            columns = slice(pair * LANES, (pair + 1) * LANES)
            merged = []
            for part in range(2):
                taken = pl.ds(part * rows * times + time, rows, stride=times)
                left = scale * source_ref[2 * pair, taken, :]
                right = scale * source_ref[2 * pair + 1, taken, :]
                left = left + pltpu.roll(left, LANES // 2, 1)
                right = right + pltpu.roll(right, LANES // 2, 1)
                merged.append(jnp.where(low, left, right))
            solution_ref[place, columns] = merged[0]
            residual_ref[place, columns] = field_ref[place, columns] - merged[1]


def call(kernel, out_shape, scratch=()):
    shapes = [jax.ShapeDtypeStruct(shape, jnp.float32) for shape in out_shape]
    return pl.pallas_call(
        kernel,
        out_shape=shapes[0] if len(shapes) == 1 else shapes,
        scratch_shapes=[pltpu.VMEM(shape, jnp.float32) for shape in scratch],
        compiler_params=PARAMS,
    )


def exchange(low, high, spaces):
    up = [(i, (i + 1) % spaces) for i in range(spaces)]
    down = [(i, (i - 1) % spaces) for i in range(spaces)]
    return lax.ppermute(high, "space", up), lax.ppermute(low, "space", down)


def shards(right_side, kappa, velocity):
    tiles = lax.axis_size("tm")
    spaces = lax.axis_size("space")
    times, rows, width = right_side.shape
    length = times * tiles
    tile = width // tiles
    around = (LANES - tile) // 2
    cas_table = jnp.asarray(hartley_table(length))
    coef_table = jnp.asarray(chebyshev_table(length))

    field = right_side.reshape(times * rows, width)
    windows = call(
        functools.partial(window_kernel, rows, times, tiles),
        [(tiles, 6 * times, LANES)],
        [(width // LANES, times * rows, LANES)],
    )(field)
    gathered = lax.all_to_all(windows, "tm", 0, 0)

    squares = velocity.astype(jnp.float32) ** 2
    planes = jnp.concatenate([kappa, squares[0], squares[1]], axis=0)
    planes = jnp.concatenate([planes[:, -around:], planes, planes[:, :around]], axis=1)
    local = lax.dynamic_slice_in_dim(planes, lax.axis_index("tm") * tile, LANES, 1)
    top, bottom = exchange(local, local, spaces)
    total = rows + 2 * HALO
    wide = call(
        functools.partial(weight_kernel, rows),
        [(total, 3 * BLOCK, SUB, LANES)],
        [(LANES, LANES)],
    )(local, top, bottom)

    tile_shape = (rows, BLOCK, SUB, LANES)
    edge_shape = (HALO, BLOCK, SUB, LANES)
    work = [(total, BLOCK, SUB, LANES), (total, BLOCK, SUB, LANES), tile_shape]
    span = LANES // 2 + 2 * SIDE
    freq, low, high = call(
        functools.partial(forward_kernel, rows, times, length),
        [tile_shape, edge_shape, edge_shape],
        [(rows * span, LANES)],
    )(cas_table, gathered)
    top, bottom = exchange(low, high, spaces)

    solved, applied, low, high, early = call(
        functools.partial(first_kernel, rows),
        [tile_shape, tile_shape, edge_shape, edge_shape, (2, SUB, LANES)],
        work,
    )(top, freq, bottom, wide, coef_table)
    top, bottom = exchange(low, high, spaces)

    solved_two, applied_two, sums = call(
        functools.partial(second_kernel, rows),
        [tile_shape, tile_shape, (tiles, 1, LANES)],
        [*work, (2, SUB, LANES)],
    )(top, applied, bottom, wide, coef_table, early)
    packed = call(
        functools.partial(inverse_kernel, rows, times, length),
        [(tiles, 2 * rows * times, LANES)],
        [(rows * 4 * span, LANES)],
    )(cas_table, solved, solved_two, applied, applied_two)
    sums = jnp.sum(lax.all_to_all(sums, "tm", 0, 0), axis=0)
    returned = lax.all_to_all(packed, "tm", 0, 0)
    distance = 1
    while distance < spaces:
        pairs = [(i, i ^ distance) for i in range(spaces)]
        sums = sums + lax.ppermute(sums, "space", pairs)
        distance *= 2

    solution, residual = call(
        functools.partial(final_kernel, rows, times, tiles),
        [(times * rows, width), (times * rows, width)],
    )(returned, field, sums)
    shape = right_side.shape
    return solution.reshape(shape), residual.reshape(shape)


def solution(mesh):
    placed = (P("tm", "space", None), P("space", None), P(None, "space", None))
    return jax.shard_map(
        shards,
        mesh=mesh,
        in_specs=placed,
        out_specs=(P("tm", "space", None), P("tm", "space", None)),
        check_vma=False,
    )
```

```python
import functools
import math

import jax
import jax.numpy as jnp
import numpy as np
from jax import lax
from jax.experimental import pallas as pl
from jax.experimental.pallas import tpu as pltpu
from jax.sharding import PartitionSpec as P

CHEB = 4
COUPLING = 2.0
KAPPA_LOW = 0.05
KAPPA_HIGH = 1.0
REACH = 16.0

LANES = 128
SUB = 8
HALO = CHEB + 1
SIDE = 16
BLOCK = 11
WINDOW = SUB * BLOCK
NEAR = 4
PARAMS = pltpu.CompilerParams(vmem_limit_bytes=24 * 1024 * 1024)


def hartley_table(length):
    index = np.arange(length)
    angle = (index[:, None] * index[None, :] % length) * (2.0 * math.pi / length)
    return ((np.cos(angle) + np.sin(angle)) / math.sqrt(length)).astype(np.float32)


def chebyshev_table(length):
    shift = COUPLING * (2.0 - 2.0 * np.cos(2.0 * math.pi * np.arange(length) / length))
    half = 0.5 * (KAPPA_HIGH + REACH - KAPPA_LOW)
    mid = 0.5 * (KAPPA_LOW + KAPPA_HIGH + REACH) + shift
    ratio = mid / half
    damp = 1.0 / ratio
    lines = [shift, 1.0 / mid]
    for _ in range(CHEB):
        damp_next = 1.0 / (2.0 * ratio - damp)
        lines += [damp_next * damp, 2.0 * damp_next / half]
        damp = damp_next
    return np.repeat(np.stack(lines).astype(np.float32)[:, None], SUB, 1)


def lane_index(shape):
    return lax.broadcasted_iota(jnp.int32, shape, len(shape) - 1)


def exact_dot(left, right, left_dim, right_dim):
    return lax.dot_general(
        left,
        right,
        (((left_dim,), (right_dim,)), ((), ())),
        precision=lax.Precision.HIGHEST,
        preferred_element_type=jnp.float32,
    )


def window_kernel(rows, times, tiles, source_ref, out_ref, scratch_ref):
    half = LANES // 2
    parts = source_ref.shape[1] // LANES
    for part in range(parts):
        scratch_ref[part] = source_ref[:, part * LANES : (part + 1) * LANES]
    lane = lane_index((times, LANES))
    fields = [
        [scratch_ref[part, pl.ds(row, times, stride=rows), :] for part in range(parts)]
        for row in range(rows)
    ]
    for pair in range(rows // 2):
        for part in range(parts):
            one, two = fields[2 * pair][part], fields[2 * pair + 1][part]
            place = slice(pair * times, (pair + 1) * times)
            out_ref[2 * part, place, :] = jnp.where(lane < half, one, pltpu.roll(two, half, 1))
            out_ref[2 * part + 1, place, :] = jnp.where(lane < half, pltpu.roll(one, half, 1), two)
    spread = 2 * SIDE
    group = LANES // spread
    for quad in range(rows // group):
        even = [None] * parts
        odd = [None] * parts
        for index in range(group):
            row = quad * group + index
            wide = jnp.concatenate(fields[row], axis=1)
            near = pltpu.roll(wide, spread * index + SIDE, 1)
            away = pltpu.roll(wide, (spread * index - half + SIDE) % wide.shape[1], 1)
            left = (lane >= spread * index) & (lane < spread * index + SIDE)
            right = (lane >= spread * index + SIDE) & (lane < spread * (index + 1))
            for part in range(parts):
                here = slice(part * LANES, (part + 1) * LANES)
                then = (part + 1) % parts
                then = slice(then * LANES, (then + 1) * LANES)
                if index == 0:
                    even[part] = jnp.where(left, near[:, here], away[:, here])
                    odd[part] = jnp.where(left, away[:, here], near[:, then])
                else:
                    even[part] = jnp.where(
                        left, near[:, here], jnp.where(right, away[:, here], even[part])
                    )
                    odd[part] = jnp.where(
                        left, away[:, here], jnp.where(right, near[:, then], odd[part])
                    )
        start = (rows // 2 + quad) * times
        for part in range(parts):
            out_ref[2 * part, start : start + times, :] = even[part]
            out_ref[2 * part + 1, start : start + times, :] = odd[part]


def forward_kernel(rows, times, length, cas_ref, field_ref, out_ref, low_ref, high_ref, line_ref):
    half = LANES // 2
    span = half + 2 * SIDE
    pieces = field_ref.shape[1] // times
    group = LANES // (2 * SIDE)
    for piece in range(pieces):
        block = field_ref[:, piece * times : (piece + 1) * times, :].reshape(length, LANES)
        freq = exact_dot(block, cas_ref[...], 0, 0)
        if piece < rows // 2:
            for part in range(2):
                start = (2 * piece + part) * span + SIDE
                line_ref[start : start + half, :] = freq[part * half : (part + 1) * half]
        else:
            for index in range(group):
                start = ((piece - rows // 2) * group + index) * span
                place = 2 * SIDE * index
                line_ref[start : start + SIDE, :] = freq[place : place + SIDE]
                line_ref[start + SIDE + half : start + span, :] = freq[
                    place + SIDE : place + 2 * SIDE
                ]
    skip = (span - WINDOW) // 2
    for row in range(rows):
        for column in range(BLOCK):
            value = line_ref[pl.ds(row * span + skip + column, SUB, stride=BLOCK), :]
            out_ref[row, column] = value
            if row < HALO:
                low_ref[row, column] = value
            if row >= rows - HALO:
                high_ref[row - (rows - HALO), column] = value


def weight_kernel(rows, local_ref, top_ref, bottom_ref, wide_ref, scratch_ref):
    planes = []
    for plane in range(3):
        start = plane * rows
        planes.append(
            jnp.concatenate(
                [
                    top_ref[start + rows - HALO : start + rows, :],
                    local_ref[start : start + rows, :],
                    bottom_ref[start : start + HALO, :],
                ],
                axis=0,
            )
        )
    east = 1.0 + 0.125 * (planes[1] + jnp.concatenate([planes[1][1:], planes[1][:1]], axis=0))
    north = 1.0 + 0.125 * (planes[2] + pltpu.roll(planes[2], LANES - 1, 1))
    total = rows + 2 * HALO
    zero = jnp.zeros((LANES - 3 * total, LANES), jnp.float32)
    scratch_ref[...] = jnp.transpose(jnp.concatenate([planes[0], east, north, zero], axis=0))
    skip = (LANES - WINDOW) // 2
    for column in range(BLOCK):
        lines = scratch_ref[pl.ds(skip + column, SUB, stride=BLOCK), :]
        for row in range(total):
            for plane in range(3):
                index = plane * total + row
                wide_ref[row, plane * BLOCK + column] = jnp.broadcast_to(
                    lines[:, index : index + 1], (SUB, LANES)
                )


def own_columns(column):
    place = lax.broadcasted_iota(jnp.int32, (SUB, LANES), 0) * BLOCK + column
    first = (WINDOW - LANES // 2) // 2
    return (place >= first) & (place < first + LANES // 2)


def passes(
    rows, top_ref, field_ref, bottom_ref, wide_ref, coef_ref, step_ref, remain_ref, solved_ref, emit
):
    total = rows + 2 * HALO
    columns = range(BLOCK)

    def begin(source_ref, offset, count):
        scale = coef_ref[1]

        @pl.loop(0, count)
        def _(row):
            for column in columns:
                value = source_ref[row, column]
                remain_ref[offset + row, column] = value
                step_ref[offset + row, column] = scale * value

    begin(top_ref, 0, HALO)
    begin(field_ref, HALO, rows)
    begin(bottom_ref, HALO + rows, HALO)

    for turn in range(CHEB + 1):
        first, last = turn + 1, total - turn - 1
        shift = coef_ref[0]

        def row_step(row, carry, *, turn=turn, inside=False, shift=shift):
            here, flux = carry[:BLOCK], carry[BLOCK:]
            after = [step_ref[row + 1, column] for column in columns]
            ahead = [wide_ref[row, BLOCK + column] * (here[column] - after[column]) for column in columns]
            beside = list(here[1:]) + [pltpu.roll(here[0], SUB - 1, 0)]
            side = [wide_ref[row, 2 * BLOCK + column] * (here[column] - beside[column]) for column in columns]
            behind = [pltpu.roll(side[-1], 1, 0)] + side[:-1]
            for column in columns:
                applied = (
                    (wide_ref[row, column] + shift) * here[column]
                    + (ahead[column] - flux[column])
                    + (side[column] - behind[column])
                )
                left = remain_ref[row, column] - applied
                if turn < CHEB:
                    remain_ref[row, column] = left
                    step_ref[row, column] = (
                        coef_ref[2 + 2 * turn] * here[column] + coef_ref[3 + 2 * turn] * left
                    )
                if inside:
                    own = row - HALO
                    if turn == 0:
                        solved_ref[own, column] = here[column]
                    elif turn < CHEB:
                        solved_ref[own, column] = solved_ref[own, column] + here[column]
                    else:
                        source = field_ref[own, column]
                        emit(own, column, source, solved_ref[own, column] + here[column], source - left)
            return (*after, *ahead)

        here = [step_ref[first, column] for column in columns]
        flux = [
            wide_ref[first - 1, BLOCK + column] * (step_ref[first - 1, column] - here[column])
            for column in columns
        ]
        carry = (*here, *flux)
        if first < HALO:
            carry = lax.fori_loop(first, HALO, row_step, carry)
        carry = lax.fori_loop(HALO, HALO + rows, functools.partial(row_step, inside=True), carry)
        if HALO + rows < last:
            lax.fori_loop(HALO + rows, last, row_step, carry)


def first_kernel(
    rows, top_ref, field_ref, bottom_ref, wide_ref, coef_ref,
    solved_ref, applied_ref, low_ref, high_ref, sums_ref, step_ref, remain_ref, part_ref,
):
    sums_ref[...] = jnp.zeros_like(sums_ref)

    def emit(row, column, source, solved, applied):
        solved_ref[row, column] = solved
        applied_ref[row, column] = applied
        inside = jnp.where(own_columns(column), solved, 0.0)
        sums_ref[0] = sums_ref[0] + source * inside
        sums_ref[1] = sums_ref[1] + applied * inside

    passes(
        rows, top_ref, field_ref, bottom_ref, wide_ref, coef_ref, step_ref, remain_ref, part_ref, emit
    )
    for row in range(HALO):
        for column in range(BLOCK):
            low_ref[row, column] = applied_ref[row, column]
            high_ref[row, column] = applied_ref[rows - HALO + row, column]


def second_kernel(
    rows, top_ref, field_ref, bottom_ref, wide_ref, coef_ref, early_ref,
    solved_ref, applied_ref, sums_ref, step_ref, remain_ref, part_ref, late_ref,
):
    late_ref[...] = jnp.zeros_like(late_ref)

    def emit(row, column, source, solved, applied):
        solved_ref[row, column] = solved
        applied_ref[row, column] = applied
        inside = jnp.where(own_columns(column), solved, 0.0)
        late_ref[0] = late_ref[0] + source * inside
        late_ref[1] = late_ref[1] + applied * inside

    passes(
        rows, top_ref, field_ref, bottom_ref, wide_ref, coef_ref, step_ref, remain_ref, part_ref, emit
    )
    values = [jnp.sum(ref[index]) for ref in (early_ref, late_ref) for index in range(2)]
    lane = lane_index((1, LANES))
    line = jnp.zeros((1, LANES), jnp.float32)
    for index, value in enumerate(values):
        line = jnp.where(lane == index, value, line)
    sums_ref[...] = jnp.broadcast_to(line[None], sums_ref.shape)


def inverse_kernel(rows, times, length, cas_ref, one_ref, two_ref, three_ref, four_ref, out_ref, line_ref):
    half = LANES // 2
    span = half + 2 * SIDE
    skip = (span - WINDOW) // 2
    refs = (one_ref, two_ref, three_ref, four_ref)
    for row in range(rows):
        for index, ref in enumerate(refs):
            for column in range(BLOCK):
                start = (row * len(refs) + index) * span + skip + column
                line_ref[pl.ds(start, SUB, stride=BLOCK), :] = ref[row, column]
    for row in range(rows):
        for pair in range(2):
            start = (row * len(refs) + 2 * pair) * span + SIDE
            points = jnp.concatenate(
                [line_ref[start : start + half, :], line_ref[start + span : start + span + half, :]],
                axis=0,
            )
            back = exact_dot(cas_ref[...], points, 1, 1).reshape(length // times, times, LANES)
            place = (pair * rows + row) * times
            out_ref[:, place : place + times, :] = back


def final_kernel(rows, times, tiles, source_ref, field_ref, sums_ref, solution_ref, residual_ref):
    line = sums_ref[...]
    gamma, curved, cross, last = (
        jnp.broadcast_to(line[:, index : index + 1], (times, LANES)) for index in range(4)
    )
    step = gamma / curved
    gamma_next = step * step * cross - gamma
    turn = gamma_next / gamma
    grown = 1.0 + turn
    next_curved = grown * grown * curved - 2.0 * step * grown * cross + step * step * last
    next_step = gamma_next / next_curved
    low = lane_index((times, LANES)) < LANES // 2
    scale = jnp.where(low, step + next_step * grown, -next_step * step)
    for time in range(times):
        place = slice(time * rows, (time + 1) * rows)
        for pair in range(tiles // 2):
            columns = slice(pair * LANES, (pair + 1) * LANES)
            merged = []
            for part in range(2):
                taken = pl.ds(part * rows * times + time, rows, stride=times)
                left = scale * source_ref[2 * pair, taken, :]
                right = scale * source_ref[2 * pair + 1, taken, :]
                left = left + pltpu.roll(left, LANES // 2, 1)
                right = right + pltpu.roll(right, LANES // 2, 1)
                merged.append(jnp.where(low, left, right))
            solution_ref[place, columns] = merged[0]
            residual_ref[place, columns] = field_ref[place, columns] - merged[1]


def call(kernel, out_shape, scratch=()):
    shapes = [jax.ShapeDtypeStruct(shape, jnp.float32) for shape in out_shape]
    return pl.pallas_call(
        kernel,
        out_shape=shapes[0] if len(shapes) == 1 else shapes,
        scratch_shapes=[pltpu.VMEM(shape, jnp.float32) for shape in scratch],
        compiler_params=PARAMS,
    )


def exchange(low, high, spaces):
    up = [(i, (i + 1) % spaces) for i in range(spaces)]
    down = [(i, (i - 1) % spaces) for i in range(spaces)]
    return lax.ppermute(high, "space", up), lax.ppermute(low, "space", down)


def shards(right_side, kappa, velocity):
    tiles = lax.axis_size("tm")
    spaces = lax.axis_size("space")
    times, rows, width = right_side.shape
    length = times * tiles
    tile = width // tiles
    around = (LANES - tile) // 2
    cas_table = jnp.asarray(hartley_table(length))
    coef_table = jnp.asarray(chebyshev_table(length))

    field = right_side.reshape(times * rows, width)
    windows = call(
        functools.partial(window_kernel, rows, times, tiles),
        [(tiles, 6 * times, LANES)],
        [(width // LANES, times * rows, LANES)],
    )(field)
    gathered = lax.all_to_all(windows, "tm", 0, 0)

    squares = velocity.astype(jnp.float32) ** 2
    planes = jnp.concatenate([kappa, squares[0], squares[1]], axis=0)
    planes = jnp.concatenate([planes[:, -around:], planes, planes[:, :around]], axis=1)
    local = lax.dynamic_slice_in_dim(planes, lax.axis_index("tm") * tile, LANES, 1)
    top, bottom = exchange(local, local, spaces)
    total = rows + 2 * HALO
    wide = call(
        functools.partial(weight_kernel, rows),
        [(total, 3 * BLOCK, SUB, LANES)],
        [(LANES, LANES)],
    )(local, top, bottom)

    tile_shape = (rows, BLOCK, SUB, LANES)
    edge_shape = (HALO, BLOCK, SUB, LANES)
    work = [(total, BLOCK, SUB, LANES), (total, BLOCK, SUB, LANES), tile_shape]
    span = LANES // 2 + 2 * SIDE
    freq, low, high = call(
        functools.partial(forward_kernel, rows, times, length),
        [tile_shape, edge_shape, edge_shape],
        [(rows * span, LANES)],
    )(cas_table, gathered)
    top, bottom = exchange(low, high, spaces)

    solved, applied, low, high, early = call(
        functools.partial(first_kernel, rows),
        [tile_shape, tile_shape, edge_shape, edge_shape, (2, SUB, LANES)],
        work,
    )(top, freq, bottom, wide, coef_table)
    top, bottom = exchange(low, high, spaces)

    groups = [
        [i * spaces + first + j for i in range(tiles) for j in range(NEAR)]
        for first in range(0, spaces, NEAR)
    ]
    solved_two, applied_two, sums = call(
        functools.partial(second_kernel, rows),
        [tile_shape, tile_shape, (tiles * NEAR, 1, LANES)],
        [*work, (2, SUB, LANES)],
    )(top, applied, bottom, wide, coef_table, early)
    packed = call(
        functools.partial(inverse_kernel, rows, times, length),
        [(tiles, 2 * rows * times, LANES)],
        [(rows * 4 * span, LANES)],
    )(cas_table, solved, solved_two, applied, applied_two)
    sums = lax.all_to_all(sums, ("tm", "space"), 0, 0, axis_index_groups=groups)
    sums = jnp.sum(sums, axis=0)
    returned = lax.all_to_all(packed, "tm", 0, 0)
    distance = NEAR
    while distance < spaces:
        pairs = [(i, i ^ distance) for i in range(spaces)]
        sums = sums + lax.ppermute(sums, "space", pairs)
        distance *= 2

    solution, residual = call(
        functools.partial(final_kernel, rows, times, tiles),
        [(times * rows, width), (times * rows, width)],
    )(returned, field, sums)
    shape = right_side.shape
    return solution.reshape(shape), residual.reshape(shape)


def solution(mesh):
    placed = (P("tm", "space", None), P("space", None), P(None, "space", None))
    return jax.shard_map(
        shards,
        mesh=mesh,
        in_specs=placed,
        out_specs=(P("tm", "space", None), P("tm", "space", None)),
        check_vma=False,
    )
```

```python
import functools
import math

import jax
import jax.numpy as jnp
import numpy as np
from jax import lax
from jax.experimental import pallas as pl
from jax.experimental.pallas import tpu as pltpu
from jax.sharding import PartitionSpec as P

CHEB = 4
COUPLING = 2.0
KAPPA_LOW = 0.05
KAPPA_HIGH = 1.0
REACH = 16.0

LANES = 128
SUB = 8
HALO = CHEB + 1
FAR = 2
SIDE = 16
BLOCK = 11
WINDOW = SUB * BLOCK
NEAR = 4
PARAMS = pltpu.CompilerParams(vmem_limit_bytes=24 * 1024 * 1024)


def hartley_table(length):
    index = np.arange(length)
    angle = (index[:, None] * index[None, :] % length) * (2.0 * math.pi / length)
    return ((np.cos(angle) + np.sin(angle)) / math.sqrt(length)).astype(np.float32)


def chebyshev_table(length):
    shift = COUPLING * (2.0 - 2.0 * np.cos(2.0 * math.pi * np.arange(length) / length))
    half = 0.5 * (KAPPA_HIGH + REACH - KAPPA_LOW)
    mid = 0.5 * (KAPPA_LOW + KAPPA_HIGH + REACH) + shift
    ratio = mid / half
    damp = 1.0 / ratio
    lines = [shift, 1.0 / mid]
    for _ in range(CHEB):
        damp_next = 1.0 / (2.0 * ratio - damp)
        lines += [damp_next * damp, 2.0 * damp_next / half]
        damp = damp_next
    return np.repeat(np.stack(lines).astype(np.float32)[:, None], SUB, 1)


def lane_index(shape):
    return lax.broadcasted_iota(jnp.int32, shape, len(shape) - 1)


def exact_dot(left, right, left_dim, right_dim):
    return lax.dot_general(
        left,
        right,
        (((left_dim,), (right_dim,)), ((), ())),
        precision=lax.Precision.HIGHEST,
        preferred_element_type=jnp.float32,
    )


def window_kernel(rows, times, tiles, source_ref, out_ref, scratch_ref):
    half = LANES // 2
    parts = source_ref.shape[1] // LANES
    for part in range(parts):
        scratch_ref[part] = source_ref[:, part * LANES : (part + 1) * LANES]
    lane = lane_index((times, LANES))
    fields = [
        [scratch_ref[part, pl.ds(row, times, stride=rows), :] for part in range(parts)]
        for row in range(rows)
    ]
    for pair in range(rows // 2):
        for part in range(parts):
            one, two = fields[2 * pair][part], fields[2 * pair + 1][part]
            place = slice(pair * times, (pair + 1) * times)
            out_ref[2 * part, place, :] = jnp.where(lane < half, one, pltpu.roll(two, half, 1))
            out_ref[2 * part + 1, place, :] = jnp.where(lane < half, pltpu.roll(one, half, 1), two)
    spread = 2 * SIDE
    group = LANES // spread
    for quad in range(rows // group):
        even = [None] * parts
        odd = [None] * parts
        for index in range(group):
            row = quad * group + index
            wide = jnp.concatenate(fields[row], axis=1)
            near = pltpu.roll(wide, spread * index + SIDE, 1)
            away = pltpu.roll(wide, (spread * index - half + SIDE) % wide.shape[1], 1)
            left = (lane >= spread * index) & (lane < spread * index + SIDE)
            right = (lane >= spread * index + SIDE) & (lane < spread * (index + 1))
            for part in range(parts):
                here = slice(part * LANES, (part + 1) * LANES)
                then = (part + 1) % parts
                then = slice(then * LANES, (then + 1) * LANES)
                if index == 0:
                    even[part] = jnp.where(left, near[:, here], away[:, here])
                    odd[part] = jnp.where(left, away[:, here], near[:, then])
                else:
                    even[part] = jnp.where(
                        left, near[:, here], jnp.where(right, away[:, here], even[part])
                    )
                    odd[part] = jnp.where(
                        left, away[:, here], jnp.where(right, near[:, then], odd[part])
                    )
        start = (rows // 2 + quad) * times
        for part in range(parts):
            out_ref[2 * part, start : start + times, :] = even[part]
            out_ref[2 * part + 1, start : start + times, :] = odd[part]


def forward_kernel(
    rows, times, length, cas_ref, field_ref, *refs
):
    out_ref, low_ref, high_ref, line_ref = refs[-4:]
    half = LANES // 2
    span = half + 2 * SIDE
    pieces = field_ref.shape[1] // times
    group = LANES // (2 * SIDE)
    for piece in range(pieces):
        block = field_ref[:, piece * times : (piece + 1) * times, :].reshape(length, LANES)
        freq = exact_dot(block, cas_ref[...], 0, 0)
        if piece < rows // 2:
            for part in range(2):
                start = (2 * piece + part) * span + SIDE
                line_ref[start : start + half, :] = freq[part * half : (part + 1) * half]
        else:
            for index in range(group):
                start = ((piece - rows // 2) * group + index) * span
                place = 2 * SIDE * index
                line_ref[start : start + SIDE, :] = freq[place : place + SIDE]
                line_ref[start + SIDE + half : start + span, :] = freq[
                    place + SIDE : place + 2 * SIDE
                ]
    skip = (span - WINDOW) // 2
    for row in range(rows):
        for column in range(BLOCK):
            value = line_ref[pl.ds(row * span + skip + column, SUB, stride=BLOCK), :]
            out_ref[row, column] = value
            if row < FAR:
                low_ref[row, column] = value
            if row >= rows - FAR:
                high_ref[row - (rows - FAR), column] = value


def weight_kernel(
    rows, local_ref, top_ref, bottom_ref, top_far_ref, bottom_far_ref, wide_ref, scratch_ref
):
    planes = []
    for plane in range(3):
        start = plane * rows
        planes.append(
            jnp.concatenate(
                [
                    top_far_ref[start + rows - FAR : start + rows, :],
                    top_ref[start : start + rows, :],
                    local_ref[start : start + rows, :],
                    bottom_ref[start : start + rows, :],
                    bottom_far_ref[start : start + FAR, :],
                ],
                axis=0,
            )
        )
    east = 1.0 + 0.125 * (planes[1] + jnp.concatenate([planes[1][1:], planes[1][:1]], axis=0))
    north = 1.0 + 0.125 * (planes[2] + pltpu.roll(planes[2], LANES - 1, 1))
    total = planes[0].shape[0]
    zero = jnp.zeros((LANES - 3 * total, LANES), jnp.float32)
    scratch_ref[...] = jnp.transpose(jnp.concatenate([planes[0], east, north, zero], axis=0))
    skip = (LANES - WINDOW) // 2
    for column in range(BLOCK):
        lines = scratch_ref[pl.ds(skip + column, SUB, stride=BLOCK), :]
        for row in range(total):
            for plane in range(3):
                index = plane * total + row
                wide_ref[row, plane * BLOCK + column] = jnp.broadcast_to(
                    lines[:, index : index + 1], (SUB, LANES)
                )


def own_columns(column):
    place = lax.broadcasted_iota(jnp.int32, (SUB, LANES), 0) * BLOCK + column
    first = (WINDOW - LANES // 2) // 2
    return (place >= first) & (place < first + LANES // 2)


def passes(edge, own, sources, wide_ref, coef_ref, step_ref, remain_ref, solved_ref, emit):
    total = step_ref.shape[0]
    columns = range(BLOCK)

    for turn in range(CHEB + 1):
        first, last = edge + turn + 1, total - edge - turn - 1

        def row_step(row, carry, *, turn, place):
            here, flux = carry[:BLOCK], carry[BLOCK:]
            after = [step_ref[row + 1, column] for column in columns]
            ahead = [wide_ref[row, BLOCK + column] * (here[column] - after[column]) for column in columns]
            beside = list(here[1:]) + [pltpu.roll(here[0], SUB - 1, 0)]
            side = [wide_ref[row, 2 * BLOCK + column] * (here[column] - beside[column]) for column in columns]
            behind = [pltpu.roll(side[-1], 1, 0)] + side[:-1]
            inside = place == 1
            results = []
            for column in columns:
                applied = (
                    (wide_ref[row, column] + coef_ref[0]) * here[column]
                    + (ahead[column] - flux[column])
                    + (side[column] - behind[column])
                )
                left = remain_ref[row, column] - applied
                if turn < CHEB:
                    remain_ref[row, column] = left
                    step_ref[row, column] = (
                        coef_ref[2 + 2 * turn] * here[column] + coef_ref[3 + 2 * turn] * left
                    )
                solved = here[column]
                if inside and turn > 0:
                    solved = solved_ref[row - own[0], column] + solved
                if inside and turn < CHEB:
                    solved_ref[row - own[0], column] = solved
                if turn == CHEB:
                    source = sources[place](row, column)
                    results.append((source, solved, source - left))
            if turn == CHEB:
                emit(row, inside, *zip(*results))
            return (*after, *ahead)

        here = [step_ref[first, column] for column in columns]
        flux = [
            wide_ref[first - 1, BLOCK + column] * (step_ref[first - 1, column] - here[column])
            for column in columns
        ]
        carry = (*here, *flux)
        for place, (low, high) in enumerate(((first, own[0]), own, (own[1], last))):
            if low < high:
                step = functools.partial(row_step, turn=turn, place=place)
                carry = lax.fori_loop(low, high, step, carry)


def stencil_kernel(
    rows, top_far_ref, top_ref, field_ref, bottom_ref, bottom_far_ref, wide_ref, coef_ref,
    solved_ref, applied_ref, solved_two_ref, applied_two_ref, sums_ref,
    step_ref, remain_ref, part_ref, line_ref,
):
    columns = range(BLOCK)
    offset = 0
    for ref in (top_far_ref, top_ref, field_ref, bottom_ref, bottom_far_ref):

        @pl.loop(0, ref.shape[0])
        def _(row, ref=ref, offset=offset):
            for column in columns:
                value = ref[row, column]
                remain_ref[offset + row, column] = value
                step_ref[offset + row, column] = coef_ref[1] * value

        offset += ref.shape[0]

    own = (FAR + rows, FAR + 2 * rows)
    line_ref[...] = jnp.zeros_like(line_ref)

    def add(index, one, two):
        total = None
        for column in columns:
            product = jnp.where(own_columns(column), one[column] * two[column], 0.0)
            total = product if total is None else total + product
        line_ref[index] = line_ref[index] + total

    def emit_first(row, inside, source, solved, applied):
        for column in columns:
            remain_ref[row, column] = applied[column]
            step_ref[row, column] = coef_ref[1] * applied[column]
        if inside:
            for column in columns:
                solved_ref[row - own[0], column] = solved[column]
                applied_ref[row - own[0], column] = applied[column]
            add(0, source, solved)
            add(1, solved, applied)

    def emit_second(row, inside, source, solved, applied):
        for column in columns:
            solved_two_ref[row - own[0], column] = solved[column]
            applied_two_ref[row - own[0], column] = applied[column]
        add(2, source, solved)
        add(3, solved, applied)

    work = (wide_ref, coef_ref, step_ref, remain_ref, part_ref)
    sources = (
        lambda row, column: top_ref[row - FAR, column],
        lambda row, column: field_ref[row - own[0], column],
        lambda row, column: bottom_ref[row - own[1], column],
    )
    passes(0, own, sources, *work, emit_first)
    sources = (None, lambda row, column: applied_ref[row - own[0], column], None)
    passes(HALO, own, sources, *work, emit_second)

    lane = lane_index((1, LANES))
    line = jnp.zeros((1, LANES), jnp.float32)
    for index in range(4):
        line = jnp.where(lane == index, jnp.sum(line_ref[index]), line)
    sums_ref[...] = jnp.broadcast_to(line[None], sums_ref.shape)


def inverse_kernel(rows, times, length, cas_ref, one_ref, two_ref, three_ref, four_ref, out_ref, line_ref):
    half = LANES // 2
    span = half + 2 * SIDE
    skip = (span - WINDOW) // 2
    refs = (one_ref, two_ref, three_ref, four_ref)
    for row in range(rows):
        for index, ref in enumerate(refs):
            for column in range(BLOCK):
                start = (row * len(refs) + index) * span + skip + column
                line_ref[pl.ds(start, SUB, stride=BLOCK), :] = ref[row, column]
    for row in range(rows):
        for pair in range(2):
            start = (row * len(refs) + 2 * pair) * span + SIDE
            points = jnp.concatenate(
                [line_ref[start : start + half, :], line_ref[start + span : start + span + half, :]],
                axis=0,
            )
            back = exact_dot(cas_ref[...], points, 1, 1).reshape(length // times, times, LANES)
            place = (pair * rows + row) * times
            out_ref[:, place : place + times, :] = back


def final_kernel(rows, times, tiles, source_ref, field_ref, sums_ref, solution_ref, residual_ref):
    line = sums_ref[...]
    gamma, curved, cross, last = (
        jnp.broadcast_to(line[:, index : index + 1], (times, LANES)) for index in range(4)
    )
    step = gamma / curved
    gamma_next = step * step * cross - gamma
    turn = gamma_next / gamma
    grown = 1.0 + turn
    next_curved = grown * grown * curved - 2.0 * step * grown * cross + step * step * last
    next_step = gamma_next / next_curved
    low = lane_index((times, LANES)) < LANES // 2
    scale = jnp.where(low, step + next_step * grown, -next_step * step)
    for time in range(times):
        place = slice(time * rows, (time + 1) * rows)
        for pair in range(tiles // 2):
            columns = slice(pair * LANES, (pair + 1) * LANES)
            merged = []
            for part in range(2):
                taken = pl.ds(part * rows * times + time, rows, stride=times)
                left = scale * source_ref[2 * pair, taken, :]
                right = scale * source_ref[2 * pair + 1, taken, :]
                left = left + pltpu.roll(left, LANES // 2, 1)
                right = right + pltpu.roll(right, LANES // 2, 1)
                merged.append(jnp.where(low, left, right))
            solution_ref[place, columns] = merged[0]
            residual_ref[place, columns] = field_ref[place, columns] - merged[1]


def call(kernel, out_shape, scratch=(), unread=0, inputs=0):
    shapes = [jax.ShapeDtypeStruct(shape, jnp.float32) for shape in out_shape]
    specs = {}
    if unread:
        whole = pl.BlockSpec(memory_space=pltpu.VMEM)
        specs["in_specs"] = [whole] * (inputs - unread) + [pl.BlockSpec(memory_space=pl.ANY)] * unread
    return pl.pallas_call(
        kernel,
        out_shape=shapes[0] if len(shapes) == 1 else shapes,
        scratch_shapes=[pltpu.VMEM(shape, jnp.float32) for shape in scratch],
        compiler_params=PARAMS,
        **specs,
    )


def shift(value, distance, spaces):
    return lax.ppermute(value, "space", [(i, (i + distance) % spaces) for i in range(spaces)])


def shards(right_side, kappa, velocity):
    tiles = lax.axis_size("tm")
    spaces = lax.axis_size("space")
    times, rows, width = right_side.shape
    length = times * tiles
    tile = width // tiles
    around = (LANES - tile) // 2
    cas_table = jnp.asarray(hartley_table(length))
    coef_table = jnp.asarray(chebyshev_table(length))

    field = right_side.reshape(times * rows, width)
    windows = call(
        functools.partial(window_kernel, rows, times, tiles),
        [(tiles, 6 * times, LANES)],
        [(width // LANES, times * rows, LANES)],
    )(field)
    gathered = lax.all_to_all(windows, "tm", 0, 0)

    squares = velocity.astype(jnp.float32) ** 2
    planes = jnp.concatenate([kappa, squares[0], squares[1]], axis=0)
    planes = jnp.concatenate([planes[:, -around:], planes, planes[:, :around]], axis=1)
    local = lax.dynamic_slice_in_dim(planes, lax.axis_index("tm") * tile, LANES, 1)
    edges = [shift(local, distance, spaces) for distance in (1, -1, 2, -2)]
    total = 3 * rows + 2 * FAR
    wide = call(
        functools.partial(weight_kernel, rows),
        [(total, 3 * BLOCK, SUB, LANES)],
        [(LANES, LANES)],
    )(local, *edges)

    tile_shape = (rows, BLOCK, SUB, LANES)
    far_shape = (FAR, BLOCK, SUB, LANES)
    span = LANES // 2 + 2 * SIDE
    freq, low, high = call(
        functools.partial(forward_kernel, rows, times, length),
        [tile_shape, far_shape, far_shape],
        [(rows * span, LANES)],
        unread=len(edges),
        inputs=2 + len(edges),
    )(cas_table, gathered, *edges)
    top, bottom = shift(freq, 1, spaces), shift(freq, -1, spaces)
    top_far, bottom_far = shift(high, 2, spaces), shift(low, -2, spaces)

    groups = [
        [i * spaces + first + j for i in range(tiles) for j in range(NEAR)]
        for first in range(0, spaces, NEAR)
    ]
    work = (total, BLOCK, SUB, LANES)
    solved, applied, solved_two, applied_two, sums = call(
        functools.partial(stencil_kernel, rows),
        [tile_shape] * 4 + [(tiles * NEAR, 1, LANES)],
        [work, work, tile_shape, (4, SUB, LANES)],
    )(top_far, top, freq, bottom, bottom_far, wide, coef_table)
    packed = call(
        functools.partial(inverse_kernel, rows, times, length),
        [(tiles, 2 * rows * times, LANES)],
        [(rows * 4 * span, LANES)],
    )(cas_table, solved, solved_two, applied, applied_two)
    sums = lax.all_to_all(sums, ("tm", "space"), 0, 0, axis_index_groups=groups)
    sums = jnp.sum(sums, axis=0)
    returned = lax.all_to_all(packed, "tm", 0, 0)
    distance = NEAR
    while distance < spaces:
        pairs = [(i, i ^ distance) for i in range(spaces)]
        sums = sums + lax.ppermute(sums, "space", pairs)
        distance *= 2

    solution, residual = call(
        functools.partial(final_kernel, rows, times, tiles),
        [(times * rows, width), (times * rows, width)],
    )(returned, field, sums)
    shape = right_side.shape
    return solution.reshape(shape), residual.reshape(shape)


def solution(mesh):
    placed = (P("tm", "space", None), P("space", None), P(None, "space", None))
    return jax.shard_map(
        shards,
        mesh=mesh,
        in_specs=placed,
        out_specs=(P("tm", "space", None), P("tm", "space", None)),
        check_vma=False,
    )
```

```python
import functools
import math

import jax
import jax.numpy as jnp
import numpy as np
from jax import lax
from jax.experimental import pallas as pl
from jax.experimental.pallas import tpu as pltpu
from jax.sharding import PartitionSpec as P

CHEB = 4
COUPLING = 2.0
KAPPA_LOW = 0.05
KAPPA_HIGH = 1.0
REACH = 16.0

LANES = 128
SUB = 8
HALO = CHEB + 1
FAR = 2
SIDE = 16
BLOCK = 11
WINDOW = SUB * BLOCK
NEAR = 4
PARAMS = pltpu.CompilerParams(vmem_limit_bytes=24 * 1024 * 1024)


def hartley_table(length):
    index = np.arange(length)
    angle = (index[:, None] * index[None, :] % length) * (2.0 * math.pi / length)
    return ((np.cos(angle) + np.sin(angle)) / math.sqrt(length)).astype(np.float32)


def chebyshev_table(length):
    shift = COUPLING * (2.0 - 2.0 * np.cos(2.0 * math.pi * np.arange(length) / length))
    half = 0.5 * (KAPPA_HIGH + REACH - KAPPA_LOW)
    mid = 0.5 * (KAPPA_LOW + KAPPA_HIGH + REACH) + shift
    ratio = mid / half
    damp = 1.0 / ratio
    lines = [shift, 1.0 / mid]
    for _ in range(CHEB):
        damp_next = 1.0 / (2.0 * ratio - damp)
        lines += [damp_next * damp, 2.0 * damp_next / half]
        damp = damp_next
    return np.repeat(np.stack(lines).astype(np.float32)[:, None], SUB, 1)


def lane_index(shape):
    return lax.broadcasted_iota(jnp.int32, shape, len(shape) - 1)


def exact_dot(left, right, left_dim, right_dim):
    return lax.dot_general(
        left,
        right,
        (((left_dim,), (right_dim,)), ((), ())),
        precision=lax.Precision.HIGHEST,
        preferred_element_type=jnp.float32,
    )


def window_kernel(rows, times, tiles, source_ref, out_ref, scratch_ref):
    half = LANES // 2
    parts = source_ref.shape[1] // LANES
    for part in range(parts):
        scratch_ref[part] = source_ref[:, part * LANES : (part + 1) * LANES]
    lane = lane_index((times, LANES))
    fields = [
        [scratch_ref[part, pl.ds(row, times, stride=rows), :] for part in range(parts)]
        for row in range(rows)
    ]
    for pair in range(rows // 2):
        for part in range(parts):
            one, two = fields[2 * pair][part], fields[2 * pair + 1][part]
            place = slice(pair * times, (pair + 1) * times)
            out_ref[2 * part, place, :] = jnp.where(lane < half, one, pltpu.roll(two, half, 1))
            out_ref[2 * part + 1, place, :] = jnp.where(lane < half, pltpu.roll(one, half, 1), two)
    spread = 2 * SIDE
    group = LANES // spread
    for quad in range(rows // group):
        even = [None] * parts
        odd = [None] * parts
        for index in range(group):
            row = quad * group + index
            wide = jnp.concatenate(fields[row], axis=1)
            near = pltpu.roll(wide, spread * index + SIDE, 1)
            away = pltpu.roll(wide, (spread * index - half + SIDE) % wide.shape[1], 1)
            left = (lane >= spread * index) & (lane < spread * index + SIDE)
            right = (lane >= spread * index + SIDE) & (lane < spread * (index + 1))
            for part in range(parts):
                here = slice(part * LANES, (part + 1) * LANES)
                then = (part + 1) % parts
                then = slice(then * LANES, (then + 1) * LANES)
                if index == 0:
                    even[part] = jnp.where(left, near[:, here], away[:, here])
                    odd[part] = jnp.where(left, away[:, here], near[:, then])
                else:
                    even[part] = jnp.where(
                        left, near[:, here], jnp.where(right, away[:, here], even[part])
                    )
                    odd[part] = jnp.where(
                        left, away[:, here], jnp.where(right, near[:, then], odd[part])
                    )
        start = (rows // 2 + quad) * times
        for part in range(parts):
            out_ref[2 * part, start : start + times, :] = even[part]
            out_ref[2 * part + 1, start : start + times, :] = odd[part]


def forward_kernel(
    rows, times, length, cas_ref, field_ref, local_ref, out_ref, low_ref, high_ref, line_ref
):
    half = LANES // 2
    span = half + 2 * SIDE
    pieces = field_ref.shape[1] // times
    group = LANES // (2 * SIDE)
    for piece in range(pieces):
        block = field_ref[:, piece * times : (piece + 1) * times, :].reshape(length, LANES)
        freq = exact_dot(block, cas_ref[...], 0, 0)
        if piece < rows // 2:
            for part in range(2):
                start = (2 * piece + part) * span + SIDE
                line_ref[start : start + half, :] = freq[part * half : (part + 1) * half]
        else:
            for index in range(group):
                start = ((piece - rows // 2) * group + index) * span
                place = 2 * SIDE * index
                line_ref[start : start + SIDE, :] = freq[place : place + SIDE]
                line_ref[start + SIDE + half : start + span, :] = freq[
                    place + SIDE : place + 2 * SIDE
                ]
    skip = (span - WINDOW) // 2
    for row in range(rows):
        for column in range(BLOCK):
            value = line_ref[pl.ds(row * span + skip + column, SUB, stride=BLOCK), :]
            out_ref[row * BLOCK + column] = value
            if row < FAR:
                low_ref[row * BLOCK + column] = value
            if row >= rows - FAR:
                high_ref[(row - (rows - FAR)) * BLOCK + column] = value
    for ref in (out_ref, low_ref, high_ref):
        first = ref.shape[0] - 3
        for plane in range(3):
            ref[first + plane] = local_ref[plane * rows : (plane + 1) * rows, :]


def weight_step(rows, refs, wide_ref, scratch_ref):
    planes = []
    for plane in range(3):
        blocks = [ref[ref.shape[0] - 3 + plane] for ref in refs]
        blocks[0] = blocks[0][rows - FAR :]
        blocks[-1] = blocks[-1][:FAR]
        planes.append(jnp.concatenate(blocks, axis=0))
    east = 1.0 + 0.125 * (planes[1] + jnp.concatenate([planes[1][1:], planes[1][:1]], axis=0))
    north = 1.0 + 0.125 * (planes[2] + pltpu.roll(planes[2], LANES - 1, 1))
    total = planes[0].shape[0]
    zero = jnp.zeros((LANES - 3 * total, LANES), jnp.float32)
    scratch_ref[...] = jnp.transpose(jnp.concatenate([planes[0], east, north, zero], axis=0))
    skip = (LANES - WINDOW) // 2
    for column in range(BLOCK):
        lines = scratch_ref[pl.ds(skip + column, SUB, stride=BLOCK), :]
        for row in range(total):
            for plane in range(3):
                index = plane * total + row
                wide_ref[row, plane * BLOCK + column] = jnp.broadcast_to(
                    lines[:, index : index + 1], (SUB, LANES)
                )


def own_columns(column):
    place = lax.broadcasted_iota(jnp.int32, (SUB, LANES), 0) * BLOCK + column
    first = (WINDOW - LANES // 2) // 2
    return (place >= first) & (place < first + LANES // 2)


def passes(edge, own, sources, wide_ref, coef_ref, step_ref, remain_ref, solved_ref, emit):
    total = step_ref.shape[0]
    columns = range(BLOCK)

    for turn in range(CHEB + 1):
        first, last = edge + turn + 1, total - edge - turn - 1

        def row_step(row, carry, *, turn, place):
            here, flux = carry[:BLOCK], carry[BLOCK:]
            after = [step_ref[row + 1, column] for column in columns]
            ahead = [wide_ref[row, BLOCK + column] * (here[column] - after[column]) for column in columns]
            beside = list(here[1:]) + [pltpu.roll(here[0], SUB - 1, 0)]
            side = [wide_ref[row, 2 * BLOCK + column] * (here[column] - beside[column]) for column in columns]
            behind = [pltpu.roll(side[-1], 1, 0)] + side[:-1]
            inside = place == 1
            results = []
            for column in columns:
                applied = (
                    (wide_ref[row, column] + coef_ref[0]) * here[column]
                    + (ahead[column] - flux[column])
                    + (side[column] - behind[column])
                )
                left = remain_ref[row, column] - applied
                if turn < CHEB:
                    remain_ref[row, column] = left
                    step_ref[row, column] = (
                        coef_ref[2 + 2 * turn] * here[column] + coef_ref[3 + 2 * turn] * left
                    )
                solved = here[column]
                if inside and turn > 0:
                    solved = solved_ref[row - own[0], column] + solved
                if inside and turn < CHEB:
                    solved_ref[row - own[0], column] = solved
                if turn == CHEB:
                    source = sources[place](row, column)
                    results.append((source, solved, source - left))
            if turn == CHEB:
                emit(row, inside, *zip(*results))
            return (*after, *ahead)

        here = [step_ref[first, column] for column in columns]
        flux = [
            wide_ref[first - 1, BLOCK + column] * (step_ref[first - 1, column] - here[column])
            for column in columns
        ]
        carry = (*here, *flux)
        for place, (low, high) in enumerate(((first, own[0]), own, (own[1], last))):
            if low < high:
                step = functools.partial(row_step, turn=turn, place=place)
                carry = lax.fori_loop(low, high, step, carry)


def stencil_kernel(
    rows, top_far_ref, top_ref, field_ref, bottom_ref, bottom_far_ref, coef_ref,
    solved_ref, applied_ref, solved_two_ref, applied_two_ref, sums_ref,
    step_ref, remain_ref, part_ref, line_ref, wide_ref, scratch_ref,
):
    columns = range(BLOCK)
    refs = (top_far_ref, top_ref, field_ref, bottom_ref, bottom_far_ref)
    weight_step(rows, refs, wide_ref, scratch_ref)
    offset = 0
    for ref in refs:
        count = (ref.shape[0] - 3) // BLOCK

        @pl.loop(0, count)
        def _(row, ref=ref, offset=offset):
            for column in columns:
                value = ref[row * BLOCK + column]
                remain_ref[offset + row, column] = value
                step_ref[offset + row, column] = coef_ref[1] * value

        offset += count

    own = (FAR + rows, FAR + 2 * rows)
    line_ref[...] = jnp.zeros_like(line_ref)

    def add(index, one, two):
        total = None
        for column in columns:
            product = jnp.where(own_columns(column), one[column] * two[column], 0.0)
            total = product if total is None else total + product
        line_ref[index] = line_ref[index] + total

    def emit_first(row, inside, source, solved, applied):
        for column in columns:
            remain_ref[row, column] = applied[column]
            step_ref[row, column] = coef_ref[1] * applied[column]
        if inside:
            for column in columns:
                solved_ref[row - own[0], column] = solved[column]
                applied_ref[row - own[0], column] = applied[column]
            add(0, source, solved)
            add(1, solved, applied)

    def emit_second(row, inside, source, solved, applied):
        for column in columns:
            solved_two_ref[row - own[0], column] = solved[column]
            applied_two_ref[row - own[0], column] = applied[column]
        add(2, source, solved)
        add(3, solved, applied)

    work = (wide_ref, coef_ref, step_ref, remain_ref, part_ref)
    sources = (
        lambda row, column: top_ref[(row - FAR) * BLOCK + column],
        lambda row, column: field_ref[(row - own[0]) * BLOCK + column],
        lambda row, column: bottom_ref[(row - own[1]) * BLOCK + column],
    )
    passes(0, own, sources, *work, emit_first)
    sources = (None, lambda row, column: applied_ref[row - own[0], column], None)
    passes(HALO, own, sources, *work, emit_second)

    lane = lane_index((1, LANES))
    line = jnp.zeros((1, LANES), jnp.float32)
    for index in range(4):
        line = jnp.where(lane == index, jnp.sum(line_ref[index]), line)
    sums_ref[...] = jnp.broadcast_to(line[None], sums_ref.shape)


def inverse_kernel(rows, times, length, cas_ref, one_ref, two_ref, three_ref, four_ref, out_ref, line_ref):
    half = LANES // 2
    span = half + 2 * SIDE
    skip = (span - WINDOW) // 2
    refs = (one_ref, two_ref, three_ref, four_ref)
    for row in range(rows):
        for index, ref in enumerate(refs):
            for column in range(BLOCK):
                start = (row * len(refs) + index) * span + skip + column
                line_ref[pl.ds(start, SUB, stride=BLOCK), :] = ref[row, column]
    for row in range(rows):
        for pair in range(2):
            start = (row * len(refs) + 2 * pair) * span + SIDE
            points = jnp.concatenate(
                [line_ref[start : start + half, :], line_ref[start + span : start + span + half, :]],
                axis=0,
            )
            back = exact_dot(cas_ref[...], points, 1, 1).reshape(length // times, times, LANES)
            place = (pair * rows + row) * times
            out_ref[:, place : place + times, :] = back


def final_kernel(rows, times, tiles, source_ref, field_ref, sums_ref, solution_ref, residual_ref):
    line = sums_ref[...]
    gamma, curved, cross, last = (
        jnp.broadcast_to(line[:, index : index + 1], (times, LANES)) for index in range(4)
    )
    step = gamma / curved
    gamma_next = step * step * cross - gamma
    turn = gamma_next / gamma
    grown = 1.0 + turn
    next_curved = grown * grown * curved - 2.0 * step * grown * cross + step * step * last
    next_step = gamma_next / next_curved
    low = lane_index((times, LANES)) < LANES // 2
    scale = jnp.where(low, step + next_step * grown, -next_step * step)
    for time in range(times):
        place = slice(time * rows, (time + 1) * rows)
        for pair in range(tiles // 2):
            columns = slice(pair * LANES, (pair + 1) * LANES)
            merged = []
            for part in range(2):
                taken = pl.ds(part * rows * times + time, rows, stride=times)
                left = scale * source_ref[2 * pair, taken, :]
                right = scale * source_ref[2 * pair + 1, taken, :]
                left = left + pltpu.roll(left, LANES // 2, 1)
                right = right + pltpu.roll(right, LANES // 2, 1)
                merged.append(jnp.where(low, left, right))
            solution_ref[place, columns] = merged[0]
            residual_ref[place, columns] = field_ref[place, columns] - merged[1]


def call(kernel, out_shape, scratch=()):
    shapes = [jax.ShapeDtypeStruct(shape, jnp.float32) for shape in out_shape]
    return pl.pallas_call(
        kernel,
        out_shape=shapes[0] if len(shapes) == 1 else shapes,
        scratch_shapes=[pltpu.VMEM(shape, jnp.float32) for shape in scratch],
        compiler_params=PARAMS,
    )


def shift(value, distance, spaces):
    return lax.ppermute(value, "space", [(i, (i + distance) % spaces) for i in range(spaces)])


def shards(right_side, kappa, velocity):
    tiles = lax.axis_size("tm")
    spaces = lax.axis_size("space")
    times, rows, width = right_side.shape
    length = times * tiles
    tile = width // tiles
    around = (LANES - tile) // 2
    cas_table = jnp.asarray(hartley_table(length))
    coef_table = jnp.asarray(chebyshev_table(length))

    field = right_side.reshape(times * rows, width)
    windows = call(
        functools.partial(window_kernel, rows, times, tiles),
        [(tiles, 6 * times, LANES)],
        [(width // LANES, times * rows, LANES)],
    )(field)
    gathered = lax.all_to_all(windows, "tm", 0, 0)

    squares = velocity.astype(jnp.float32) ** 2
    planes = jnp.concatenate([kappa, squares[0], squares[1]], axis=0)
    planes = jnp.concatenate([planes[:, -around:], planes, planes[:, :around]], axis=1)
    local = lax.dynamic_slice_in_dim(planes, lax.axis_index("tm") * tile, LANES, 1)
    total = 3 * rows + 2 * FAR
    tile_shape = (rows, BLOCK, SUB, LANES)
    row_shape = (rows * BLOCK + 3, SUB, LANES)
    far_shape = (FAR * BLOCK + 3, SUB, LANES)
    span = LANES // 2 + 2 * SIDE
    freq, low, high = call(
        functools.partial(forward_kernel, rows, times, length),
        [row_shape, far_shape, far_shape],
        [(rows * span, LANES)],
    )(cas_table, gathered, local)
    top, bottom = shift(freq, 1, spaces), shift(freq, -1, spaces)
    top_far, bottom_far = shift(high, 2, spaces), shift(low, -2, spaces)

    groups = [
        [i * spaces + first + j for i in range(tiles) for j in range(NEAR)]
        for first in range(0, spaces, NEAR)
    ]
    work = (total, BLOCK, SUB, LANES)
    solved, applied, solved_two, applied_two, sums = call(
        functools.partial(stencil_kernel, rows),
        [tile_shape] * 4 + [(tiles * NEAR, 1, LANES)],
        [
            work,
            work,
            tile_shape,
            (4, SUB, LANES),
            (total, 3 * BLOCK, SUB, LANES),
            (LANES, LANES),
        ],
    )(top_far, top, freq, bottom, bottom_far, coef_table)
    packed = call(
        functools.partial(inverse_kernel, rows, times, length),
        [(tiles, 2 * rows * times, LANES)],
        [(rows * 4 * span, LANES)],
    )(cas_table, solved, solved_two, applied, applied_two)
    sums = lax.all_to_all(sums, ("tm", "space"), 0, 0, axis_index_groups=groups)
    sums = jnp.sum(sums, axis=0)
    returned = lax.all_to_all(packed, "tm", 0, 0)
    distance = NEAR
    while distance < spaces:
        pairs = [(i, i ^ distance) for i in range(spaces)]
        sums = sums + lax.ppermute(sums, "space", pairs)
        distance *= 2

    solution, residual = call(
        functools.partial(final_kernel, rows, times, tiles),
        [(times * rows, width), (times * rows, width)],
    )(returned, field, sums)
    shape = right_side.shape
    return solution.reshape(shape), residual.reshape(shape)


def solution(mesh):
    placed = (P("tm", "space", None), P("space", None), P(None, "space", None))
    return jax.shard_map(
        shards,
        mesh=mesh,
        in_specs=placed,
        out_specs=(P("tm", "space", None), P("tm", "space", None)),
        check_vma=False,
    )
```

```python
import functools
import math

import jax
import jax.numpy as jnp
import numpy as np
from jax import lax
from jax.experimental import pallas as pl
from jax.experimental.pallas import tpu as pltpu
from jax.sharding import PartitionSpec as P

CHEB = 4
COUPLING = 2.0
KAPPA_LOW = 0.05
KAPPA_HIGH = 1.0
REACH = 16.0

LANES = 128
SUB = 8
HALO = CHEB + 1
FAR = 2
SIDE = 16
BLOCK = 11
WINDOW = SUB * BLOCK
NEAR = 4
PARAMS = pltpu.CompilerParams(vmem_limit_bytes=24 * 1024 * 1024)


def hartley_table(length):
    index = np.arange(length)
    angle = (index[:, None] * index[None, :] % length) * (2.0 * math.pi / length)
    return ((np.cos(angle) + np.sin(angle)) / math.sqrt(length)).astype(np.float32)


def chebyshev_table(length):
    shift = COUPLING * (2.0 - 2.0 * np.cos(2.0 * math.pi * np.arange(length) / length))
    half = 0.5 * (KAPPA_HIGH + REACH - KAPPA_LOW)
    mid = 0.5 * (KAPPA_LOW + KAPPA_HIGH + REACH) + shift
    ratio = mid / half
    damp = 1.0 / ratio
    lines = [shift, 1.0 / mid]
    for _ in range(CHEB):
        damp_next = 1.0 / (2.0 * ratio - damp)
        lines += [damp_next * damp, 2.0 * damp_next / half]
        damp = damp_next
    return np.repeat(np.stack(lines).astype(np.float32)[:, None], SUB, 1)


def lane_index(shape):
    return lax.broadcasted_iota(jnp.int32, shape, len(shape) - 1)


def exact_dot(left, right, left_dim, right_dim):
    return lax.dot_general(
        left,
        right,
        (((left_dim,), (right_dim,)), ((), ())),
        precision=lax.Precision.HIGHEST,
        preferred_element_type=jnp.float32,
    )


def window_kernel(rows, times, tiles, source_ref, out_ref, scratch_ref):
    half = LANES // 2
    parts = source_ref.shape[1] // LANES
    for part in range(parts):
        scratch_ref[part] = source_ref[:, part * LANES : (part + 1) * LANES]
    lane = lane_index((times, LANES))
    fields = [
        [scratch_ref[part, pl.ds(row, times, stride=rows), :] for part in range(parts)]
        for row in range(rows)
    ]
    for pair in range(rows // 2):
        for part in range(parts):
            one, two = fields[2 * pair][part], fields[2 * pair + 1][part]
            place = slice(pair * times, (pair + 1) * times)
            out_ref[2 * part, place, :] = jnp.where(lane < half, one, pltpu.roll(two, half, 1))
            out_ref[2 * part + 1, place, :] = jnp.where(lane < half, pltpu.roll(one, half, 1), two)
    spread = 2 * SIDE
    group = LANES // spread
    for quad in range(rows // group):
        even = [None] * parts
        odd = [None] * parts
        for index in range(group):
            row = quad * group + index
            wide = jnp.concatenate(fields[row], axis=1)
            near = pltpu.roll(wide, spread * index + SIDE, 1)
            away = pltpu.roll(wide, (spread * index - half + SIDE) % wide.shape[1], 1)
            left = (lane >= spread * index) & (lane < spread * index + SIDE)
            right = (lane >= spread * index + SIDE) & (lane < spread * (index + 1))
            for part in range(parts):
                here = slice(part * LANES, (part + 1) * LANES)
                then = (part + 1) % parts
                then = slice(then * LANES, (then + 1) * LANES)
                if index == 0:
                    even[part] = jnp.where(left, near[:, here], away[:, here])
                    odd[part] = jnp.where(left, away[:, here], near[:, then])
                else:
                    even[part] = jnp.where(
                        left, near[:, here], jnp.where(right, away[:, here], even[part])
                    )
                    odd[part] = jnp.where(
                        left, away[:, here], jnp.where(right, near[:, then], odd[part])
                    )
        start = (rows // 2 + quad) * times
        for part in range(parts):
            out_ref[2 * part, start : start + times, :] = even[part]
            out_ref[2 * part + 1, start : start + times, :] = odd[part]


def forward_kernel(
    rows, times, length, cas_ref, field_ref, local_ref, out_ref, low_ref, high_ref, line_ref
):
    half = LANES // 2
    span = half + 2 * SIDE
    pieces = field_ref.shape[1] // times
    group = LANES // (2 * SIDE)
    for piece in range(pieces):
        block = field_ref[:, piece * times : (piece + 1) * times, :].reshape(length, LANES)
        freq = exact_dot(block, cas_ref[...], 0, 0)
        if piece < rows // 2:
            for part in range(2):
                start = (2 * piece + part) * span + SIDE
                line_ref[start : start + half, :] = freq[part * half : (part + 1) * half]
        else:
            for index in range(group):
                start = ((piece - rows // 2) * group + index) * span
                place = 2 * SIDE * index
                line_ref[start : start + SIDE, :] = freq[place : place + SIDE]
                line_ref[start + SIDE + half : start + span, :] = freq[
                    place + SIDE : place + 2 * SIDE
                ]
    skip = (span - WINDOW) // 2
    for row in range(rows):
        for column in range(BLOCK):
            value = line_ref[pl.ds(row * span + skip + column, SUB, stride=BLOCK), :]
            out_ref[row * BLOCK + column] = value
            if row < FAR:
                low_ref[row * BLOCK + column] = value
            if row >= rows - FAR:
                high_ref[(row - (rows - FAR)) * BLOCK + column] = value
    for ref in (out_ref, low_ref, high_ref):
        first = ref.shape[0] - 3
        for plane in range(3):
            ref[first + plane] = local_ref[plane * rows : (plane + 1) * rows, :]


def weight_step(rows, refs, wide_ref, scratch_ref):
    planes = []
    for plane in range(3):
        blocks = [ref[ref.shape[0] - 3 + plane] for ref in refs]
        blocks[0] = blocks[0][rows - FAR :]
        blocks[-1] = blocks[-1][:FAR]
        planes.append(jnp.concatenate(blocks, axis=0))
    east = 1.0 + 0.125 * (planes[1] + jnp.concatenate([planes[1][1:], planes[1][:1]], axis=0))
    north = 1.0 + 0.125 * (planes[2] + pltpu.roll(planes[2], LANES - 1, 1))
    total = planes[0].shape[0]
    zero = jnp.zeros((LANES - 3 * total, LANES), jnp.float32)
    scratch_ref[...] = jnp.transpose(jnp.concatenate([planes[0], east, north, zero], axis=0))
    skip = (LANES - WINDOW) // 2
    for column in range(BLOCK):
        lines = scratch_ref[pl.ds(skip + column, SUB, stride=BLOCK), :]
        for row in range(total):
            for plane in range(3):
                index = plane * total + row
                wide_ref[row, plane * BLOCK + column] = jnp.broadcast_to(
                    lines[:, index : index + 1], (SUB, LANES)
                )


def own_columns(column):
    place = lax.broadcasted_iota(jnp.int32, (SUB, LANES), 0) * BLOCK + column
    first = (WINDOW - LANES // 2) // 2
    return (place >= first) & (place < first + LANES // 2)


def passes(edge, own, sources, wide_ref, coef_ref, step_ref, remain_ref, solved_ref, emit):
    total = step_ref.shape[0]
    columns = range(BLOCK)

    for turn in range(CHEB + 1):
        first, last = edge + turn + 1, total - edge - turn - 1

        def row_step(row, carry, *, turn, place):
            here, flux = carry[:BLOCK], carry[BLOCK:]
            after = [step_ref[row + 1, column] for column in columns]
            ahead = [wide_ref[row, BLOCK + column] * (here[column] - after[column]) for column in columns]
            beside = list(here[1:]) + [pltpu.roll(here[0], SUB - 1, 0)]
            side = [wide_ref[row, 2 * BLOCK + column] * (here[column] - beside[column]) for column in columns]
            behind = [pltpu.roll(side[-1], 1, 0)] + side[:-1]
            inside = place == 1
            results = []
            for column in columns:
                applied = (
                    (wide_ref[row, column] + coef_ref[0]) * here[column]
                    + (ahead[column] - flux[column])
                    + (side[column] - behind[column])
                )
                left = remain_ref[row, column] - applied
                if turn < CHEB:
                    remain_ref[row, column] = left
                    step_ref[row, column] = (
                        coef_ref[2 + 2 * turn] * here[column] + coef_ref[3 + 2 * turn] * left
                    )
                solved = here[column]
                if inside and turn > 0:
                    solved = solved_ref[row - own[0], column] + solved
                if inside and turn < CHEB:
                    solved_ref[row - own[0], column] = solved
                if turn == CHEB:
                    source = sources[place](row, column)
                    results.append((source, solved, source - left))
            if turn == CHEB:
                emit(row, inside, *zip(*results))
            return (*after, *ahead)

        here = [step_ref[first, column] for column in columns]
        flux = [
            wide_ref[first - 1, BLOCK + column] * (step_ref[first - 1, column] - here[column])
            for column in columns
        ]
        carry = (*here, *flux)
        for place, (low, high) in enumerate(((first, own[0]), own, (own[1], last))):
            if low < high:
                step = functools.partial(row_step, turn=turn, place=place)
                carry = lax.fori_loop(low, high, step, carry)


def stencil_kernel(
    rows, top_far_ref, top_ref, field_ref, bottom_ref, bottom_far_ref, coef_ref,
    solved_ref, applied_ref, solved_two_ref, applied_two_ref, sums_ref,
    step_ref, remain_ref, part_ref, line_ref, wide_ref, scratch_ref,
):
    columns = range(BLOCK)
    refs = (top_far_ref, top_ref, field_ref, bottom_ref, bottom_far_ref)
    weight_step(rows, refs, wide_ref, scratch_ref)
    offset = 0
    for ref in refs:
        count = (ref.shape[0] - 3) // BLOCK

        @pl.loop(0, count)
        def _(row, ref=ref, offset=offset):
            for column in columns:
                value = ref[row * BLOCK + column]
                remain_ref[offset + row, column] = value
                step_ref[offset + row, column] = coef_ref[1] * value

        offset += count

    own = (FAR + rows, FAR + 2 * rows)
    line_ref[...] = jnp.zeros_like(line_ref)

    def add(index, one, two):
        total = None
        for column in columns:
            product = jnp.where(own_columns(column), one[column] * two[column], 0.0)
            total = product if total is None else total + product
        line_ref[index] = line_ref[index] + total

    def emit_first(row, inside, source, solved, applied):
        for column in columns:
            remain_ref[row, column] = applied[column]
            step_ref[row, column] = coef_ref[1] * applied[column]
        if inside:
            for column in columns:
                solved_ref[row - own[0], column] = solved[column]
                applied_ref[row - own[0], column] = applied[column]
            add(0, source, solved)
            add(1, solved, applied)

    def emit_second(row, inside, source, solved, applied):
        for column in columns:
            solved_two_ref[row - own[0], column] = solved[column]
            applied_two_ref[row - own[0], column] = applied[column]
        add(2, source, solved)
        add(3, solved, applied)

    work = (wide_ref, coef_ref, step_ref, remain_ref, part_ref)
    sources = (
        lambda row, column: top_ref[(row - FAR) * BLOCK + column],
        lambda row, column: field_ref[(row - own[0]) * BLOCK + column],
        lambda row, column: bottom_ref[(row - own[1]) * BLOCK + column],
    )
    passes(0, own, sources, *work, emit_first)
    sources = (None, lambda row, column: applied_ref[row - own[0], column], None)
    passes(HALO, own, sources, *work, emit_second)

    lane = lane_index((1, LANES))
    line = jnp.zeros((1, LANES), jnp.float32)
    for index in range(4):
        line = jnp.where(lane == index, jnp.sum(line_ref[index]), line)
    sums_ref[...] = jnp.broadcast_to(line[None], sums_ref.shape)


def inverse_kernel(
    rows, times, length, cas_ref, sums_ref, one_ref, two_ref, three_ref, four_ref, out_ref, line_ref
):
    half = LANES // 2
    span = half + 2 * SIDE
    skip = (span - WINDOW) // 2
    line = jnp.sum(sums_ref[...].reshape(sums_ref.shape[0], LANES), axis=0, keepdims=True)
    gamma, curved, cross, last = (
        jnp.broadcast_to(line[:, index : index + 1], (SUB, LANES)) for index in range(4)
    )
    step = gamma / curved
    gamma_next = step * step * cross - gamma
    turn = gamma_next / gamma
    grown = 1.0 + turn
    next_curved = grown * grown * curved - 2.0 * step * grown * cross + step * step * last
    next_step = gamma_next / next_curved
    first = step + next_step * grown
    second = -next_step * step
    for row in range(rows):
        for index, (left_ref, right_ref) in enumerate(((one_ref, two_ref), (three_ref, four_ref))):
            for column in range(BLOCK):
                start = (2 * row + index) * span + skip + column
                value = first * left_ref[row, column] + second * right_ref[row, column]
                line_ref[pl.ds(start, SUB, stride=BLOCK), :] = value
    for row in range(rows):
        start = 2 * row * span + SIDE
        points = jnp.concatenate(
            [line_ref[start : start + half, :], line_ref[start + span : start + span + half, :]],
            axis=0,
        )
        back = exact_dot(cas_ref[...], points, 1, 1).reshape(length // times, times, LANES)
        out_ref[:, row * times : (row + 1) * times, :] = back


def final_kernel(rows, times, tiles, source_ref, field_ref, solution_ref, residual_ref):
    half = LANES // 2
    low = lane_index((rows, LANES)) < half
    for time in range(times):
        place = slice(time * rows, (time + 1) * rows)
        taken = pl.ds(time, rows, stride=times)
        for pair in range(tiles // 2):
            columns = slice(pair * LANES, (pair + 1) * LANES)
            left = source_ref[2 * pair, taken, :]
            right = source_ref[2 * pair + 1, taken, :]
            solution_ref[place, columns] = jnp.where(low, left, pltpu.roll(right, half, 1))
            change = jnp.where(low, pltpu.roll(left, half, 1), right)
            residual_ref[place, columns] = field_ref[place, columns] - change


def call(kernel, out_shape, scratch=()):
    shapes = [jax.ShapeDtypeStruct(shape, jnp.float32) for shape in out_shape]
    return pl.pallas_call(
        kernel,
        out_shape=shapes[0] if len(shapes) == 1 else shapes,
        scratch_shapes=[pltpu.VMEM(shape, jnp.float32) for shape in scratch],
        compiler_params=PARAMS,
    )


def shift(value, distance, spaces):
    return lax.ppermute(value, "space", [(i, (i + distance) % spaces) for i in range(spaces)])


def shards(right_side, kappa, velocity):
    tiles = lax.axis_size("tm")
    spaces = lax.axis_size("space")
    times, rows, width = right_side.shape
    length = times * tiles
    tile = width // tiles
    around = (LANES - tile) // 2
    cas_table = jnp.asarray(hartley_table(length))
    coef_table = jnp.asarray(chebyshev_table(length))

    field = right_side.reshape(times * rows, width)
    windows = call(
        functools.partial(window_kernel, rows, times, tiles),
        [(tiles, 6 * times, LANES)],
        [(width // LANES, times * rows, LANES)],
    )(field)
    gathered = lax.all_to_all(windows, "tm", 0, 0)

    squares = velocity.astype(jnp.float32) ** 2
    planes = jnp.concatenate([kappa, squares[0], squares[1]], axis=0)
    planes = jnp.concatenate([planes[:, -around:], planes, planes[:, :around]], axis=1)
    local = lax.dynamic_slice_in_dim(planes, lax.axis_index("tm") * tile, LANES, 1)
    total = 3 * rows + 2 * FAR
    tile_shape = (rows, BLOCK, SUB, LANES)
    row_shape = (rows * BLOCK + 3, SUB, LANES)
    far_shape = (FAR * BLOCK + 3, SUB, LANES)
    span = LANES // 2 + 2 * SIDE
    freq, low, high = call(
        functools.partial(forward_kernel, rows, times, length),
        [row_shape, far_shape, far_shape],
        [(rows * span, LANES)],
    )(cas_table, gathered, local)
    top, bottom = shift(freq, 1, spaces), shift(freq, -1, spaces)
    top_far, bottom_far = shift(high, 2, spaces), shift(low, -2, spaces)

    groups = [
        [i * spaces + first + j for i in range(tiles) for j in range(NEAR)]
        for first in range(0, spaces, NEAR)
    ]
    work = (total, BLOCK, SUB, LANES)
    solved, applied, solved_two, applied_two, sums = call(
        functools.partial(stencil_kernel, rows),
        [tile_shape] * 4 + [(tiles * NEAR, 1, LANES)],
        [
            work,
            work,
            tile_shape,
            (4, SUB, LANES),
            (total, 3 * BLOCK, SUB, LANES),
            (LANES, LANES),
        ],
    )(top_far, top, freq, bottom, bottom_far, coef_table)
    sums = lax.all_to_all(sums, ("tm", "space"), 0, 0, axis_index_groups=groups)
    planes = spaces // NEAR
    groups = [[first + NEAR * i for i in range(planes)] for first in range(NEAR)]
    sums = jnp.broadcast_to(jnp.sum(sums, axis=0)[None], (planes, 1, LANES))
    sums = lax.all_to_all(sums, "space", 0, 0, axis_index_groups=groups)
    packed = call(
        functools.partial(inverse_kernel, rows, times, length),
        [(tiles, rows * times, LANES)],
        [(rows * 2 * span, LANES)],
    )(cas_table, sums, solved, solved_two, applied, applied_two)
    returned = lax.all_to_all(packed, "tm", 0, 0)

    solution, residual = call(
        functools.partial(final_kernel, rows, times, tiles),
        [(times * rows, width), (times * rows, width)],
    )(returned, field)
    shape = right_side.shape
    return solution.reshape(shape), residual.reshape(shape)


def solution(mesh):
    placed = (P("tm", "space", None), P("space", None), P(None, "space", None))
    return jax.shard_map(
        shards,
        mesh=mesh,
        in_specs=placed,
        out_specs=(P("tm", "space", None), P("tm", "space", None)),
        check_vma=False,
    )
```

```python
import functools
import math

import jax
import jax.numpy as jnp
import numpy as np
from jax import lax
from jax.experimental import pallas as pl
from jax.experimental.pallas import tpu as pltpu
from jax.sharding import PartitionSpec as P

CHEB = 4
COUPLING = 2.0
KAPPA_LOW = 0.05
KAPPA_HIGH = 1.0
REACH = 16.0

LANES = 128
SUB = 8
HALO = CHEB + 1
FAR = 2
SIDE = 16
BLOCK = 11
WINDOW = SUB * BLOCK
NEAR = 4
PARAMS = pltpu.CompilerParams(vmem_limit_bytes=24 * 1024 * 1024)


def hartley_table(length):
    index = np.arange(length)
    angle = (index[:, None] * index[None, :] % length) * (2.0 * math.pi / length)
    return ((np.cos(angle) + np.sin(angle)) / math.sqrt(length)).astype(np.float32)


def chebyshev_table(length):
    shift = COUPLING * (2.0 - 2.0 * np.cos(2.0 * math.pi * np.arange(length) / length))
    half = 0.5 * (KAPPA_HIGH + REACH - KAPPA_LOW)
    mid = 0.5 * (KAPPA_LOW + KAPPA_HIGH + REACH) + shift
    ratio = mid / half
    damp = 1.0 / ratio
    lines = [shift, 1.0 / mid]
    for _ in range(CHEB):
        damp_next = 1.0 / (2.0 * ratio - damp)
        lines += [damp_next * damp, 2.0 * damp_next / half]
        damp = damp_next
    return np.repeat(np.stack(lines).astype(np.float32)[:, None], SUB, 1)


def lane_index(shape):
    return lax.broadcasted_iota(jnp.int32, shape, len(shape) - 1)


def exact_dot(left, right, left_dim, right_dim):
    return lax.dot_general(
        left,
        right,
        (((left_dim,), (right_dim,)), ((), ())),
        precision=lax.Precision.HIGHEST,
        preferred_element_type=jnp.float32,
    )


def window_kernel(rows, times, tiles, source_ref, out_ref, scratch_ref):
    half = LANES // 2
    parts = source_ref.shape[1] // LANES
    for part in range(parts):
        scratch_ref[part] = source_ref[:, part * LANES : (part + 1) * LANES]
    lane = lane_index((times, LANES))
    fields = [
        [scratch_ref[part, pl.ds(row, times, stride=rows), :] for part in range(parts)]
        for row in range(rows)
    ]
    for pair in range(rows // 2):
        for part in range(parts):
            one, two = fields[2 * pair][part], fields[2 * pair + 1][part]
            place = slice(pair * times, (pair + 1) * times)
            out_ref[2 * part, place, :] = jnp.where(lane < half, one, pltpu.roll(two, half, 1))
            out_ref[2 * part + 1, place, :] = jnp.where(lane < half, pltpu.roll(one, half, 1), two)
    spread = 2 * SIDE
    group = LANES // spread
    for quad in range(rows // group):
        even = [None] * parts
        odd = [None] * parts
        for index in range(group):
            row = quad * group + index
            wide = jnp.concatenate(fields[row], axis=1)
            near = pltpu.roll(wide, spread * index + SIDE, 1)
            away = pltpu.roll(wide, (spread * index - half + SIDE) % wide.shape[1], 1)
            left = (lane >= spread * index) & (lane < spread * index + SIDE)
            right = (lane >= spread * index + SIDE) & (lane < spread * (index + 1))
            for part in range(parts):
                here = slice(part * LANES, (part + 1) * LANES)
                then = (part + 1) % parts
                then = slice(then * LANES, (then + 1) * LANES)
                if index == 0:
                    even[part] = jnp.where(left, near[:, here], away[:, here])
                    odd[part] = jnp.where(left, away[:, here], near[:, then])
                else:
                    even[part] = jnp.where(
                        left, near[:, here], jnp.where(right, away[:, here], even[part])
                    )
                    odd[part] = jnp.where(
                        left, away[:, here], jnp.where(right, near[:, then], odd[part])
                    )
        start = (rows // 2 + quad) * times
        for part in range(parts):
            out_ref[2 * part, start : start + times, :] = even[part]
            out_ref[2 * part + 1, start : start + times, :] = odd[part]


def forward_kernel(
    rows, times, length, cas_ref, field_ref, local_ref, out_ref, low_ref, high_ref, line_ref
):
    half = LANES // 2
    span = half + 2 * SIDE
    pieces = field_ref.shape[1] // times
    group = LANES // (2 * SIDE)
    for piece in range(pieces):
        block = field_ref[:, piece * times : (piece + 1) * times, :].reshape(length, LANES)
        freq = exact_dot(block, cas_ref[...], 0, 0)
        if piece < rows // 2:
            for part in range(2):
                start = (2 * piece + part) * span + SIDE
                line_ref[start : start + half, :] = freq[part * half : (part + 1) * half]
        else:
            for index in range(group):
                start = ((piece - rows // 2) * group + index) * span
                place = 2 * SIDE * index
                line_ref[start : start + SIDE, :] = freq[place : place + SIDE]
                line_ref[start + SIDE + half : start + span, :] = freq[
                    place + SIDE : place + 2 * SIDE
                ]
    skip = (span - WINDOW) // 2
    for row in range(rows):
        for column in range(BLOCK):
            value = line_ref[pl.ds(row * span + skip + column, SUB, stride=BLOCK), :]
            out_ref[row * BLOCK + column] = value
            if row < FAR:
                low_ref[row * BLOCK + column] = value
            if row >= rows - FAR:
                high_ref[(row - (rows - FAR)) * BLOCK + column] = value
    for ref in (out_ref, low_ref, high_ref):
        first = ref.shape[0] - 3
        for plane in range(3):
            ref[first + plane] = local_ref[plane * rows : (plane + 1) * rows, :]


def weight_lines(rows, refs, scratch_ref):
    planes = []
    for plane in range(3):
        blocks = [ref[ref.shape[0] - 3 + plane] for ref in refs]
        blocks[0] = blocks[0][rows - FAR :]
        blocks[-1] = blocks[-1][:FAR]
        planes.append(jnp.concatenate(blocks, axis=0))
    east = 1.0 + 0.125 * (planes[1] + jnp.concatenate([planes[1][1:], planes[1][:1]], axis=0))
    north = 1.0 + 0.125 * (planes[2] + pltpu.roll(planes[2], LANES - 1, 1))
    total = planes[0].shape[0]
    zero = jnp.zeros((LANES - 3 * total, LANES), jnp.float32)
    scratch_ref[...] = jnp.transpose(jnp.concatenate([planes[0], east, north, zero], axis=0))
    skip = (LANES - WINDOW) // 2
    return [scratch_ref[pl.ds(skip + column, SUB, stride=BLOCK), :] for column in range(BLOCK)]


def own_columns(column):
    place = lax.broadcasted_iota(jnp.int32, (SUB, LANES), 0) * BLOCK + column
    first = (WINDOW - LANES // 2) // 2
    return (place >= first) & (place < first + LANES // 2)


def passes(edge, own, total, source, weight, coef, step_ref, remain_ref, solved_ref, emit):
    columns = range(BLOCK)

    for turn in range(CHEB + 1):
        first, last = edge + turn + 1, total - edge - turn - 1

        def load(row, turn=turn):
            if turn == 0:
                return [coef[1] * source(row, column) for column in columns]
            return [step_ref[row, column] for column in columns]

        here = load(first - 1)
        flux = None
        for row in range(first - 1, last):
            after = load(row + 1)
            ahead = [weight(1, row, column) * (here[column] - after[column]) for column in columns]
            if row >= first:
                beside = here[1:] + [pltpu.roll(here[0], SUB - 1, 0)]
                side = [weight(2, row, column) * (here[column] - beside[column]) for column in columns]
                behind = [pltpu.roll(side[-1], 1, 0)] + side[:-1]
                inside = row in range(*own)
                results = []
                for column in columns:
                    applied = (
                        weight(0, row, column) * here[column]
                        + (ahead[column] - flux[column])
                        + (side[column] - behind[column])
                    )
                    before = source(row, column) if turn == 0 else remain_ref[row, column]
                    left = before - applied
                    if turn < CHEB:
                        remain_ref[row, column] = left
                        step_ref[row, column] = (
                            coef[2 + 2 * turn] * here[column] + coef[3 + 2 * turn] * left
                        )
                    solved = None
                    if inside:
                        place = row - own[0]
                        solved = here[column]
                        if turn > 0:
                            solved = solved_ref[place, column] + solved
                        if turn < CHEB:
                            solved_ref[place, column] = solved
                    if turn == CHEB:
                        begun = source(row, column)
                        results.append((begun, solved, begun - left))
                if turn == CHEB:
                    emit(row, *zip(*results))
            here, flux = after, ahead


def stencil_kernel(
    rows, top_far_ref, top_ref, field_ref, bottom_ref, bottom_far_ref, coef_ref,
    solved_ref, applied_ref, solved_two_ref, applied_two_ref, sums_ref,
    step_ref, remain_ref, part_ref, middle_ref, wide_ref, scratch_ref,
):
    columns = range(BLOCK)
    refs = (top_far_ref, top_ref, field_ref, bottom_ref, bottom_far_ref)
    lines = weight_lines(rows, refs, scratch_ref)
    coef = [coef_ref[index] for index in range(2 + 2 * CHEB)]
    places = [
        (ref, row) for ref in refs for row in range((ref.shape[0] - 3) // BLOCK)
    ]
    total = len(places)
    own = (FAR + rows, FAR + 2 * rows)
    made = set()

    def weight(plane, row, column):
        place = plane * BLOCK + column
        if (row, place) in made:
            return wide_ref[row, place]
        index = plane * total + row
        value = jnp.broadcast_to(lines[column][:, index : index + 1], (SUB, LANES))
        if plane == 0:
            value = value + coef[0]
        wide_ref[row, place] = value
        made.add((row, place))
        return value

    def first_source(row, column):
        ref, place = places[row]
        return ref[place * BLOCK + column]

    def second_source(row, column):
        return middle_ref[row, column]

    sums = [jnp.zeros((SUB, LANES), jnp.float32) for _ in range(4)]

    def add(index, one, two):
        for column in columns:
            product = one[column] * two[column]
            sums[index] = sums[index] + jnp.where(own_columns(column), product, 0.0)

    def emit_first(row, source, solved, applied):
        for column in columns:
            middle_ref[row, column] = applied[column]
        if row in range(*own):
            for column in columns:
                solved_ref[row - own[0], column] = solved[column]
                applied_ref[row - own[0], column] = applied[column]
            add(0, source, solved)
            add(1, solved, applied)

    def emit_second(row, source, solved, applied):
        for column in columns:
            solved_two_ref[row - own[0], column] = solved[column]
            applied_two_ref[row - own[0], column] = applied[column]
        add(2, source, solved)
        add(3, solved, applied)

    work = (weight, coef, step_ref, remain_ref, part_ref)
    passes(0, own, total, first_source, *work, emit_first)
    passes(HALO, own, total, second_source, *work, emit_second)

    lane = lane_index((1, LANES))
    line = jnp.zeros((1, LANES), jnp.float32)
    for index in range(4):
        line = jnp.where(lane == index, jnp.sum(sums[index]), line)
    sums_ref[...] = jnp.broadcast_to(line[None], sums_ref.shape)


def inverse_kernel(
    rows, times, length, cas_ref, sums_ref, one_ref, two_ref, three_ref, four_ref, out_ref, line_ref
):
    half = LANES // 2
    span = half + 2 * SIDE
    skip = (span - WINDOW) // 2
    line = jnp.sum(sums_ref[...].reshape(sums_ref.shape[0], LANES), axis=0, keepdims=True)
    gamma, curved, cross, last = (
        jnp.broadcast_to(line[:, index : index + 1], (SUB, LANES)) for index in range(4)
    )
    step = gamma / curved
    gamma_next = step * step * cross - gamma
    turn = gamma_next / gamma
    grown = 1.0 + turn
    next_curved = grown * grown * curved - 2.0 * step * grown * cross + step * step * last
    next_step = gamma_next / next_curved
    first = step + next_step * grown
    second = -next_step * step
    for row in range(rows):
        for index, (left_ref, right_ref) in enumerate(((one_ref, two_ref), (three_ref, four_ref))):
            for column in range(BLOCK):
                start = (2 * row + index) * span + skip + column
                value = first * left_ref[row, column] + second * right_ref[row, column]
                line_ref[pl.ds(start, SUB, stride=BLOCK), :] = value
    for row in range(rows):
        start = 2 * row * span + SIDE
        points = jnp.concatenate(
            [line_ref[start : start + half, :], line_ref[start + span : start + span + half, :]],
            axis=0,
        )
        back = exact_dot(cas_ref[...], points, 1, 1).reshape(length // times, times, LANES)
        out_ref[:, row * times : (row + 1) * times, :] = back


def final_kernel(rows, times, tiles, source_ref, field_ref, solution_ref, residual_ref):
    half = LANES // 2
    low = lane_index((rows, LANES)) < half
    for time in range(times):
        place = slice(time * rows, (time + 1) * rows)
        taken = pl.ds(time, rows, stride=times)
        for pair in range(tiles // 2):
            columns = slice(pair * LANES, (pair + 1) * LANES)
            left = source_ref[2 * pair, taken, :]
            right = source_ref[2 * pair + 1, taken, :]
            solution_ref[place, columns] = jnp.where(low, left, pltpu.roll(right, half, 1))
            change = jnp.where(low, pltpu.roll(left, half, 1), right)
            residual_ref[place, columns] = field_ref[place, columns] - change


def call(kernel, out_shape, scratch=()):
    shapes = [jax.ShapeDtypeStruct(shape, jnp.float32) for shape in out_shape]
    return pl.pallas_call(
        kernel,
        out_shape=shapes[0] if len(shapes) == 1 else shapes,
        scratch_shapes=[pltpu.VMEM(shape, jnp.float32) for shape in scratch],
        compiler_params=PARAMS,
    )


def shift(value, distance, spaces):
    return lax.ppermute(value, "space", [(i, (i + distance) % spaces) for i in range(spaces)])


def shards(right_side, kappa, velocity):
    tiles = lax.axis_size("tm")
    spaces = lax.axis_size("space")
    times, rows, width = right_side.shape
    length = times * tiles
    tile = width // tiles
    around = (LANES - tile) // 2
    cas_table = jnp.asarray(hartley_table(length))
    coef_table = jnp.asarray(chebyshev_table(length))

    field = right_side.reshape(times * rows, width)
    windows = call(
        functools.partial(window_kernel, rows, times, tiles),
        [(tiles, 6 * times, LANES)],
        [(width // LANES, times * rows, LANES)],
    )(field)
    gathered = lax.all_to_all(windows, "tm", 0, 0)

    squares = velocity.astype(jnp.float32) ** 2
    planes = jnp.concatenate([kappa, squares[0], squares[1]], axis=0)
    planes = jnp.concatenate([planes[:, -around:], planes, planes[:, :around]], axis=1)
    local = lax.dynamic_slice_in_dim(planes, lax.axis_index("tm") * tile, LANES, 1)
    total = 3 * rows + 2 * FAR
    tile_shape = (rows, BLOCK, SUB, LANES)
    row_shape = (rows * BLOCK + 3, SUB, LANES)
    far_shape = (FAR * BLOCK + 3, SUB, LANES)
    span = LANES // 2 + 2 * SIDE
    freq, low, high = call(
        functools.partial(forward_kernel, rows, times, length),
        [row_shape, far_shape, far_shape],
        [(rows * span, LANES)],
    )(cas_table, gathered, local)
    top, bottom = shift(freq, 1, spaces), shift(freq, -1, spaces)
    top_far, bottom_far = shift(high, 2, spaces), shift(low, -2, spaces)

    groups = [
        [i * spaces + first + j for i in range(tiles) for j in range(NEAR)]
        for first in range(0, spaces, NEAR)
    ]
    work = (total, BLOCK, SUB, LANES)
    solved, applied, solved_two, applied_two, sums = call(
        functools.partial(stencil_kernel, rows),
        [tile_shape] * 4 + [(tiles * NEAR, 1, LANES)],
        [
            work,
            work,
            tile_shape,
            work,
            (total, 3 * BLOCK, SUB, LANES),
            (LANES, LANES),
        ],
    )(top_far, top, freq, bottom, bottom_far, coef_table)
    sums = lax.all_to_all(sums, ("tm", "space"), 0, 0, axis_index_groups=groups)
    planes = spaces // NEAR
    groups = [[first + NEAR * i for i in range(planes)] for first in range(NEAR)]
    sums = jnp.broadcast_to(jnp.sum(sums, axis=0)[None], (planes, 1, LANES))
    sums = lax.all_to_all(sums, "space", 0, 0, axis_index_groups=groups)
    packed = call(
        functools.partial(inverse_kernel, rows, times, length),
        [(tiles, rows * times, LANES)],
        [(rows * 2 * span, LANES)],
    )(cas_table, sums, solved, solved_two, applied, applied_two)
    returned = lax.all_to_all(packed, "tm", 0, 0)

    solution, residual = call(
        functools.partial(final_kernel, rows, times, tiles),
        [(times * rows, width), (times * rows, width)],
    )(returned, field)
    shape = right_side.shape
    return solution.reshape(shape), residual.reshape(shape)


def solution(mesh):
    placed = (P("tm", "space", None), P("space", None), P(None, "space", None))
    return jax.shard_map(
        shards,
        mesh=mesh,
        in_specs=placed,
        out_specs=(P("tm", "space", None), P("tm", "space", None)),
        check_vma=False,
    )
```

```python
import functools
import math

import jax
import jax.numpy as jnp
import numpy as np
from jax import lax
from jax.experimental import pallas as pl
from jax.experimental.pallas import tpu as pltpu
from jax.sharding import PartitionSpec as P

CHEB = 4
COUPLING = 2.0
KAPPA_LOW = 0.05
KAPPA_HIGH = 1.0
REACH = 16.0

LANES = 128
SUB = 8
HALO = CHEB + 1
FAR = 2
SIDE = 16
BLOCK = 11
WINDOW = SUB * BLOCK
NEAR = 4
PARAMS = pltpu.CompilerParams(vmem_limit_bytes=24 * 1024 * 1024)


def hartley_table(length):
    index = np.arange(length)
    angle = (index[:, None] * index[None, :] % length) * (2.0 * math.pi / length)
    return ((np.cos(angle) + np.sin(angle)) / math.sqrt(length)).astype(np.float32)


def chebyshev_table(length):
    shift = COUPLING * (2.0 - 2.0 * np.cos(2.0 * math.pi * np.arange(length) / length))
    half = 0.5 * (KAPPA_HIGH + REACH - KAPPA_LOW)
    mid = 0.5 * (KAPPA_LOW + KAPPA_HIGH + REACH) + shift
    ratio = mid / half
    damp = 1.0 / ratio
    lines = [shift, 1.0 / mid]
    for _ in range(CHEB):
        damp_next = 1.0 / (2.0 * ratio - damp)
        lines += [damp_next * damp, 2.0 * damp_next / half]
        damp = damp_next
    return np.repeat(np.stack(lines).astype(np.float32)[:, None], SUB, 1)


def lane_index(shape):
    return lax.broadcasted_iota(jnp.int32, shape, len(shape) - 1)


def exact_dot(left, right, left_dim, right_dim):
    return lax.dot_general(
        left,
        right,
        (((left_dim,), (right_dim,)), ((), ())),
        precision=lax.Precision.HIGHEST,
        preferred_element_type=jnp.float32,
    )


def window_kernel(rows, times, tiles, source_ref, out_ref, scratch_ref):
    half = LANES // 2
    parts = source_ref.shape[1] // LANES
    for part in range(parts):
        scratch_ref[part] = source_ref[:, part * LANES : (part + 1) * LANES]
    lane = lane_index((times, LANES))
    fields = [
        [scratch_ref[part, pl.ds(row, times, stride=rows), :] for part in range(parts)]
        for row in range(rows)
    ]
    for pair in range(rows // 2):
        for part in range(parts):
            one, two = fields[2 * pair][part], fields[2 * pair + 1][part]
            place = slice(pair * times, (pair + 1) * times)
            out_ref[2 * part, place, :] = jnp.where(lane < half, one, pltpu.roll(two, half, 1))
            out_ref[2 * part + 1, place, :] = jnp.where(lane < half, pltpu.roll(one, half, 1), two)
    spread = 2 * SIDE
    group = LANES // spread
    for quad in range(rows // group):
        even = [None] * parts
        odd = [None] * parts
        for index in range(group):
            row = quad * group + index
            wide = jnp.concatenate(fields[row], axis=1)
            near = pltpu.roll(wide, spread * index + SIDE, 1)
            away = pltpu.roll(wide, (spread * index - half + SIDE) % wide.shape[1], 1)
            left = (lane >= spread * index) & (lane < spread * index + SIDE)
            right = (lane >= spread * index + SIDE) & (lane < spread * (index + 1))
            for part in range(parts):
                here = slice(part * LANES, (part + 1) * LANES)
                then = (part + 1) % parts
                then = slice(then * LANES, (then + 1) * LANES)
                if index == 0:
                    even[part] = jnp.where(left, near[:, here], away[:, here])
                    odd[part] = jnp.where(left, away[:, here], near[:, then])
                else:
                    even[part] = jnp.where(
                        left, near[:, here], jnp.where(right, away[:, here], even[part])
                    )
                    odd[part] = jnp.where(
                        left, away[:, here], jnp.where(right, near[:, then], odd[part])
                    )
        start = (rows // 2 + quad) * times
        for part in range(parts):
            out_ref[2 * part, start : start + times, :] = even[part]
            out_ref[2 * part + 1, start : start + times, :] = odd[part]


def forward_kernel(
    rows, times, length, cas_ref, field_ref, local_ref, place_ref, out_ref, one_ref, two_ref, line_ref
):
    second = place_ref[1] == 1
    half = LANES // 2
    span = half + 2 * SIDE
    pieces = field_ref.shape[1] // times
    group = LANES // (2 * SIDE)
    for piece in range(pieces):
        block = field_ref[:, piece * times : (piece + 1) * times, :].reshape(length, LANES)
        freq = exact_dot(block, cas_ref[...], 0, 0)
        if piece < rows // 2:
            for part in range(2):
                start = (2 * piece + part) * span + SIDE
                line_ref[start : start + half, :] = freq[part * half : (part + 1) * half]
        else:
            for index in range(group):
                start = ((piece - rows // 2) * group + index) * span
                place = 2 * SIDE * index
                line_ref[start : start + SIDE, :] = freq[place : place + SIDE]
                line_ref[start + SIDE + half : start + span, :] = freq[
                    place + SIDE : place + 2 * SIDE
                ]
    skip = (span - WINDOW) // 2
    for row in range(rows):
        for column in range(BLOCK):
            value = line_ref[pl.ds(row * span + skip + column, SUB, stride=BLOCK), :]
            out_ref[row * BLOCK + column] = value
    for index in range(FAR * BLOCK):
        low = out_ref[index]
        high = out_ref[(rows - FAR) * BLOCK + index]
        one_ref[index] = jnp.where(second, low, high)
        two_ref[index] = jnp.where(second, high, low)
    for ref in (out_ref, one_ref, two_ref):
        first = ref.shape[0] - 3
        for plane in range(3):
            ref[first + plane] = local_ref[plane * rows : (plane + 1) * rows, :]


def weight_lines(rows, parts, scratch_ref):
    planes = []
    for plane in range(3):
        blocks = [part[plane] for part in parts]
        blocks[0] = blocks[0][rows - FAR :]
        blocks[-1] = blocks[-1][:FAR]
        planes.append(jnp.concatenate(blocks, axis=0))
    east = 1.0 + 0.125 * (planes[1] + jnp.concatenate([planes[1][1:], planes[1][:1]], axis=0))
    north = 1.0 + 0.125 * (planes[2] + pltpu.roll(planes[2], LANES - 1, 1))
    total = planes[0].shape[0]
    zero = jnp.zeros((LANES - 3 * total, LANES), jnp.float32)
    scratch_ref[...] = jnp.transpose(jnp.concatenate([planes[0], east, north, zero], axis=0))
    skip = (LANES - WINDOW) // 2
    return [scratch_ref[pl.ds(skip + column, SUB, stride=BLOCK), :] for column in range(BLOCK)]


def own_columns(column):
    place = lax.broadcasted_iota(jnp.int32, (SUB, LANES), 0) * BLOCK + column
    first = (WINDOW - LANES // 2) // 2
    return (place >= first) & (place < first + LANES // 2)


def passes(edge, own, total, source, weight, coef, step_ref, remain_ref, solved_ref, emit):
    columns = range(BLOCK)

    for turn in range(CHEB + 1):
        first, last = edge + turn + 1, total - edge - turn - 1

        def load(row, turn=turn):
            if turn == 0:
                return [coef[1] * source(row, column) for column in columns]
            return [step_ref[row, column] for column in columns]

        here = load(first - 1)
        flux = None
        for row in range(first - 1, last):
            after = load(row + 1)
            ahead = [weight(1, row, column) * (here[column] - after[column]) for column in columns]
            if row >= first:
                beside = here[1:] + [pltpu.roll(here[0], SUB - 1, 0)]
                side = [weight(2, row, column) * (here[column] - beside[column]) for column in columns]
                behind = [pltpu.roll(side[-1], 1, 0)] + side[:-1]
                inside = row in range(*own)
                results = []
                for column in columns:
                    applied = (
                        weight(0, row, column) * here[column]
                        + (ahead[column] - flux[column])
                        + (side[column] - behind[column])
                    )
                    before = source(row, column) if turn == 0 else remain_ref[row, column]
                    left = before - applied
                    if turn < CHEB:
                        remain_ref[row, column] = left
                        step_ref[row, column] = (
                            coef[2 + 2 * turn] * here[column] + coef[3 + 2 * turn] * left
                        )
                    solved = None
                    if inside:
                        place = row - own[0]
                        solved = here[column]
                        if turn > 0:
                            solved = solved_ref[place, column] + solved
                        if turn < CHEB:
                            solved_ref[place, column] = solved
                    if turn == CHEB:
                        begun = source(row, column)
                        results.append((begun, solved, begun - left))
                if turn == CHEB:
                    emit(row, *zip(*results))
            here, flux = after, ahead


def stencil_kernel(
    rows, one_ref, two_ref, one_far_ref, two_far_ref, field_ref, coef_ref, place_ref,
    solved_ref, applied_ref, solved_two_ref, applied_two_ref, sums_ref,
    step_ref, remain_ref, part_ref, middle_ref, wide_ref, scratch_ref, near_ref, far_ref,
):
    columns = range(BLOCK)
    for ref, above, target_ref in (
        (one_ref, place_ref[0], near_ref),
        (two_ref, 1 - place_ref[0], near_ref),
        (one_far_ref, place_ref[1], far_ref),
        (two_far_ref, 1 - place_ref[1], far_ref),
    ):
        for index in range(ref.shape[0]):
            target_ref[1 - above, index] = ref[index]
    refs = (far_ref.at[0], near_ref.at[0], field_ref, near_ref.at[1], far_ref.at[1])
    parts = [[ref[ref.shape[0] - 3 + plane] for plane in range(3)] for ref in refs]
    lines = weight_lines(rows, parts, scratch_ref)
    coef = [coef_ref[index] for index in range(2 + 2 * CHEB)]
    places = [
        (ref, row) for ref in refs for row in range((ref.shape[0] - 3) // BLOCK)
    ]
    total = len(places)
    own = (FAR + rows, FAR + 2 * rows)
    made = set()

    def weight(plane, row, column):
        place = plane * BLOCK + column
        if (row, place) in made:
            return wide_ref[row, place]
        index = plane * total + row
        value = jnp.broadcast_to(lines[column][:, index : index + 1], (SUB, LANES))
        if plane == 0:
            value = value + coef[0]
        wide_ref[row, place] = value
        made.add((row, place))
        return value

    def first_source(row, column):
        ref, place = places[row]
        return ref[place * BLOCK + column]

    def second_source(row, column):
        return middle_ref[row, column]

    sums = [jnp.zeros((SUB, LANES), jnp.float32) for _ in range(4)]

    def add(index, one, two):
        for column in columns:
            product = one[column] * two[column]
            sums[index] = sums[index] + jnp.where(own_columns(column), product, 0.0)

    def emit_first(row, source, solved, applied):
        for column in columns:
            middle_ref[row, column] = applied[column]
        if row in range(*own):
            for column in columns:
                solved_ref[row - own[0], column] = solved[column]
                applied_ref[row - own[0], column] = applied[column]
            add(0, source, solved)
            add(1, solved, applied)

    def emit_second(row, source, solved, applied):
        for column in columns:
            solved_two_ref[row - own[0], column] = solved[column]
            applied_two_ref[row - own[0], column] = applied[column]
        add(2, source, solved)
        add(3, solved, applied)

    work = (weight, coef, step_ref, remain_ref, part_ref)
    passes(0, own, total, first_source, *work, emit_first)
    passes(HALO, own, total, second_source, *work, emit_second)

    lane = lane_index((1, LANES))
    line = jnp.zeros((1, LANES), jnp.float32)
    for index in range(4):
        line = jnp.where(lane == index, jnp.sum(sums[index]), line)
    sums_ref[...] = jnp.broadcast_to(line[None], sums_ref.shape)


def inverse_kernel(
    rows, times, length, cas_ref, sums_ref, one_ref, two_ref, three_ref, four_ref, out_ref, line_ref
):
    half = LANES // 2
    span = half + 2 * SIDE
    skip = (span - WINDOW) // 2
    line = jnp.sum(sums_ref[...].reshape(sums_ref.shape[0], LANES), axis=0, keepdims=True)
    gamma, curved, cross, last = (
        jnp.broadcast_to(line[:, index : index + 1], (SUB, LANES)) for index in range(4)
    )
    step = gamma / curved
    gamma_next = step * step * cross - gamma
    turn = gamma_next / gamma
    grown = 1.0 + turn
    next_curved = grown * grown * curved - 2.0 * step * grown * cross + step * step * last
    next_step = gamma_next / next_curved
    first = step + next_step * grown
    second = -next_step * step
    for row in range(rows):
        for index, (left_ref, right_ref) in enumerate(((one_ref, two_ref), (three_ref, four_ref))):
            for column in range(BLOCK):
                start = (2 * row + index) * span + skip + column
                value = first * left_ref[row, column] + second * right_ref[row, column]
                line_ref[pl.ds(start, SUB, stride=BLOCK), :] = value
    for row in range(rows):
        start = 2 * row * span + SIDE
        points = jnp.concatenate(
            [line_ref[start : start + half, :], line_ref[start + span : start + span + half, :]],
            axis=0,
        )
        back = exact_dot(cas_ref[...], points, 1, 1).reshape(length // times, times, LANES)
        out_ref[:, row * times : (row + 1) * times, :] = back


def final_kernel(rows, times, tiles, source_ref, field_ref, solution_ref, residual_ref):
    half = LANES // 2
    low = lane_index((rows, LANES)) < half
    for time in range(times):
        place = slice(time * rows, (time + 1) * rows)
        taken = pl.ds(time, rows, stride=times)
        for pair in range(tiles // 2):
            columns = slice(pair * LANES, (pair + 1) * LANES)
            left = source_ref[2 * pair, taken, :]
            right = source_ref[2 * pair + 1, taken, :]
            solution_ref[place, columns] = jnp.where(low, left, pltpu.roll(right, half, 1))
            change = jnp.where(low, pltpu.roll(left, half, 1), right)
            residual_ref[place, columns] = field_ref[place, columns] - change


def call(kernel, out_shape, scratch=(), inputs=0):
    shapes = [jax.ShapeDtypeStruct(shape, jnp.float32) for shape in out_shape]
    specs = {}
    if inputs:
        whole = pl.BlockSpec(memory_space=pltpu.VMEM)
        specs["in_specs"] = [whole] * (inputs - 1) + [pl.BlockSpec(memory_space=pltpu.SMEM)]
    return pl.pallas_call(
        kernel,
        out_shape=shapes[0] if len(shapes) == 1 else shapes,
        scratch_shapes=[pltpu.VMEM(shape, jnp.float32) for shape in scratch],
        compiler_params=PARAMS,
        **specs,
    )


def swap(value, distance, offset, spaces):
    pairs = [(i, (((i - offset) % spaces ^ distance) + offset) % spaces) for i in range(spaces)]
    return lax.ppermute(value, "space", pairs)


def shards(right_side, kappa, velocity):
    tiles = lax.axis_size("tm")
    spaces = lax.axis_size("space")
    times, rows, width = right_side.shape
    length = times * tiles
    tile = width // tiles
    around = (LANES - tile) // 2
    cas_table = jnp.asarray(hartley_table(length))
    coef_table = jnp.asarray(chebyshev_table(length))

    field = right_side.reshape(times * rows, width)
    windows = call(
        functools.partial(window_kernel, rows, times, tiles),
        [(tiles, 6 * times, LANES)],
        [(width // LANES, times * rows, LANES)],
    )(field)
    gathered = lax.all_to_all(windows, "tm", 0, 0)

    squares = velocity.astype(jnp.float32) ** 2
    planes = jnp.concatenate([kappa, squares[0], squares[1]], axis=0)
    planes = jnp.concatenate([planes[:, -around:], planes, planes[:, :around]], axis=1)
    local = lax.dynamic_slice_in_dim(planes, lax.axis_index("tm") * tile, LANES, 1)
    total = 3 * rows + 2 * FAR
    tile_shape = (rows, BLOCK, SUB, LANES)
    row_shape = (rows * BLOCK + 3, SUB, LANES)
    far_shape = (FAR * BLOCK + 3, SUB, LANES)
    span = LANES // 2 + 2 * SIDE
    index = lax.axis_index("space")
    place = jnp.stack([index % 2, index // 2 % 2]).astype(jnp.int32)
    freq, inner_far, outer_far = call(
        functools.partial(forward_kernel, rows, times, length),
        [row_shape, far_shape, far_shape],
        [(rows * span, LANES)],
        inputs=4,
    )(cas_table, gathered, local, place)
    outer = swap(freq, 1, 1, spaces)
    inner = swap(freq, 1, 0, spaces)
    outer_far = swap(outer_far, 2, 2, spaces)
    inner_far = swap(inner_far, 2, 0, spaces)

    groups = [
        [i * spaces + first + j for i in range(tiles) for j in range(NEAR)]
        for first in range(0, spaces, NEAR)
    ]
    work = (total, BLOCK, SUB, LANES)
    solved, applied, solved_two, applied_two, sums = call(
        functools.partial(stencil_kernel, rows),
        [tile_shape] * 4 + [(tiles * NEAR, 1, LANES)],
        [
            work,
            work,
            tile_shape,
            work,
            (total, 3 * BLOCK, SUB, LANES),
            (LANES, LANES),
            (2, *row_shape),
            (2, *far_shape),
        ],
        inputs=7,
    )(inner, outer, inner_far, outer_far, freq, coef_table, place)
    sums = lax.all_to_all(sums, ("tm", "space"), 0, 0, axis_index_groups=groups)
    planes = spaces // NEAR
    groups = [[first + NEAR * i for i in range(planes)] for first in range(NEAR)]
    sums = jnp.broadcast_to(jnp.sum(sums, axis=0)[None], (planes, 1, LANES))
    sums = lax.all_to_all(sums, "space", 0, 0, axis_index_groups=groups)
    packed = call(
        functools.partial(inverse_kernel, rows, times, length),
        [(tiles, rows * times, LANES)],
        [(rows * 2 * span, LANES)],
    )(cas_table, sums, solved, solved_two, applied, applied_two)
    returned = lax.all_to_all(packed, "tm", 0, 0)

    solution, residual = call(
        functools.partial(final_kernel, rows, times, tiles),
        [(times * rows, width), (times * rows, width)],
    )(returned, field)
    shape = right_side.shape
    return solution.reshape(shape), residual.reshape(shape)


def solution(mesh):
    placed = (P("tm", "space", None), P("space", None), P(None, "space", None))
    return jax.shard_map(
        shards,
        mesh=mesh,
        in_specs=placed,
        out_specs=(P("tm", "space", None), P("tm", "space", None)),
        check_vma=False,
    )
```

```python
import functools
import math

import jax
import jax.numpy as jnp
import numpy as np
from jax import lax
from jax.experimental import pallas as pl
from jax.experimental.pallas import tpu as pltpu
from jax.sharding import PartitionSpec as P

CHEB = 4
COUPLING = 2.0
KAPPA_LOW = 0.05
KAPPA_HIGH = 1.0
REACH = 16.0

LANES = 128
SUB = 8
HALO = CHEB + 1
FAR = 2
SIDE = 16
BLOCK = 11
WINDOW = SUB * BLOCK
NEAR = 4
PARAMS = pltpu.CompilerParams(vmem_limit_bytes=24 * 1024 * 1024)


def hartley_table(length):
    index = np.arange(length)
    angle = (index[:, None] * index[None, :] % length) * (2.0 * math.pi / length)
    return ((np.cos(angle) + np.sin(angle)) / math.sqrt(length)).astype(np.float32)


def chebyshev_table(length):
    shift = COUPLING * (2.0 - 2.0 * np.cos(2.0 * math.pi * np.arange(length) / length))
    half = 0.5 * (KAPPA_HIGH + REACH - KAPPA_LOW)
    mid = 0.5 * (KAPPA_LOW + KAPPA_HIGH + REACH) + shift
    ratio = mid / half
    damp = 1.0 / ratio
    lines = [shift, 1.0 / mid]
    for _ in range(CHEB):
        damp_next = 1.0 / (2.0 * ratio - damp)
        lines += [damp_next * damp, 2.0 * damp_next / half]
        damp = damp_next
    return np.repeat(np.stack(lines).astype(np.float32)[:, None], SUB, 1)


def lane_index(shape):
    return lax.broadcasted_iota(jnp.int32, shape, len(shape) - 1)


def exact_dot(left, right, left_dim, right_dim):
    return lax.dot_general(
        left,
        right,
        (((left_dim,), (right_dim,)), ((), ())),
        precision=lax.Precision.HIGHEST,
        preferred_element_type=jnp.float32,
    )


def window_kernel(rows, times, tiles, source_ref, out_ref, scratch_ref):
    half = LANES // 2
    parts = source_ref.shape[1] // LANES
    for part in range(parts):
        scratch_ref[part] = source_ref[:, part * LANES : (part + 1) * LANES]
    lane = lane_index((times, LANES))
    fields = [
        [scratch_ref[part, pl.ds(row, times, stride=rows), :] for part in range(parts)]
        for row in range(rows)
    ]
    for pair in range(rows // 2):
        for part in range(parts):
            one, two = fields[2 * pair][part], fields[2 * pair + 1][part]
            place = slice(pair * times, (pair + 1) * times)
            out_ref[2 * part, place, :] = jnp.where(lane < half, one, pltpu.roll(two, half, 1))
            out_ref[2 * part + 1, place, :] = jnp.where(lane < half, pltpu.roll(one, half, 1), two)
    spread = 2 * SIDE
    group = LANES // spread
    for quad in range(rows // group):
        even = [None] * parts
        odd = [None] * parts
        for index in range(group):
            row = quad * group + index
            wide = jnp.concatenate(fields[row], axis=1)
            near = pltpu.roll(wide, spread * index + SIDE, 1)
            away = pltpu.roll(wide, (spread * index - half + SIDE) % wide.shape[1], 1)
            left = (lane >= spread * index) & (lane < spread * index + SIDE)
            right = (lane >= spread * index + SIDE) & (lane < spread * (index + 1))
            for part in range(parts):
                here = slice(part * LANES, (part + 1) * LANES)
                then = (part + 1) % parts
                then = slice(then * LANES, (then + 1) * LANES)
                if index == 0:
                    even[part] = jnp.where(left, near[:, here], away[:, here])
                    odd[part] = jnp.where(left, away[:, here], near[:, then])
                else:
                    even[part] = jnp.where(
                        left, near[:, here], jnp.where(right, away[:, here], even[part])
                    )
                    odd[part] = jnp.where(
                        left, away[:, here], jnp.where(right, near[:, then], odd[part])
                    )
        start = (rows // 2 + quad) * times
        for part in range(parts):
            out_ref[2 * part, start : start + times, :] = even[part]
            out_ref[2 * part + 1, start : start + times, :] = odd[part]


def forward_kernel(
    rows, times, length, cas_ref, field_ref, local_ref, place_ref, out_ref, one_ref, two_ref, line_ref
):
    second = place_ref[1]
    half = LANES // 2
    span = half + 2 * SIDE
    pieces = field_ref.shape[1] // times
    group = LANES // (2 * SIDE)
    for piece in range(pieces):
        block = field_ref[:, piece * times : (piece + 1) * times, :].reshape(length, LANES)
        freq = exact_dot(block, cas_ref[...], 0, 0)
        if piece < rows // 2:
            for part in range(2):
                start = (2 * piece + part) * span + SIDE
                line_ref[start : start + half, :] = freq[part * half : (part + 1) * half]
        else:
            for index in range(group):
                start = ((piece - rows // 2) * group + index) * span
                place = 2 * SIDE * index
                line_ref[start : start + SIDE, :] = freq[place : place + SIDE]
                line_ref[start + SIDE + half : start + span, :] = freq[
                    place + SIDE : place + 2 * SIDE
                ]
    skip = (span - WINDOW) // 2
    for row in range(rows):
        for column in range(BLOCK):
            value = line_ref[pl.ds(row * span + skip + column, SUB, stride=BLOCK), :]
            out_ref[row * BLOCK + column] = value
    last = (rows - FAR) * BLOCK
    for index in range(FAR * BLOCK):
        one_ref[index] = out_ref[last - last * second + index]
        two_ref[index] = out_ref[last * second + index]
    for ref in (out_ref, one_ref, two_ref):
        first = ref.shape[0] - 3
        for plane in range(3):
            ref[first + plane] = local_ref[plane * rows : (plane + 1) * rows, :]


def weight_lines(rows, parts, scratch_ref):
    planes = []
    for plane in range(3):
        blocks = [part[plane] for part in parts]
        blocks[0] = blocks[0][rows - FAR :]
        blocks[-1] = blocks[-1][:FAR]
        planes.append(jnp.concatenate(blocks, axis=0))
    east = 1.0 + 0.125 * (planes[1] + jnp.concatenate([planes[1][1:], planes[1][:1]], axis=0))
    north = 1.0 + 0.125 * (planes[2] + pltpu.roll(planes[2], LANES - 1, 1))
    total = planes[0].shape[0]
    zero = jnp.zeros((LANES - 3 * total, LANES), jnp.float32)
    scratch_ref[...] = jnp.transpose(jnp.concatenate([planes[0], east, north, zero], axis=0))
    skip = (LANES - WINDOW) // 2
    return [scratch_ref[pl.ds(skip + column, SUB, stride=BLOCK), :] for column in range(BLOCK)]


def own_columns(column):
    place = lax.broadcasted_iota(jnp.int32, (SUB, LANES), 0) * BLOCK + column
    first = (WINDOW - LANES // 2) // 2
    return (place >= first) & (place < first + LANES // 2)


def passes(edge, own, total, source, weight, coef, step_ref, remain_ref, solved_ref, emit):
    columns = range(BLOCK)

    for turn in range(CHEB + 1):
        first, last = edge + turn + 1, total - edge - turn - 1

        def load(row, turn=turn):
            if turn == 0:
                return [coef[1] * source(row, column) for column in columns]
            return [step_ref[row, column] for column in columns]

        here = load(first - 1)
        flux = None
        for row in range(first - 1, last):
            after = load(row + 1)
            ahead = [weight(1, row, column) * (here[column] - after[column]) for column in columns]
            if row >= first:
                beside = here[1:] + [pltpu.roll(here[0], SUB - 1, 0)]
                side = [weight(2, row, column) * (here[column] - beside[column]) for column in columns]
                behind = [pltpu.roll(side[-1], 1, 0)] + side[:-1]
                inside = row in range(*own)
                results = []
                for column in columns:
                    applied = (
                        weight(0, row, column) * here[column]
                        + (ahead[column] - flux[column])
                        + (side[column] - behind[column])
                    )
                    before = source(row, column) if turn == 0 else remain_ref[row, column]
                    left = before - applied
                    if turn < CHEB:
                        remain_ref[row, column] = left
                        step_ref[row, column] = (
                            coef[2 + 2 * turn] * here[column] + coef[3 + 2 * turn] * left
                        )
                    solved = None
                    if inside:
                        place = row - own[0]
                        solved = here[column]
                        if turn > 0:
                            solved = solved_ref[place, column] + solved
                        if turn < CHEB:
                            solved_ref[place, column] = solved
                    if turn == CHEB:
                        begun = source(row, column)
                        results.append((begun, solved, begun - left))
                if turn == CHEB:
                    emit(row, *zip(*results))
            here, flux = after, ahead


def stencil_kernel(
    rows, two_ref, one_ref, one_far_ref, two_far_ref, field_ref, coef_ref, place_ref,
    solved_ref, applied_ref, solved_two_ref, applied_two_ref, sums_ref,
    step_ref, remain_ref, part_ref, middle_ref, wide_ref, scratch_ref, near_ref, far_ref,
):
    columns = range(BLOCK)
    for ref, above, target_ref in (
        (one_ref, place_ref[0], near_ref),
        (two_ref, 1 - place_ref[0], near_ref),
        (one_far_ref, place_ref[1], far_ref),
        (two_far_ref, 1 - place_ref[1], far_ref),
    ):
        for index in range(ref.shape[0]):
            target_ref[1 - above, index] = ref[index]
    refs = (far_ref.at[0], near_ref.at[0], field_ref, near_ref.at[1], far_ref.at[1])
    parts = [[ref[ref.shape[0] - 3 + plane] for plane in range(3)] for ref in refs]
    lines = weight_lines(rows, parts, scratch_ref)
    coef = [coef_ref[index] for index in range(2 + 2 * CHEB)]
    places = [
        (ref, row) for ref in refs for row in range((ref.shape[0] - 3) // BLOCK)
    ]
    total = len(places)
    own = (FAR + rows, FAR + 2 * rows)
    made = set()

    def weight(plane, row, column):
        place = plane * BLOCK + column
        if (row, place) in made:
            return wide_ref[row, place]
        index = plane * total + row
        value = jnp.broadcast_to(lines[column][:, index : index + 1], (SUB, LANES))
        if plane == 0:
            value = value + coef[0]
        wide_ref[row, place] = value
        made.add((row, place))
        return value

    def first_source(row, column):
        ref, place = places[row]
        return ref[place * BLOCK + column]

    def second_source(row, column):
        return middle_ref[row, column]

    sums = [jnp.zeros((SUB, LANES), jnp.float32) for _ in range(4)]

    def add(index, one, two):
        for column in columns:
            product = one[column] * two[column]
            sums[index] = sums[index] + jnp.where(own_columns(column), product, 0.0)

    def emit_first(row, source, solved, applied):
        for column in columns:
            middle_ref[row, column] = applied[column]
        if row in range(*own):
            for column in columns:
                solved_ref[row - own[0], column] = solved[column]
                applied_ref[row - own[0], column] = applied[column]
            add(0, source, solved)
            add(1, solved, applied)

    def emit_second(row, source, solved, applied):
        for column in columns:
            solved_two_ref[row - own[0], column] = solved[column]
            applied_two_ref[row - own[0], column] = applied[column]
        add(2, source, solved)
        add(3, solved, applied)

    work = (weight, coef, step_ref, remain_ref, part_ref)
    passes(0, own, total, first_source, *work, emit_first)
    passes(HALO, own, total, second_source, *work, emit_second)

    lane = lane_index((1, LANES))
    line = jnp.zeros((1, LANES), jnp.float32)
    for index in range(4):
        line = jnp.where(lane == index, jnp.sum(sums[index]), line)
    sums_ref[...] = jnp.broadcast_to(line[None], sums_ref.shape)


def inverse_kernel(
    rows, times, length, cas_ref, sums_ref, one_ref, two_ref, three_ref, four_ref, out_ref, line_ref
):
    half = LANES // 2
    span = half + 2 * SIDE
    skip = (span - WINDOW) // 2
    line = jnp.sum(sums_ref[...].reshape(sums_ref.shape[0], LANES), axis=0, keepdims=True)
    gamma, curved, cross, last = (
        jnp.broadcast_to(line[:, index : index + 1], (SUB, LANES)) for index in range(4)
    )
    step = gamma / curved
    gamma_next = step * step * cross - gamma
    turn = gamma_next / gamma
    grown = 1.0 + turn
    next_curved = grown * grown * curved - 2.0 * step * grown * cross + step * step * last
    next_step = gamma_next / next_curved
    first = step + next_step * grown
    second = -next_step * step
    for row in range(rows):
        for index, (left_ref, right_ref) in enumerate(((one_ref, two_ref), (three_ref, four_ref))):
            for column in range(BLOCK):
                start = (2 * row + index) * span + skip + column
                value = first * left_ref[row, column] + second * right_ref[row, column]
                line_ref[pl.ds(start, SUB, stride=BLOCK), :] = value
    for row in range(rows):
        start = 2 * row * span + SIDE
        points = jnp.concatenate(
            [line_ref[start : start + half, :], line_ref[start + span : start + span + half, :]],
            axis=0,
        )
        back = exact_dot(cas_ref[...], points, 1, 1).reshape(length // times, times, LANES)
        out_ref[:, row * times : (row + 1) * times, :] = back


def final_kernel(rows, times, tiles, source_ref, field_ref, solution_ref, residual_ref):
    half = LANES // 2
    low = lane_index((rows, LANES)) < half
    for time in range(times):
        place = slice(time * rows, (time + 1) * rows)
        taken = pl.ds(time, rows, stride=times)
        for pair in range(tiles // 2):
            columns = slice(pair * LANES, (pair + 1) * LANES)
            left = source_ref[2 * pair, taken, :]
            right = source_ref[2 * pair + 1, taken, :]
            solution_ref[place, columns] = jnp.where(low, left, pltpu.roll(right, half, 1))
            change = jnp.where(low, pltpu.roll(left, half, 1), right)
            residual_ref[place, columns] = field_ref[place, columns] - change


def call(kernel, out_shape, scratch=(), inputs=0):
    shapes = [jax.ShapeDtypeStruct(shape, jnp.float32) for shape in out_shape]
    specs = {}
    if inputs:
        whole = pl.BlockSpec(memory_space=pltpu.VMEM)
        specs["in_specs"] = [whole] * (inputs - 1) + [pl.BlockSpec(memory_space=pltpu.SMEM)]
    return pl.pallas_call(
        kernel,
        out_shape=shapes[0] if len(shapes) == 1 else shapes,
        scratch_shapes=[pltpu.VMEM(shape, jnp.float32) for shape in scratch],
        compiler_params=PARAMS,
        **specs,
    )


def swap(value, distance, offset, spaces):
    pairs = [(i, (((i - offset) % spaces ^ distance) + offset) % spaces) for i in range(spaces)]
    return lax.ppermute(value, "space", pairs)


def shards(right_side, kappa, velocity):
    tiles = lax.axis_size("tm")
    spaces = lax.axis_size("space")
    times, rows, width = right_side.shape
    length = times * tiles
    tile = width // tiles
    around = (LANES - tile) // 2
    cas_table = jnp.asarray(hartley_table(length))
    coef_table = jnp.asarray(chebyshev_table(length))

    field = right_side.reshape(times * rows, width)
    windows = call(
        functools.partial(window_kernel, rows, times, tiles),
        [(tiles, 6 * times, LANES)],
        [(width // LANES, times * rows, LANES)],
    )(field)
    gathered = lax.all_to_all(windows, "tm", 0, 0)

    squares = velocity.astype(jnp.float32) ** 2
    planes = jnp.concatenate([kappa, squares[0], squares[1]], axis=0)
    planes = jnp.concatenate([planes[:, -around:], planes, planes[:, :around]], axis=1)
    local = lax.dynamic_slice_in_dim(planes, lax.axis_index("tm") * tile, LANES, 1)
    total = 3 * rows + 2 * FAR
    tile_shape = (rows, BLOCK, SUB, LANES)
    row_shape = (rows * BLOCK + 3, SUB, LANES)
    far_shape = (FAR * BLOCK + 3, SUB, LANES)
    span = LANES // 2 + 2 * SIDE
    index = lax.axis_index("space")
    place = jnp.stack([index % 2, index // 2 % 2]).astype(jnp.int32)
    freq, inner_far, outer_far = call(
        functools.partial(forward_kernel, rows, times, length),
        [row_shape, far_shape, far_shape],
        [(rows * span, LANES)],
        inputs=4,
    )(cas_table, gathered, local, place)
    outer = swap(freq, 1, 1, spaces)
    inner = swap(freq, 1, 0, spaces)
    outer_far = swap(outer_far, 2, 2, spaces)
    inner_far = swap(inner_far, 2, 0, spaces)

    groups = [
        [i * spaces + first + j for i in range(tiles) for j in range(NEAR)]
        for first in range(0, spaces, NEAR)
    ]
    work = (total, BLOCK, SUB, LANES)
    solved, applied, solved_two, applied_two, sums = call(
        functools.partial(stencil_kernel, rows),
        [tile_shape] * 4 + [(tiles * NEAR, 1, LANES)],
        [
            work,
            work,
            tile_shape,
            work,
            (total, 3 * BLOCK, SUB, LANES),
            (LANES, LANES),
            (2, *row_shape),
            (2, *far_shape),
        ],
        inputs=7,
    )(outer, inner, inner_far, outer_far, freq, coef_table, place)
    sums = lax.all_to_all(sums, ("tm", "space"), 0, 0, axis_index_groups=groups)
    planes = spaces // NEAR
    groups = [[first + NEAR * i for i in range(planes)] for first in range(NEAR)]
    sums = jnp.broadcast_to(jnp.sum(sums, axis=0)[None], (planes, 1, LANES))
    sums = lax.all_to_all(sums, "space", 0, 0, axis_index_groups=groups)
    packed = call(
        functools.partial(inverse_kernel, rows, times, length),
        [(tiles, rows * times, LANES)],
        [(rows * 2 * span, LANES)],
    )(cas_table, sums, solved, solved_two, applied, applied_two)
    returned = lax.all_to_all(packed, "tm", 0, 0)

    solution, residual = call(
        functools.partial(final_kernel, rows, times, tiles),
        [(times * rows, width), (times * rows, width)],
    )(returned, field)
    shape = right_side.shape
    return solution.reshape(shape), residual.reshape(shape)


def solution(mesh):
    placed = (P("tm", "space", None), P("space", None), P(None, "space", None))
    return jax.shard_map(
        shards,
        mesh=mesh,
        in_specs=placed,
        out_specs=(P("tm", "space", None), P("tm", "space", None)),
        check_vma=False,
    )
```

```python
import functools
import math

import jax
import jax.numpy as jnp
import numpy as np
from jax import lax
from jax.experimental import pallas as pl
from jax.experimental.pallas import tpu as pltpu
from jax.sharding import PartitionSpec as P

CHEB = 4
COUPLING = 2.0
KAPPA_LOW = 0.05
KAPPA_HIGH = 1.0
REACH = 16.0

LANES = 128
SUB = 8
HALO = CHEB + 1
FAR = 2
SIDE = 16
BLOCK = 11
WINDOW = SUB * BLOCK
NEAR = 4
PARAMS = pltpu.CompilerParams(vmem_limit_bytes=24 * 1024 * 1024)


def hartley_table(length):
    index = np.arange(length)
    angle = (index[:, None] * index[None, :] % length) * (2.0 * math.pi / length)
    return ((np.cos(angle) + np.sin(angle)) / math.sqrt(length)).astype(np.float32)


def chebyshev_table(length):
    shift = COUPLING * (2.0 - 2.0 * np.cos(2.0 * math.pi * np.arange(length) / length))
    half = 0.5 * (KAPPA_HIGH + REACH - KAPPA_LOW)
    mid = 0.5 * (KAPPA_LOW + KAPPA_HIGH + REACH) + shift
    ratio = mid / half
    damp = 1.0 / ratio
    lines = [shift, 1.0 / mid]
    for _ in range(CHEB):
        damp_next = 1.0 / (2.0 * ratio - damp)
        lines += [damp_next * damp, 2.0 * damp_next / half]
        damp = damp_next
    return np.repeat(np.stack(lines).astype(np.float32)[:, None], SUB, 1)


def lane_index(shape):
    return lax.broadcasted_iota(jnp.int32, shape, len(shape) - 1)


def exact_dot(left, right, left_dim, right_dim):
    return lax.dot_general(
        left,
        right,
        (((left_dim,), (right_dim,)), ((), ())),
        precision=lax.Precision.HIGHEST,
        preferred_element_type=jnp.float32,
    )


def window_kernel(rows, times, tiles, source_ref, out_ref, scratch_ref):
    half = LANES // 2
    parts = source_ref.shape[1] // LANES
    for part in range(parts):
        scratch_ref[part] = source_ref[:, part * LANES : (part + 1) * LANES]
    lane = lane_index((times, LANES))
    fields = [
        [scratch_ref[part, pl.ds(row, times, stride=rows), :] for part in range(parts)]
        for row in range(rows)
    ]
    for pair in range(rows // 2):
        for part in range(parts):
            one, two = fields[2 * pair][part], fields[2 * pair + 1][part]
            place = slice(pair * times, (pair + 1) * times)
            out_ref[2 * part, place, :] = jnp.where(lane < half, one, pltpu.roll(two, half, 1))
            out_ref[2 * part + 1, place, :] = jnp.where(lane < half, pltpu.roll(one, half, 1), two)
    spread = 2 * SIDE
    group = LANES // spread
    for quad in range(rows // group):
        even = [None] * parts
        odd = [None] * parts
        for index in range(group):
            row = quad * group + index
            wide = jnp.concatenate(fields[row], axis=1)
            near = pltpu.roll(wide, spread * index + SIDE, 1)
            away = pltpu.roll(wide, (spread * index - half + SIDE) % wide.shape[1], 1)
            left = (lane >= spread * index) & (lane < spread * index + SIDE)
            right = (lane >= spread * index + SIDE) & (lane < spread * (index + 1))
            for part in range(parts):
                here = slice(part * LANES, (part + 1) * LANES)
                then = (part + 1) % parts
                then = slice(then * LANES, (then + 1) * LANES)
                if index == 0:
                    even[part] = jnp.where(left, near[:, here], away[:, here])
                    odd[part] = jnp.where(left, away[:, here], near[:, then])
                else:
                    even[part] = jnp.where(
                        left, near[:, here], jnp.where(right, away[:, here], even[part])
                    )
                    odd[part] = jnp.where(
                        left, away[:, here], jnp.where(right, near[:, then], odd[part])
                    )
        start = (rows // 2 + quad) * times
        for part in range(parts):
            out_ref[2 * part, start : start + times, :] = even[part]
            out_ref[2 * part + 1, start : start + times, :] = odd[part]


def forward_kernel(
    rows, times, length, cas_ref, field_ref, local_ref, out_ref, low_ref, high_ref, line_ref
):
    half = LANES // 2
    span = half + 2 * SIDE
    pieces = field_ref.shape[1] // times
    group = LANES // (2 * SIDE)
    for piece in range(pieces):
        block = field_ref[:, piece * times : (piece + 1) * times, :].reshape(length, LANES)
        freq = exact_dot(block, cas_ref[...], 0, 0)
        if piece < rows // 2:
            for part in range(2):
                start = (2 * piece + part) * span + SIDE
                line_ref[start : start + half, :] = freq[part * half : (part + 1) * half]
        else:
            for index in range(group):
                start = ((piece - rows // 2) * group + index) * span
                place = 2 * SIDE * index
                line_ref[start : start + SIDE, :] = freq[place : place + SIDE]
                line_ref[start + SIDE + half : start + span, :] = freq[
                    place + SIDE : place + 2 * SIDE
                ]
    skip = (span - WINDOW) // 2
    for row in range(rows):
        for column in range(BLOCK):
            value = line_ref[pl.ds(row * span + skip + column, SUB, stride=BLOCK), :]
            out_ref[row * BLOCK + column] = value
            if row < FAR:
                low_ref[row * BLOCK + column] = value
            if row >= rows - FAR:
                high_ref[(row - (rows - FAR)) * BLOCK + column] = value
    for ref in (out_ref, low_ref, high_ref):
        first = ref.shape[0] - 3
        for plane in range(3):
            ref[first + plane] = local_ref[plane * rows : (plane + 1) * rows, :]


def weight_lines(parts, scratch_ref):
    planes = [jnp.concatenate(blocks, axis=0) for blocks in zip(*parts)]
    east = 1.0 + 0.125 * (planes[1] + jnp.concatenate([planes[1][1:], planes[1][:1]], axis=0))
    north = 1.0 + 0.125 * (planes[2] + pltpu.roll(planes[2], LANES - 1, 1))
    zero = jnp.zeros((LANES - 3 * planes[0].shape[0], LANES), jnp.float32)
    scratch_ref[...] = jnp.transpose(jnp.concatenate([planes[0], east, north, zero], axis=0))
    skip = (LANES - WINDOW) // 2
    return [scratch_ref[pl.ds(skip + column, SUB, stride=BLOCK), :] for column in range(BLOCK)]


def weight_part(ref):
    return [ref[ref.shape[0] - 3 + plane] for plane in range(3)]


def spread(lines, index, plane, coef):
    value = jnp.broadcast_to(lines[:, index : index + 1], (SUB, LANES))
    return value + coef[0] if plane == 0 else value


def own_columns(column):
    place = lax.broadcasted_iota(jnp.int32, (SUB, LANES), 0) * BLOCK + column
    first = (WINDOW - LANES // 2) // 2
    return (place >= first) & (place < first + LANES // 2)


def stencil(weight, row, above, here, below, flux=None):
    columns = range(BLOCK)
    if flux is None:
        flux = [weight(1, row - 1, column) * (above[column] - here[column]) for column in columns]
    ahead = [weight(1, row, column) * (here[column] - below[column]) for column in columns]
    beside = here[1:] + [pltpu.roll(here[0], SUB - 1, 0)]
    side = [weight(2, row, column) * (here[column] - beside[column]) for column in columns]
    behind = [pltpu.roll(side[-1], 1, 0)] + side[:-1]
    applied = [
        weight(0, row, column) * here[column]
        + (ahead[column] - flux[column])
        + (side[column] - behind[column])
        for column in columns
    ]
    return applied, ahead


def passes(
    edge, own, total, source, weight, coef, step_ref, remain_ref, solved_ref, emit, border=None
):
    columns = range(BLOCK)

    for turn in range(CHEB + 1):
        first, last = edge + turn + 1, total - edge - turn - 1

        def load(row, turn=turn):
            if turn == 0:
                return [coef[1] * source(row, column) for column in columns]
            return [step_ref[row, column] for column in columns]

        above, here = load(first - 1), load(first)
        flux = None
        for row in range(first, last):
            below = load(row + 1)
            if border and row == first:
                border(0, turn, here)
            if border and row == last - 1:
                border(1, turn, here)
            applied, flux = stencil(weight, row, above, here, below, flux)
            inside = row in range(*own)
            results = []
            for column in columns:
                before = source(row, column) if turn == 0 else remain_ref[row, column]
                left = before - applied[column]
                if turn < CHEB:
                    remain_ref[row, column] = left
                    step_ref[row, column] = (
                        coef[2 + 2 * turn] * here[column] + coef[3 + 2 * turn] * left
                    )
                solved = None
                if inside:
                    place = row - own[0]
                    solved = here[column]
                    if turn > 0:
                        solved = solved_ref[place, column] + solved
                    if turn < CHEB:
                        solved_ref[place, column] = solved
                if turn == CHEB:
                    begun = source(row, column)
                    results.append((begun, solved, begun - left))
            if turn == CHEB:
                emit(row, *zip(*results))
            above, here = here, below


def add_products(sums, index, one, two):
    for column in range(BLOCK):
        product = one[column] * two[column]
        sums[index] = sums[index] + jnp.where(own_columns(column), product, 0.0)


def near_kernel(
    rows, top_ref, field_ref, bottom_ref, coef_ref,
    solved_ref, middle_ref, step_ref, remain_ref, border_ref, wide_ref, early_ref,
    part_ref, scratch_ref,
):
    refs = (top_ref, field_ref, bottom_ref)
    lines = weight_lines([weight_part(ref) for ref in refs], scratch_ref)
    coef = [coef_ref[index] for index in range(2 + 2 * CHEB)]
    places = [None] * FAR + [(ref, row) for ref in refs for row in range(rows)]
    total = 3 * rows + 2 * FAR
    own = (FAR + rows, FAR + 2 * rows)
    made = set()

    def weight(plane, row, column):
        place = plane * BLOCK + column
        if (row, place) not in made:
            made.add((row, place))
            wide_ref[row, place] = spread(lines[column], plane * 3 * rows + row - FAR, plane, coef)
        return wide_ref[row, place]

    def source(row, column):
        ref, place = places[row]
        return ref[place * BLOCK + column]

    sums = [jnp.zeros((SUB, LANES), jnp.float32) for _ in range(2)]

    def emit(row, begun, solved, applied):
        for column in range(BLOCK):
            middle_ref[row, column] = applied[column]
        if row in range(*own):
            for column in range(BLOCK):
                solved_ref[row - own[0], column] = solved[column]
            add_products(sums, 0, begun, solved)
            add_products(sums, 1, solved, applied)

    def border(side, turn, step):
        for column in range(BLOCK):
            border_ref[side, turn, column] = step[column]

    passes(
        FAR, own, total, source, weight, coef, step_ref, remain_ref, part_ref, emit, border
    )
    early_ref[0] = sums[0]
    early_ref[1] = sums[1]


def far_kernel(
    rows, top_far_ref, top_ref, field_ref, bottom_ref, bottom_far_ref, coef_ref,
    middle_ref, frozen_step_ref, frozen_remain_ref, border_ref, wide_ref, early_ref,
    solved_ref, applied_ref, sums_ref,
    step_ref, remain_ref, part_ref, outer_ref, scratch_ref,
):
    columns = range(BLOCK)
    refs = (top_far_ref, top_ref, field_ref, bottom_ref, bottom_far_ref)
    parts = [weight_part(ref) for ref in refs]
    parts[0] = [block[rows - FAR :] for block in parts[0]]
    parts[-1] = [block[:FAR] for block in parts[-1]]
    lines = weight_lines(parts, scratch_ref)
    coef = [coef_ref[index] for index in range(2 + 2 * CHEB)]
    total = 3 * rows + 2 * FAR
    own = (FAR + rows, FAR + 2 * rows)
    places = [
        (ref, row) for ref in refs for row in range((ref.shape[0] - 3) // BLOCK)
    ]
    made = {}

    def weight(plane, row, column):
        if FAR < row < total - FAR - 1 or (plane == 1 and row == FAR):
            return wide_ref[row, plane * BLOCK + column]
        key = (plane, row, column)
        if key not in made:
            made[key] = spread(lines[column], plane * total + row, plane, coef)
        return made[key]

    def source(row):
        ref, place = places[row]
        return [ref[place * BLOCK + column] for column in columns]

    for side in range(2):

        def at(index, side=side):
            return total - 1 - index if side else index

        ends = [[coef[1] * value for value in source(at(index))] for index in range(FAR)]
        rest = source(at(1))
        for turn in range(CHEB + 1):
            edge_row = at(turn + 2)
            if turn == 0:
                inner = [coef[1] * value for value in source(edge_row)]
                inner_rest = source(edge_row)
            else:
                inner = [frozen_step_ref[edge_row, column] for column in columns]
                inner_rest = [frozen_remain_ref[edge_row, column] for column in columns]
            steps = ends + [inner, [border_ref[side, turn, column] for column in columns]]
            new_ends, new_rest = [], []
            for index, before in ((1, rest), (2, inner_rest)):
                row = at(turn + index)
                near, away = steps[index - 1], steps[index + 1]
                above, below = (away, near) if side else (near, away)
                here = steps[index]
                applied, _ = stencil(weight, row, above, here, below)
                left = [before[column] - applied[column] for column in columns]
                new_rest.append(left)
                if turn < CHEB:
                    new_ends.append(
                        [
                            coef[2 + 2 * turn] * here[column] + coef[3 + 2 * turn] * left[column]
                            for column in columns
                        ]
                    )
                else:
                    begun = source(row)
                    for column in columns:
                        outer_ref[side * FAR + index - 1, column] = begun[column] - left[column]
            ends, rest = new_ends, new_rest[1]

    def middle(row, column):
        index = min(row, total - 1 - row)
        if index < HALO + FAR:
            return outer_ref[FAR * (row > index) + index - HALO, column]
        return middle_ref[row, column]

    sums = [early_ref[0], early_ref[1]] + [jnp.zeros((SUB, LANES), jnp.float32) for _ in range(2)]

    def emit(row, begun, solved, applied):
        for column in columns:
            solved_ref[row - own[0], column] = solved[column]
            applied_ref[row - own[0], column] = applied[column]
        add_products(sums, 2, begun, solved)
        add_products(sums, 3, solved, applied)

    passes(HALO, own, total, middle, weight, coef, step_ref, remain_ref, part_ref, emit)

    lane = lane_index((1, LANES))
    line = jnp.zeros((1, LANES), jnp.float32)
    for index in range(4):
        line = jnp.where(lane == index, jnp.sum(sums[index]), line)
    sums_ref[...] = jnp.broadcast_to(line[None], sums_ref.shape)


def inverse_kernel(
    rows, times, length, cas_ref, sums_ref, one_ref, two_ref, three_ref, four_ref, out_ref, line_ref
):
    half = LANES // 2
    span = half + 2 * SIDE
    skip = (span - WINDOW) // 2
    line = jnp.sum(sums_ref[...].reshape(sums_ref.shape[0], LANES), axis=0, keepdims=True)
    gamma, curved, cross, last = (
        jnp.broadcast_to(line[:, index : index + 1], (SUB, LANES)) for index in range(4)
    )
    step = gamma / curved
    gamma_next = step * step * cross - gamma
    turn = gamma_next / gamma
    grown = 1.0 + turn
    next_curved = grown * grown * curved - 2.0 * step * grown * cross + step * step * last
    next_step = gamma_next / next_curved
    first = step + next_step * grown
    second = -next_step * step
    for row in range(rows):
        for index, (left_ref, right_ref) in enumerate(((one_ref, two_ref), (three_ref, four_ref))):
            offset = left_ref.shape[0] // 2 - rows // 2
            for column in range(BLOCK):
                start = (2 * row + index) * span + skip + column
                value = first * left_ref[offset + row, column] + second * right_ref[row, column]
                line_ref[pl.ds(start, SUB, stride=BLOCK), :] = value
    for row in range(rows):
        start = 2 * row * span + SIDE
        points = jnp.concatenate(
            [line_ref[start : start + half, :], line_ref[start + span : start + span + half, :]],
            axis=0,
        )
        back = exact_dot(cas_ref[...], points, 1, 1).reshape(length // times, times, LANES)
        out_ref[:, row * times : (row + 1) * times, :] = back


def final_kernel(rows, times, tiles, source_ref, field_ref, solution_ref, residual_ref):
    half = LANES // 2
    low = lane_index((rows, LANES)) < half
    for time in range(times):
        place = slice(time * rows, (time + 1) * rows)
        taken = pl.ds(time, rows, stride=times)
        for pair in range(tiles // 2):
            columns = slice(pair * LANES, (pair + 1) * LANES)
            left = source_ref[2 * pair, taken, :]
            right = source_ref[2 * pair + 1, taken, :]
            solution_ref[place, columns] = jnp.where(low, left, pltpu.roll(right, half, 1))
            change = jnp.where(low, pltpu.roll(left, half, 1), right)
            residual_ref[place, columns] = field_ref[place, columns] - change


def call(kernel, out_shape, scratch=()):
    shapes = [jax.ShapeDtypeStruct(shape, jnp.float32) for shape in out_shape]
    return pl.pallas_call(
        kernel,
        out_shape=shapes[0] if len(shapes) == 1 else shapes,
        scratch_shapes=[pltpu.VMEM(shape, jnp.float32) for shape in scratch],
        compiler_params=PARAMS,
    )


def shift(value, distance, spaces):
    return lax.ppermute(value, "space", [(i, (i + distance) % spaces) for i in range(spaces)])


def shards(right_side, kappa, velocity):
    tiles = lax.axis_size("tm")
    spaces = lax.axis_size("space")
    times, rows, width = right_side.shape
    length = times * tiles
    tile = width // tiles
    around = (LANES - tile) // 2
    cas_table = jnp.asarray(hartley_table(length))
    coef_table = jnp.asarray(chebyshev_table(length))

    field = right_side.reshape(times * rows, width)
    windows = call(
        functools.partial(window_kernel, rows, times, tiles),
        [(tiles, 6 * times, LANES)],
        [(width // LANES, times * rows, LANES)],
    )(field)
    gathered = lax.all_to_all(windows, "tm", 0, 0)

    squares = velocity.astype(jnp.float32) ** 2
    planes = jnp.concatenate([kappa, squares[0], squares[1]], axis=0)
    planes = jnp.concatenate([planes[:, -around:], planes, planes[:, :around]], axis=1)
    local = lax.dynamic_slice_in_dim(planes, lax.axis_index("tm") * tile, LANES, 1)
    total = 3 * rows + 2 * FAR
    tile_shape = (rows, BLOCK, SUB, LANES)
    row_shape = (rows * BLOCK + 3, SUB, LANES)
    far_shape = (FAR * BLOCK + 3, SUB, LANES)
    span = LANES // 2 + 2 * SIDE
    freq, low, high = call(
        functools.partial(forward_kernel, rows, times, length),
        [row_shape, far_shape, far_shape],
        [(rows * span, LANES)],
    )(cas_table, gathered, local)
    top, bottom = shift(freq, 1, spaces), shift(freq, -1, spaces)
    top_far, bottom_far = shift(high, 2, spaces), shift(low, -2, spaces)

    groups = [
        [i * spaces + first + j for i in range(tiles) for j in range(NEAR)]
        for first in range(0, spaces, NEAR)
    ]
    work = (total, BLOCK, SUB, LANES)
    solved, middle, step, remain, border, wide, early = call(
        functools.partial(near_kernel, rows),
        [
            tile_shape,
            work,
            work,
            work,
            (2, CHEB + 1, BLOCK, SUB, LANES),
            (total, 3 * BLOCK, SUB, LANES),
            (2, SUB, LANES),
        ],
        [tile_shape, (LANES, LANES)],
    )(top, freq, bottom, coef_table)
    solved_two, applied_two, sums = call(
        functools.partial(far_kernel, rows),
        [tile_shape, tile_shape, (tiles * NEAR, 1, LANES)],
        [work, work, tile_shape, (2 * FAR, BLOCK, SUB, LANES), (LANES, LANES)],
    )(
        top_far, top, freq, bottom, bottom_far, coef_table, middle, step, remain, border, wide, early
    )
    sums = lax.all_to_all(sums, ("tm", "space"), 0, 0, axis_index_groups=groups)
    planes = spaces // NEAR
    groups = [[first + NEAR * i for i in range(planes)] for first in range(NEAR)]
    sums = jnp.broadcast_to(jnp.sum(sums, axis=0)[None], (planes, 1, LANES))
    sums = lax.all_to_all(sums, "space", 0, 0, axis_index_groups=groups)
    packed = call(
        functools.partial(inverse_kernel, rows, times, length),
        [(tiles, rows * times, LANES)],
        [(rows * 2 * span, LANES)],
    )(cas_table, sums, solved, solved_two, middle, applied_two)
    returned = lax.all_to_all(packed, "tm", 0, 0)

    solution, residual = call(
        functools.partial(final_kernel, rows, times, tiles),
        [(times * rows, width), (times * rows, width)],
    )(returned, field)
    shape = right_side.shape
    return solution.reshape(shape), residual.reshape(shape)


def solution(mesh):
    placed = (P("tm", "space", None), P("space", None), P(None, "space", None))
    return jax.shard_map(
        shards,
        mesh=mesh,
        in_specs=placed,
        out_specs=(P("tm", "space", None), P("tm", "space", None)),
        check_vma=False,
    )
```

```python
import functools
import math

import jax
import jax.numpy as jnp
import numpy as np
from jax import lax
from jax.experimental import pallas as pl
from jax.experimental.pallas import tpu as pltpu
from jax.sharding import PartitionSpec as P

CHEB = 4
COUPLING = 2.0
KAPPA_LOW = 0.05
KAPPA_HIGH = 1.0
REACH = 16.0

LANES = 128
SUB = 8
HALO = CHEB + 1
FAR = 2
SIDE = 16
BLOCK = 11
WINDOW = SUB * BLOCK
NEAR = 4
PARAMS = pltpu.CompilerParams(vmem_limit_bytes=24 * 1024 * 1024)


def hartley_table(length):
    index = np.arange(length)
    angle = (index[:, None] * index[None, :] % length) * (2.0 * math.pi / length)
    return ((np.cos(angle) + np.sin(angle)) / math.sqrt(length)).astype(np.float32)


def chebyshev_table(length):
    shift = COUPLING * (2.0 - 2.0 * np.cos(2.0 * math.pi * np.arange(length) / length))
    half = 0.5 * (KAPPA_HIGH + REACH - KAPPA_LOW)
    mid = 0.5 * (KAPPA_LOW + KAPPA_HIGH + REACH) + shift
    ratio = mid / half
    damp = 1.0 / ratio
    lines = [shift, 1.0 / mid]
    for _ in range(CHEB):
        damp_next = 1.0 / (2.0 * ratio - damp)
        lines += [damp_next * damp, 2.0 * damp_next / half]
        damp = damp_next
    return np.repeat(np.stack(lines).astype(np.float32)[:, None], SUB, 1)


def lane_index(shape):
    return lax.broadcasted_iota(jnp.int32, shape, len(shape) - 1)


def exact_dot(left, right, left_dim, right_dim):
    return lax.dot_general(
        left,
        right,
        (((left_dim,), (right_dim,)), ((), ())),
        precision=lax.Precision.HIGHEST,
        preferred_element_type=jnp.float32,
    )


def window_kernel(rows, times, tiles, source_ref, out_ref, scratch_ref):
    half = LANES // 2
    parts = source_ref.shape[1] // LANES
    for part in range(parts):
        scratch_ref[part] = source_ref[:, part * LANES : (part + 1) * LANES]
    lane = lane_index((times, LANES))
    fields = [
        [scratch_ref[part, pl.ds(row, times, stride=rows), :] for part in range(parts)]
        for row in range(rows)
    ]
    for pair in range(rows // 2):
        for part in range(parts):
            one, two = fields[2 * pair][part], fields[2 * pair + 1][part]
            place = slice(pair * times, (pair + 1) * times)
            out_ref[2 * part, place, :] = jnp.where(lane < half, one, pltpu.roll(two, half, 1))
            out_ref[2 * part + 1, place, :] = jnp.where(lane < half, pltpu.roll(one, half, 1), two)
    spread = 2 * SIDE
    group = LANES // spread
    for quad in range(rows // group):
        even = [None] * parts
        odd = [None] * parts
        for index in range(group):
            row = quad * group + index
            wide = jnp.concatenate(fields[row], axis=1)
            near = pltpu.roll(wide, spread * index + SIDE, 1)
            away = pltpu.roll(wide, (spread * index - half + SIDE) % wide.shape[1], 1)
            left = (lane >= spread * index) & (lane < spread * index + SIDE)
            right = (lane >= spread * index + SIDE) & (lane < spread * (index + 1))
            for part in range(parts):
                here = slice(part * LANES, (part + 1) * LANES)
                then = (part + 1) % parts
                then = slice(then * LANES, (then + 1) * LANES)
                if index == 0:
                    even[part] = jnp.where(left, near[:, here], away[:, here])
                    odd[part] = jnp.where(left, away[:, here], near[:, then])
                else:
                    even[part] = jnp.where(
                        left, near[:, here], jnp.where(right, away[:, here], even[part])
                    )
                    odd[part] = jnp.where(
                        left, away[:, here], jnp.where(right, near[:, then], odd[part])
                    )
        start = (rows // 2 + quad) * times
        for part in range(parts):
            out_ref[2 * part, start : start + times, :] = even[part]
            out_ref[2 * part + 1, start : start + times, :] = odd[part]


def forward_kernel(
    rows, times, length, cas_ref, field_ref, local_ref, out_ref, low_ref, high_ref, line_ref
):
    half = LANES // 2
    span = half + 2 * SIDE
    pieces = field_ref.shape[1] // times
    group = LANES // (2 * SIDE)
    for piece in range(pieces):
        block = field_ref[:, piece * times : (piece + 1) * times, :].reshape(length, LANES)
        freq = exact_dot(block, cas_ref[...], 0, 0)
        if piece < rows // 2:
            for part in range(2):
                start = (2 * piece + part) * span + SIDE
                line_ref[start : start + half, :] = freq[part * half : (part + 1) * half]
        else:
            for index in range(group):
                start = ((piece - rows // 2) * group + index) * span
                place = 2 * SIDE * index
                line_ref[start : start + SIDE, :] = freq[place : place + SIDE]
                line_ref[start + SIDE + half : start + span, :] = freq[
                    place + SIDE : place + 2 * SIDE
                ]
    skip = (span - WINDOW) // 2
    for row in range(rows):
        for column in range(BLOCK):
            value = line_ref[pl.ds(row * span + skip + column, SUB, stride=BLOCK), :]
            out_ref[row * BLOCK + column] = value
            if row < FAR:
                low_ref[row * BLOCK + column] = value
            if row >= rows - FAR:
                high_ref[(row - (rows - FAR)) * BLOCK + column] = value
    for ref in (out_ref, low_ref, high_ref):
        first = ref.shape[0] - 3
        for plane in range(3):
            ref[first + plane] = local_ref[plane * rows : (plane + 1) * rows, :]


def weight_lines(parts, scratch_ref):
    planes = [jnp.concatenate(blocks, axis=0) for blocks in zip(*parts)]
    east = 1.0 + 0.125 * (planes[1] + jnp.concatenate([planes[1][1:], planes[1][:1]], axis=0))
    north = 1.0 + 0.125 * (planes[2] + pltpu.roll(planes[2], LANES - 1, 1))
    zero = jnp.zeros((LANES - 3 * planes[0].shape[0], LANES), jnp.float32)
    scratch_ref[...] = jnp.transpose(jnp.concatenate([planes[0], east, north, zero], axis=0))
    skip = (LANES - WINDOW) // 2
    return [scratch_ref[pl.ds(skip + column, SUB, stride=BLOCK), :] for column in range(BLOCK)]


def weight_part(ref):
    return [ref[ref.shape[0] - 3 + plane] for plane in range(3)]


def spread(lines, index, plane, coef):
    value = jnp.broadcast_to(lines[:, index : index + 1], (SUB, LANES))
    return value + coef[0] if plane == 0 else value


def own_columns(column):
    place = lax.broadcasted_iota(jnp.int32, (SUB, LANES), 0) * BLOCK + column
    first = (WINDOW - LANES // 2) // 2
    return (place >= first) & (place < first + LANES // 2)


def stencil(weight, row, above, here, below, flux=None):
    columns = range(BLOCK)
    if flux is None:
        flux = [weight(1, row - 1, column) * (above[column] - here[column]) for column in columns]
    ahead = [weight(1, row, column) * (here[column] - below[column]) for column in columns]
    beside = here[1:] + [pltpu.roll(here[0], SUB - 1, 0)]
    side = [weight(2, row, column) * (here[column] - beside[column]) for column in columns]
    behind = [pltpu.roll(side[-1], 1, 0)] + side[:-1]
    applied = [
        weight(0, row, column) * here[column]
        + (ahead[column] - flux[column])
        + (side[column] - behind[column])
        for column in columns
    ]
    return applied, ahead


def passes(
    edge, own, total, source, weight, coef, step_ref, remain_ref, solved_ref, emit, border=None
):
    columns = range(BLOCK)

    for turn in range(CHEB + 1):
        first, last = edge + turn + 1, total - edge - turn - 1

        def load(row, turn=turn):
            if turn == 0:
                return [coef[1] * source(row, column) for column in columns]
            return [step_ref[row, column] for column in columns]

        above, here = load(first - 1), load(first)
        flux = None
        for row in range(first, last):
            below = load(row + 1)
            if border and row == first:
                border(0, turn, here)
            if border and row == last - 1:
                border(1, turn, here)
            applied, flux = stencil(weight, row, above, here, below, flux)
            inside = row in range(*own)
            results = []
            for column in columns:
                before = source(row, column) if turn == 0 else remain_ref[row, column]
                left = before - applied[column]
                if turn < CHEB:
                    remain_ref[row, column] = left
                    step_ref[row, column] = (
                        coef[2 + 2 * turn] * here[column] + coef[3 + 2 * turn] * left
                    )
                solved = None
                if inside:
                    place = row - own[0]
                    solved = here[column]
                    if turn > 0:
                        solved = solved_ref[place, column] + solved
                    if turn < CHEB:
                        solved_ref[place, column] = solved
                if turn == CHEB:
                    begun = source(row, column)
                    results.append((begun, solved, begun - left))
            if turn == CHEB:
                emit(row, *zip(*results))
            above, here = here, below


def add_products(sums, index, one, two):
    for column in range(BLOCK):
        product = one[column] * two[column]
        sums[index] = sums[index] + jnp.where(own_columns(column), product, 0.0)


def near_kernel(
    rows, bottom_ref, field_ref, top_ref, coef_ref,
    solved_ref, middle_ref, step_ref, remain_ref, border_ref, wide_ref, early_ref,
    part_ref, scratch_ref,
):
    refs = (top_ref, field_ref, bottom_ref)
    lines = weight_lines([weight_part(ref) for ref in refs], scratch_ref)
    coef = [coef_ref[index] for index in range(2 + 2 * CHEB)]
    places = [None] * FAR + [(ref, row) for ref in refs for row in range(rows)]
    total = 3 * rows + 2 * FAR
    own = (FAR + rows, FAR + 2 * rows)
    made = set()

    def weight(plane, row, column):
        place = plane * BLOCK + column
        if (row, place) not in made:
            made.add((row, place))
            wide_ref[row, place] = spread(lines[column], plane * 3 * rows + row - FAR, plane, coef)
        return wide_ref[row, place]

    def source(row, column):
        ref, place = places[row]
        return ref[place * BLOCK + column]

    sums = [jnp.zeros((SUB, LANES), jnp.float32) for _ in range(2)]

    def emit(row, begun, solved, applied):
        for column in range(BLOCK):
            middle_ref[row, column] = applied[column]
        if row in range(*own):
            for column in range(BLOCK):
                solved_ref[row - own[0], column] = solved[column]
            add_products(sums, 0, begun, solved)
            add_products(sums, 1, solved, applied)

    def border(side, turn, step):
        for column in range(BLOCK):
            border_ref[side, turn, column] = step[column]

    passes(
        FAR, own, total, source, weight, coef, step_ref, remain_ref, part_ref, emit, border
    )
    early_ref[0] = sums[0]
    early_ref[1] = sums[1]


def far_kernel(
    rows, top_far_ref, top_ref, field_ref, bottom_ref, bottom_far_ref, coef_ref,
    middle_ref, frozen_step_ref, frozen_remain_ref, border_ref, wide_ref, early_ref,
    solved_ref, applied_ref, sums_ref,
    step_ref, remain_ref, part_ref, outer_ref, scratch_ref,
):
    columns = range(BLOCK)
    refs = (top_far_ref, top_ref, field_ref, bottom_ref, bottom_far_ref)
    parts = [weight_part(ref) for ref in refs]
    parts[0] = [block[rows - FAR :] for block in parts[0]]
    parts[-1] = [block[:FAR] for block in parts[-1]]
    lines = weight_lines(parts, scratch_ref)
    coef = [coef_ref[index] for index in range(2 + 2 * CHEB)]
    total = 3 * rows + 2 * FAR
    own = (FAR + rows, FAR + 2 * rows)
    places = [
        (ref, row) for ref in refs for row in range((ref.shape[0] - 3) // BLOCK)
    ]
    made = {}

    def weight(plane, row, column):
        if FAR < row < total - FAR - 1 or (plane == 1 and row == FAR):
            return wide_ref[row, plane * BLOCK + column]
        key = (plane, row, column)
        if key not in made:
            made[key] = spread(lines[column], plane * total + row, plane, coef)
        return made[key]

    def source(row):
        ref, place = places[row]
        return [ref[place * BLOCK + column] for column in columns]

    for side in range(2):

        def at(index, side=side):
            return total - 1 - index if side else index

        ends = [[coef[1] * value for value in source(at(index))] for index in range(FAR)]
        rest = source(at(1))
        for turn in range(CHEB + 1):
            edge_row = at(turn + 2)
            if turn == 0:
                inner = [coef[1] * value for value in source(edge_row)]
                inner_rest = source(edge_row)
            else:
                inner = [frozen_step_ref[edge_row, column] for column in columns]
                inner_rest = [frozen_remain_ref[edge_row, column] for column in columns]
            steps = ends + [inner, [border_ref[side, turn, column] for column in columns]]
            new_ends, new_rest = [], []
            for index, before in ((1, rest), (2, inner_rest)):
                row = at(turn + index)
                near, away = steps[index - 1], steps[index + 1]
                above, below = (away, near) if side else (near, away)
                here = steps[index]
                applied, _ = stencil(weight, row, above, here, below)
                left = [before[column] - applied[column] for column in columns]
                new_rest.append(left)
                if turn < CHEB:
                    new_ends.append(
                        [
                            coef[2 + 2 * turn] * here[column] + coef[3 + 2 * turn] * left[column]
                            for column in columns
                        ]
                    )
                else:
                    begun = source(row)
                    for column in columns:
                        outer_ref[side * FAR + index - 1, column] = begun[column] - left[column]
            ends, rest = new_ends, new_rest[1]

    def middle(row, column):
        index = min(row, total - 1 - row)
        if index < HALO + FAR:
            return outer_ref[FAR * (row > index) + index - HALO, column]
        return middle_ref[row, column]

    sums = [early_ref[0], early_ref[1]] + [jnp.zeros((SUB, LANES), jnp.float32) for _ in range(2)]

    def emit(row, begun, solved, applied):
        for column in columns:
            solved_ref[row - own[0], column] = solved[column]
            applied_ref[row - own[0], column] = applied[column]
        add_products(sums, 2, begun, solved)
        add_products(sums, 3, solved, applied)

    passes(HALO, own, total, middle, weight, coef, step_ref, remain_ref, part_ref, emit)

    lane = lane_index((1, LANES))
    line = jnp.zeros((1, LANES), jnp.float32)
    for index in range(4):
        line = jnp.where(lane == index, jnp.sum(sums[index]), line)
    sums_ref[...] = jnp.broadcast_to(line[None], sums_ref.shape)


def inverse_kernel(
    rows, times, length, cas_ref, sums_ref, one_ref, two_ref, three_ref, four_ref, out_ref, line_ref
):
    half = LANES // 2
    span = half + 2 * SIDE
    skip = (span - WINDOW) // 2
    line = jnp.sum(sums_ref[...].reshape(sums_ref.shape[0], LANES), axis=0, keepdims=True)
    gamma, curved, cross, last = (
        jnp.broadcast_to(line[:, index : index + 1], (SUB, LANES)) for index in range(4)
    )
    step = gamma / curved
    gamma_next = step * step * cross - gamma
    turn = gamma_next / gamma
    grown = 1.0 + turn
    next_curved = grown * grown * curved - 2.0 * step * grown * cross + step * step * last
    next_step = gamma_next / next_curved
    first = step + next_step * grown
    second = -next_step * step
    for row in range(rows):
        for index, (left_ref, right_ref) in enumerate(((one_ref, two_ref), (three_ref, four_ref))):
            offset = left_ref.shape[0] // 2 - rows // 2
            for column in range(BLOCK):
                start = (2 * row + index) * span + skip + column
                value = first * left_ref[offset + row, column] + second * right_ref[row, column]
                line_ref[pl.ds(start, SUB, stride=BLOCK), :] = value
    for row in range(rows):
        start = 2 * row * span + SIDE
        points = jnp.concatenate(
            [line_ref[start : start + half, :], line_ref[start + span : start + span + half, :]],
            axis=0,
        )
        back = exact_dot(cas_ref[...], points, 1, 1).reshape(length // times, times, LANES)
        out_ref[:, row * times : (row + 1) * times, :] = back


def final_kernel(rows, times, tiles, source_ref, field_ref, solution_ref, residual_ref):
    half = LANES // 2
    low = lane_index((rows, LANES)) < half
    for time in range(times):
        place = slice(time * rows, (time + 1) * rows)
        taken = pl.ds(time, rows, stride=times)
        for pair in range(tiles // 2):
            columns = slice(pair * LANES, (pair + 1) * LANES)
            left = source_ref[2 * pair, taken, :]
            right = source_ref[2 * pair + 1, taken, :]
            solution_ref[place, columns] = jnp.where(low, left, pltpu.roll(right, half, 1))
            change = jnp.where(low, pltpu.roll(left, half, 1), right)
            residual_ref[place, columns] = field_ref[place, columns] - change


def call(kernel, out_shape, scratch=()):
    shapes = [jax.ShapeDtypeStruct(shape, jnp.float32) for shape in out_shape]
    return pl.pallas_call(
        kernel,
        out_shape=shapes[0] if len(shapes) == 1 else shapes,
        scratch_shapes=[pltpu.VMEM(shape, jnp.float32) for shape in scratch],
        compiler_params=PARAMS,
    )


def shift(value, distance, spaces):
    return lax.ppermute(value, "space", [(i, (i + distance) % spaces) for i in range(spaces)])


def shards(right_side, kappa, velocity):
    tiles = lax.axis_size("tm")
    spaces = lax.axis_size("space")
    times, rows, width = right_side.shape
    length = times * tiles
    tile = width // tiles
    around = (LANES - tile) // 2
    cas_table = jnp.asarray(hartley_table(length))
    coef_table = jnp.asarray(chebyshev_table(length))

    field = right_side.reshape(times * rows, width)
    windows = call(
        functools.partial(window_kernel, rows, times, tiles),
        [(tiles, 6 * times, LANES)],
        [(width // LANES, times * rows, LANES)],
    )(field)
    gathered = lax.all_to_all(windows, "tm", 0, 0)

    squares = velocity.astype(jnp.float32) ** 2
    planes = jnp.concatenate([kappa, squares[0], squares[1]], axis=0)
    planes = jnp.concatenate([planes[:, -around:], planes, planes[:, :around]], axis=1)
    local = lax.dynamic_slice_in_dim(planes, lax.axis_index("tm") * tile, LANES, 1)
    total = 3 * rows + 2 * FAR
    tile_shape = (rows, BLOCK, SUB, LANES)
    row_shape = (rows * BLOCK + 3, SUB, LANES)
    far_shape = (FAR * BLOCK + 3, SUB, LANES)
    span = LANES // 2 + 2 * SIDE
    freq, low, high = call(
        functools.partial(forward_kernel, rows, times, length),
        [row_shape, far_shape, far_shape],
        [(rows * span, LANES)],
    )(cas_table, gathered, local)
    top, bottom = shift(freq, 1, spaces), shift(freq, -1, spaces)
    top_far, bottom_far = shift(high, 2, spaces), shift(low, -2, spaces)

    groups = [
        [i * spaces + first + j for i in range(tiles) for j in range(NEAR)]
        for first in range(0, spaces, NEAR)
    ]
    work = (total, BLOCK, SUB, LANES)
    solved, middle, step, remain, border, wide, early = call(
        functools.partial(near_kernel, rows),
        [
            tile_shape,
            work,
            work,
            work,
            (2, CHEB + 1, BLOCK, SUB, LANES),
            (total, 3 * BLOCK, SUB, LANES),
            (2, SUB, LANES),
        ],
        [tile_shape, (LANES, LANES)],
    )(bottom, freq, top, coef_table)
    solved_two, applied_two, sums = call(
        functools.partial(far_kernel, rows),
        [tile_shape, tile_shape, (tiles * NEAR, 1, LANES)],
        [work, work, tile_shape, (2 * FAR, BLOCK, SUB, LANES), (LANES, LANES)],
    )(
        top_far, top, freq, bottom, bottom_far, coef_table, middle, step, remain, border, wide, early
    )
    sums = lax.all_to_all(sums, ("tm", "space"), 0, 0, axis_index_groups=groups)
    planes = spaces // NEAR
    groups = [[first + NEAR * i for i in range(planes)] for first in range(NEAR)]
    sums = jnp.broadcast_to(jnp.sum(sums, axis=0)[None], (planes, 1, LANES))
    sums = lax.all_to_all(sums, "space", 0, 0, axis_index_groups=groups)
    packed = call(
        functools.partial(inverse_kernel, rows, times, length),
        [(tiles, rows * times, LANES)],
        [(rows * 2 * span, LANES)],
    )(cas_table, sums, solved, solved_two, middle, applied_two)
    returned = lax.all_to_all(packed, "tm", 0, 0)

    solution, residual = call(
        functools.partial(final_kernel, rows, times, tiles),
        [(times * rows, width), (times * rows, width)],
    )(returned, field)
    shape = right_side.shape
    return solution.reshape(shape), residual.reshape(shape)


def solution(mesh):
    placed = (P("tm", "space", None), P("space", None), P(None, "space", None))
    return jax.shard_map(
        shards,
        mesh=mesh,
        in_specs=placed,
        out_specs=(P("tm", "space", None), P("tm", "space", None)),
        check_vma=False,
    )
```

```python
import functools
import math

import jax
import jax.numpy as jnp
import numpy as np
from jax import lax
from jax.experimental import pallas as pl
from jax.experimental.pallas import tpu as pltpu
from jax.sharding import PartitionSpec as P

CHEB = 4
COUPLING = 2.0
KAPPA_LOW = 0.05
KAPPA_HIGH = 1.0
REACH = 16.0

LANES = 128
SUB = 8
HALO = CHEB + 1
FAR = 2
SIDE = 16
BLOCK = 11
WINDOW = SUB * BLOCK
NEAR = 4
PARAMS = pltpu.CompilerParams(vmem_limit_bytes=24 * 1024 * 1024)


def hartley_table(length):
    index = np.arange(length)
    angle = (index[:, None] * index[None, :] % length) * (2.0 * math.pi / length)
    return ((np.cos(angle) + np.sin(angle)) / math.sqrt(length)).astype(np.float32)


def chebyshev_table(length):
    shift = COUPLING * (2.0 - 2.0 * np.cos(2.0 * math.pi * np.arange(length) / length))
    half = 0.5 * (KAPPA_HIGH + REACH - KAPPA_LOW)
    mid = 0.5 * (KAPPA_LOW + KAPPA_HIGH + REACH) + shift
    ratio = mid / half
    damp = 1.0 / ratio
    lines = [shift, 1.0 / mid]
    for _ in range(CHEB):
        damp_next = 1.0 / (2.0 * ratio - damp)
        lines += [damp_next * damp, 2.0 * damp_next / half]
        damp = damp_next
    return np.repeat(np.stack(lines).astype(np.float32)[:, None], SUB, 1)


def lane_index(shape):
    return lax.broadcasted_iota(jnp.int32, shape, len(shape) - 1)


def exact_dot(left, right, left_dim, right_dim):
    return lax.dot_general(
        left,
        right,
        (((left_dim,), (right_dim,)), ((), ())),
        precision=lax.Precision.HIGHEST,
        preferred_element_type=jnp.float32,
    )


def window_kernel(rows, times, tiles, source_ref, out_ref, scratch_ref):
    half = LANES // 2
    parts = source_ref.shape[1] // LANES
    for part in range(parts):
        scratch_ref[part] = source_ref[:, part * LANES : (part + 1) * LANES]
    lane = lane_index((times, LANES))
    fields = [
        [scratch_ref[part, pl.ds(row, times, stride=rows), :] for part in range(parts)]
        for row in range(rows)
    ]
    for pair in range(rows // 2):
        for part in range(parts):
            one, two = fields[2 * pair][part], fields[2 * pair + 1][part]
            place = slice(pair * times, (pair + 1) * times)
            out_ref[2 * part, place, :] = jnp.where(lane < half, one, pltpu.roll(two, half, 1))
            out_ref[2 * part + 1, place, :] = jnp.where(lane < half, pltpu.roll(one, half, 1), two)
    spread = 2 * SIDE
    group = LANES // spread
    for quad in range(rows // group):
        even = [None] * parts
        odd = [None] * parts
        for index in range(group):
            row = quad * group + index
            wide = jnp.concatenate(fields[row], axis=1)
            near = pltpu.roll(wide, spread * index + SIDE, 1)
            away = pltpu.roll(wide, (spread * index - half + SIDE) % wide.shape[1], 1)
            left = (lane >= spread * index) & (lane < spread * index + SIDE)
            right = (lane >= spread * index + SIDE) & (lane < spread * (index + 1))
            for part in range(parts):
                here = slice(part * LANES, (part + 1) * LANES)
                then = (part + 1) % parts
                then = slice(then * LANES, (then + 1) * LANES)
                if index == 0:
                    even[part] = jnp.where(left, near[:, here], away[:, here])
                    odd[part] = jnp.where(left, away[:, here], near[:, then])
                else:
                    even[part] = jnp.where(
                        left, near[:, here], jnp.where(right, away[:, here], even[part])
                    )
                    odd[part] = jnp.where(
                        left, away[:, here], jnp.where(right, near[:, then], odd[part])
                    )
        start = (rows // 2 + quad) * times
        for part in range(parts):
            out_ref[2 * part, start : start + times, :] = even[part]
            out_ref[2 * part + 1, start : start + times, :] = odd[part]


def forward_kernel(
    rows, times, length, cas_ref, field_ref, local_ref, out_ref, low_ref, high_ref, line_ref
):
    half = LANES // 2
    span = half + 2 * SIDE
    pieces = field_ref.shape[1] // times
    group = LANES // (2 * SIDE)
    for piece in range(pieces):
        block = field_ref[:, piece * times : (piece + 1) * times, :].reshape(length, LANES)
        freq = exact_dot(block, cas_ref[...], 0, 0)
        if piece < rows // 2:
            for part in range(2):
                start = (2 * piece + part) * span + SIDE
                line_ref[start : start + half, :] = freq[part * half : (part + 1) * half]
        else:
            for index in range(group):
                start = ((piece - rows // 2) * group + index) * span
                place = 2 * SIDE * index
                line_ref[start : start + SIDE, :] = freq[place : place + SIDE]
                line_ref[start + SIDE + half : start + span, :] = freq[
                    place + SIDE : place + 2 * SIDE
                ]
    skip = (span - WINDOW) // 2
    for row in range(rows):
        for column in range(BLOCK):
            value = line_ref[pl.ds(row * span + skip + column, SUB, stride=BLOCK), :]
            out_ref[row * BLOCK + column] = value
            if row < FAR:
                low_ref[row * BLOCK + column] = value
            if row >= rows - FAR:
                high_ref[(row - (rows - FAR)) * BLOCK + column] = value
    for ref in (out_ref, low_ref, high_ref):
        first = ref.shape[0] - 3
        for plane in range(3):
            ref[first + plane] = local_ref[plane * rows : (plane + 1) * rows, :]


def weight_lines(parts, scratch_ref):
    planes = [jnp.concatenate(blocks, axis=0) for blocks in zip(*parts)]
    east = 1.0 + 0.125 * (planes[1] + jnp.concatenate([planes[1][1:], planes[1][:1]], axis=0))
    north = 1.0 + 0.125 * (planes[2] + pltpu.roll(planes[2], LANES - 1, 1))
    zero = jnp.zeros((LANES - 3 * planes[0].shape[0], LANES), jnp.float32)
    scratch_ref[...] = jnp.transpose(jnp.concatenate([planes[0], east, north, zero], axis=0))
    skip = (LANES - WINDOW) // 2
    return [scratch_ref[pl.ds(skip + column, SUB, stride=BLOCK), :] for column in range(BLOCK)]


def weight_part(ref):
    return [ref[ref.shape[0] - 3 + plane] for plane in range(3)]


def spread(lines, index, plane, coef):
    value = jnp.broadcast_to(lines[:, index : index + 1], (SUB, LANES))
    return value + coef[0] if plane == 0 else value


def own_columns(column):
    place = lax.broadcasted_iota(jnp.int32, (SUB, LANES), 0) * BLOCK + column
    first = (WINDOW - LANES // 2) // 2
    return (place >= first) & (place < first + LANES // 2)


def stencil(weight, row, above, here, below, flux=None):
    columns = range(BLOCK)
    if flux is None:
        flux = [weight(1, row - 1, column) * (above[column] - here[column]) for column in columns]
    ahead = [weight(1, row, column) * (here[column] - below[column]) for column in columns]
    beside = here[1:] + [pltpu.roll(here[0], SUB - 1, 0)]
    side = [weight(2, row, column) * (here[column] - beside[column]) for column in columns]
    behind = [pltpu.roll(side[-1], 1, 0)] + side[:-1]
    applied = [
        weight(0, row, column) * here[column]
        + (ahead[column] - flux[column])
        + (side[column] - behind[column])
        for column in columns
    ]
    return applied, ahead


def passes(
    edge, own, total, source, weight, coef, step_ref, remain_ref, solved_ref, emit, border=None
):
    columns = range(BLOCK)

    for turn in range(CHEB + 1):
        first, last = edge + turn + 1, total - edge - turn - 1

        def load(row, turn=turn):
            if turn == 0:
                return [coef[1] * source(row, column) for column in columns]
            return [step_ref[row, column] for column in columns]

        above, here = load(first - 1), load(first)
        flux = None
        for row in range(first, last):
            below = load(row + 1)
            if border and row == first:
                border(0, turn, here)
            if border and row == last - 1:
                border(1, turn, here)
            applied, flux = stencil(weight, row, above, here, below, flux)
            inside = row in range(*own)
            results = []
            for column in columns:
                before = source(row, column) if turn == 0 else remain_ref[row, column]
                left = before - applied[column]
                if turn < CHEB:
                    remain_ref[row, column] = left
                    step_ref[row, column] = (
                        coef[2 + 2 * turn] * here[column] + coef[3 + 2 * turn] * left
                    )
                solved = None
                if inside:
                    place = row - own[0]
                    solved = here[column]
                    if turn > 0:
                        solved = solved_ref[place, column] + solved
                    if turn < CHEB:
                        solved_ref[place, column] = solved
                if turn == CHEB:
                    begun = source(row, column)
                    results.append((begun, solved, begun - left))
            if turn == CHEB:
                emit(row, *zip(*results))
            above, here = here, below


def add_products(sums, index, one, two):
    for column in range(BLOCK):
        product = one[column] * two[column]
        sums[index] = sums[index] + jnp.where(own_columns(column), product, 0.0)


def near_kernel(
    rows, bottom_ref, field_ref, top_ref, coef_ref,
    solved_ref, middle_ref, step_ref, remain_ref, border_ref, wide_ref, early_ref,
    part_ref, scratch_ref,
):
    refs = (top_ref, field_ref, bottom_ref)
    lines = weight_lines([weight_part(ref) for ref in refs], scratch_ref)
    coef = [coef_ref[index] for index in range(2 + 2 * CHEB)]
    places = [None] * FAR + [(ref, row) for ref in refs for row in range(rows)]
    total = 3 * rows + 2 * FAR
    own = (FAR + rows, FAR + 2 * rows)
    made = set()

    def weight(plane, row, column):
        place = plane * BLOCK + column
        if (row, place) not in made:
            made.add((row, place))
            wide_ref[row, place] = spread(lines[column], plane * 3 * rows + row - FAR, plane, coef)
        return wide_ref[row, place]

    def source(row, column):
        ref, place = places[row]
        return ref[place * BLOCK + column]

    sums = [jnp.zeros((SUB, LANES), jnp.float32) for _ in range(2)]

    def emit(row, begun, solved, applied):
        for column in range(BLOCK):
            middle_ref[row, column] = applied[column]
        if row in range(*own):
            for column in range(BLOCK):
                solved_ref[row - own[0], column] = solved[column]
            add_products(sums, 0, begun, solved)
            add_products(sums, 1, solved, applied)

    def border(side, turn, step):
        for column in range(BLOCK):
            border_ref[side, turn, column] = step[column]

    passes(
        FAR, own, total, source, weight, coef, step_ref, remain_ref, part_ref, emit, border
    )
    early_ref[0] = sums[0]
    early_ref[1] = sums[1]


def far_kernel(
    rows, top_far_ref, bottom_ref, field_ref, top_ref, bottom_far_ref, coef_ref,
    middle_ref, frozen_step_ref, frozen_remain_ref, border_ref, wide_ref, early_ref,
    solved_ref, applied_ref, sums_ref,
    step_ref, remain_ref, part_ref, outer_ref, scratch_ref,
):
    columns = range(BLOCK)
    refs = (top_far_ref, top_ref, field_ref, bottom_ref, bottom_far_ref)
    parts = [weight_part(ref) for ref in refs]
    parts[0] = [block[rows - FAR :] for block in parts[0]]
    parts[-1] = [block[:FAR] for block in parts[-1]]
    lines = weight_lines(parts, scratch_ref)
    coef = [coef_ref[index] for index in range(2 + 2 * CHEB)]
    total = 3 * rows + 2 * FAR
    own = (FAR + rows, FAR + 2 * rows)
    places = [
        (ref, row) for ref in refs for row in range((ref.shape[0] - 3) // BLOCK)
    ]
    made = {}

    def weight(plane, row, column):
        if FAR < row < total - FAR - 1 or (plane == 1 and row == FAR):
            return wide_ref[row, plane * BLOCK + column]
        key = (plane, row, column)
        if key not in made:
            made[key] = spread(lines[column], plane * total + row, plane, coef)
        return made[key]

    def source(row):
        ref, place = places[row]
        return [ref[place * BLOCK + column] for column in columns]

    for side in range(2):

        def at(index, side=side):
            return total - 1 - index if side else index

        ends = [[coef[1] * value for value in source(at(index))] for index in range(FAR)]
        rest = source(at(1))
        for turn in range(CHEB + 1):
            edge_row = at(turn + 2)
            if turn == 0:
                inner = [coef[1] * value for value in source(edge_row)]
                inner_rest = source(edge_row)
            else:
                inner = [frozen_step_ref[edge_row, column] for column in columns]
                inner_rest = [frozen_remain_ref[edge_row, column] for column in columns]
            steps = ends + [inner, [border_ref[side, turn, column] for column in columns]]
            new_ends, new_rest = [], []
            for index, before in ((1, rest), (2, inner_rest)):
                row = at(turn + index)
                near, away = steps[index - 1], steps[index + 1]
                above, below = (away, near) if side else (near, away)
                here = steps[index]
                applied, _ = stencil(weight, row, above, here, below)
                left = [before[column] - applied[column] for column in columns]
                new_rest.append(left)
                if turn < CHEB:
                    new_ends.append(
                        [
                            coef[2 + 2 * turn] * here[column] + coef[3 + 2 * turn] * left[column]
                            for column in columns
                        ]
                    )
                else:
                    begun = source(row)
                    for column in columns:
                        outer_ref[side * FAR + index - 1, column] = begun[column] - left[column]
            ends, rest = new_ends, new_rest[1]

    def middle(row, column):
        index = min(row, total - 1 - row)
        if index < HALO + FAR:
            return outer_ref[FAR * (row > index) + index - HALO, column]
        return middle_ref[row, column]

    sums = [early_ref[0], early_ref[1]] + [jnp.zeros((SUB, LANES), jnp.float32) for _ in range(2)]

    def emit(row, begun, solved, applied):
        for column in columns:
            solved_ref[row - own[0], column] = solved[column]
            applied_ref[row - own[0], column] = applied[column]
        add_products(sums, 2, begun, solved)
        add_products(sums, 3, solved, applied)

    passes(HALO, own, total, middle, weight, coef, step_ref, remain_ref, part_ref, emit)

    lane = lane_index((1, LANES))
    line = jnp.zeros((1, LANES), jnp.float32)
    for index in range(4):
        line = jnp.where(lane == index, jnp.sum(sums[index]), line)
    sums_ref[...] = jnp.broadcast_to(line[None], sums_ref.shape)


def inverse_kernel(
    rows, times, length, cas_ref, sums_ref, one_ref, two_ref, three_ref, four_ref, out_ref, line_ref
):
    half = LANES // 2
    span = half + 2 * SIDE
    skip = (span - WINDOW) // 2
    line = jnp.sum(sums_ref[...].reshape(sums_ref.shape[0], LANES), axis=0, keepdims=True)
    gamma, curved, cross, last = (
        jnp.broadcast_to(line[:, index : index + 1], (SUB, LANES)) for index in range(4)
    )
    step = gamma / curved
    gamma_next = step * step * cross - gamma
    turn = gamma_next / gamma
    grown = 1.0 + turn
    next_curved = grown * grown * curved - 2.0 * step * grown * cross + step * step * last
    next_step = gamma_next / next_curved
    first = step + next_step * grown
    second = -next_step * step
    for row in range(rows):
        for index, (left_ref, right_ref) in enumerate(((one_ref, two_ref), (three_ref, four_ref))):
            offset = left_ref.shape[0] // 2 - rows // 2
            for column in range(BLOCK):
                start = (2 * row + index) * span + skip + column
                value = first * left_ref[offset + row, column] + second * right_ref[row, column]
                line_ref[pl.ds(start, SUB, stride=BLOCK), :] = value
    for row in range(rows):
        start = 2 * row * span + SIDE
        points = jnp.concatenate(
            [line_ref[start : start + half, :], line_ref[start + span : start + span + half, :]],
            axis=0,
        )
        back = exact_dot(cas_ref[...], points, 1, 1).reshape(length // times, times, LANES)
        out_ref[:, row * times : (row + 1) * times, :] = back


def final_kernel(rows, times, tiles, source_ref, field_ref, solution_ref, residual_ref):
    half = LANES // 2
    low = lane_index((rows, LANES)) < half
    for time in range(times):
        place = slice(time * rows, (time + 1) * rows)
        taken = pl.ds(time, rows, stride=times)
        for pair in range(tiles // 2):
            columns = slice(pair * LANES, (pair + 1) * LANES)
            left = source_ref[2 * pair, taken, :]
            right = source_ref[2 * pair + 1, taken, :]
            solution_ref[place, columns] = jnp.where(low, left, pltpu.roll(right, half, 1))
            change = jnp.where(low, pltpu.roll(left, half, 1), right)
            residual_ref[place, columns] = field_ref[place, columns] - change


def call(kernel, out_shape, scratch=()):
    shapes = [jax.ShapeDtypeStruct(shape, jnp.float32) for shape in out_shape]
    return pl.pallas_call(
        kernel,
        out_shape=shapes[0] if len(shapes) == 1 else shapes,
        scratch_shapes=[pltpu.VMEM(shape, jnp.float32) for shape in scratch],
        compiler_params=PARAMS,
    )


def shift(value, distance, spaces):
    return lax.ppermute(value, "space", [(i, (i + distance) % spaces) for i in range(spaces)])


def shards(right_side, kappa, velocity):
    tiles = lax.axis_size("tm")
    spaces = lax.axis_size("space")
    times, rows, width = right_side.shape
    length = times * tiles
    tile = width // tiles
    around = (LANES - tile) // 2
    cas_table = jnp.asarray(hartley_table(length))
    coef_table = jnp.asarray(chebyshev_table(length))

    field = right_side.reshape(times * rows, width)
    windows = call(
        functools.partial(window_kernel, rows, times, tiles),
        [(tiles, 6 * times, LANES)],
        [(width // LANES, times * rows, LANES)],
    )(field)
    gathered = lax.all_to_all(windows, "tm", 0, 0)

    squares = velocity.astype(jnp.float32) ** 2
    planes = jnp.concatenate([kappa, squares[0], squares[1]], axis=0)
    planes = jnp.concatenate([planes[:, -around:], planes, planes[:, :around]], axis=1)
    local = lax.dynamic_slice_in_dim(planes, lax.axis_index("tm") * tile, LANES, 1)
    total = 3 * rows + 2 * FAR
    tile_shape = (rows, BLOCK, SUB, LANES)
    row_shape = (rows * BLOCK + 3, SUB, LANES)
    far_shape = (FAR * BLOCK + 3, SUB, LANES)
    span = LANES // 2 + 2 * SIDE
    freq, low, high = call(
        functools.partial(forward_kernel, rows, times, length),
        [row_shape, far_shape, far_shape],
        [(rows * span, LANES)],
    )(cas_table, gathered, local)
    top, bottom = shift(freq, 1, spaces), shift(freq, -1, spaces)
    top_far, bottom_far = shift(high, 2, spaces), shift(low, -2, spaces)

    groups = [
        [i * spaces + first + j for i in range(tiles) for j in range(NEAR)]
        for first in range(0, spaces, NEAR)
    ]
    work = (total, BLOCK, SUB, LANES)
    solved, middle, step, remain, border, wide, early = call(
        functools.partial(near_kernel, rows),
        [
            tile_shape,
            work,
            work,
            work,
            (2, CHEB + 1, BLOCK, SUB, LANES),
            (total, 3 * BLOCK, SUB, LANES),
            (2, SUB, LANES),
        ],
        [tile_shape, (LANES, LANES)],
    )(bottom, freq, top, coef_table)
    solved_two, applied_two, sums = call(
        functools.partial(far_kernel, rows),
        [tile_shape, tile_shape, (tiles * NEAR, 1, LANES)],
        [work, work, tile_shape, (2 * FAR, BLOCK, SUB, LANES), (LANES, LANES)],
    )(
        top_far, bottom, freq, top, bottom_far, coef_table, middle, step, remain, border, wide, early
    )
    sums = lax.all_to_all(sums, ("tm", "space"), 0, 0, axis_index_groups=groups)
    planes = spaces // NEAR
    groups = [[first + NEAR * i for i in range(planes)] for first in range(NEAR)]
    sums = jnp.broadcast_to(jnp.sum(sums, axis=0)[None], (planes, 1, LANES))
    sums = lax.all_to_all(sums, "space", 0, 0, axis_index_groups=groups)
    packed = call(
        functools.partial(inverse_kernel, rows, times, length),
        [(tiles, rows * times, LANES)],
        [(rows * 2 * span, LANES)],
    )(cas_table, sums, solved, solved_two, middle, applied_two)
    returned = lax.all_to_all(packed, "tm", 0, 0)

    solution, residual = call(
        functools.partial(final_kernel, rows, times, tiles),
        [(times * rows, width), (times * rows, width)],
    )(returned, field)
    shape = right_side.shape
    return solution.reshape(shape), residual.reshape(shape)


def solution(mesh):
    placed = (P("tm", "space", None), P("space", None), P(None, "space", None))
    return jax.shard_map(
        shards,
        mesh=mesh,
        in_specs=placed,
        out_specs=(P("tm", "space", None), P("tm", "space", None)),
        check_vma=False,
    )
```

```python
import functools
import math

import jax
import jax.numpy as jnp
import numpy as np
from jax import lax
from jax.experimental import pallas as pl
from jax.experimental.pallas import tpu as pltpu
from jax.sharding import PartitionSpec as P

CHEB = 4
COUPLING = 2.0
KAPPA_LOW = 0.05
KAPPA_HIGH = 1.0
REACH = 16.0

LANES = 128
SUB = 8
HALO = CHEB + 1
FAR = 2
SIDE = 16
BLOCK = 11
WINDOW = SUB * BLOCK
NEAR = 4
PARAMS = pltpu.CompilerParams(vmem_limit_bytes=24 * 1024 * 1024)


def hartley_table(length):
    index = np.arange(length)
    angle = (index[:, None] * index[None, :] % length) * (2.0 * math.pi / length)
    return ((np.cos(angle) + np.sin(angle)) / math.sqrt(length)).astype(np.float32)


def chebyshev_table(length):
    shift = COUPLING * (2.0 - 2.0 * np.cos(2.0 * math.pi * np.arange(length) / length))
    half = 0.5 * (KAPPA_HIGH + REACH - KAPPA_LOW)
    mid = 0.5 * (KAPPA_LOW + KAPPA_HIGH + REACH) + shift
    ratio = mid / half
    damp = 1.0 / ratio
    lines = [shift, 1.0 / mid]
    for _ in range(CHEB):
        damp_next = 1.0 / (2.0 * ratio - damp)
        lines += [damp_next * damp, 2.0 * damp_next / half]
        damp = damp_next
    return np.repeat(np.stack(lines).astype(np.float32)[:, None], SUB, 1)


def lane_index(shape):
    return lax.broadcasted_iota(jnp.int32, shape, len(shape) - 1)


def exact_dot(left, right, left_dim, right_dim):
    return lax.dot_general(
        left,
        right,
        (((left_dim,), (right_dim,)), ((), ())),
        precision=lax.Precision.HIGHEST,
        preferred_element_type=jnp.float32,
    )


def window_kernel(rows, times, tiles, source_ref, out_ref, scratch_ref):
    half = LANES // 2
    parts = source_ref.shape[1] // LANES
    for part in range(parts):
        scratch_ref[part] = source_ref[:, part * LANES : (part + 1) * LANES]
    lane = lane_index((times, LANES))
    fields = [
        [scratch_ref[part, pl.ds(row, times, stride=rows), :] for part in range(parts)]
        for row in range(rows)
    ]
    for pair in range(rows // 2):
        for part in range(parts):
            one, two = fields[2 * pair][part], fields[2 * pair + 1][part]
            place = slice(pair * times, (pair + 1) * times)
            out_ref[2 * part, place, :] = jnp.where(lane < half, one, pltpu.roll(two, half, 1))
            out_ref[2 * part + 1, place, :] = jnp.where(lane < half, pltpu.roll(one, half, 1), two)
    spread = 2 * SIDE
    group = LANES // spread
    for quad in range(rows // group):
        even = [None] * parts
        odd = [None] * parts
        for index in range(group):
            row = quad * group + index
            wide = jnp.concatenate(fields[row], axis=1)
            near = pltpu.roll(wide, spread * index + SIDE, 1)
            away = pltpu.roll(wide, (spread * index - half + SIDE) % wide.shape[1], 1)
            left = (lane >= spread * index) & (lane < spread * index + SIDE)
            right = (lane >= spread * index + SIDE) & (lane < spread * (index + 1))
            for part in range(parts):
                here = slice(part * LANES, (part + 1) * LANES)
                then = (part + 1) % parts
                then = slice(then * LANES, (then + 1) * LANES)
                if index == 0:
                    even[part] = jnp.where(left, near[:, here], away[:, here])
                    odd[part] = jnp.where(left, away[:, here], near[:, then])
                else:
                    even[part] = jnp.where(
                        left, near[:, here], jnp.where(right, away[:, here], even[part])
                    )
                    odd[part] = jnp.where(
                        left, away[:, here], jnp.where(right, near[:, then], odd[part])
                    )
        start = (rows // 2 + quad) * times
        for part in range(parts):
            out_ref[2 * part, start : start + times, :] = even[part]
            out_ref[2 * part + 1, start : start + times, :] = odd[part]


def forward_kernel(
    rows, times, length, cas_ref, field_ref, local_ref, out_ref, low_ref, high_ref, line_ref
):
    half = LANES // 2
    span = half + 2 * SIDE
    pieces = field_ref.shape[1] // times
    group = LANES // (2 * SIDE)
    for piece in range(pieces):
        block = field_ref[:, piece * times : (piece + 1) * times, :].reshape(length, LANES)
        freq = exact_dot(block, cas_ref[...], 0, 0)
        if piece < rows // 2:
            for part in range(2):
                start = (2 * piece + part) * span + SIDE
                line_ref[start : start + half, :] = freq[part * half : (part + 1) * half]
        else:
            for index in range(group):
                start = ((piece - rows // 2) * group + index) * span
                place = 2 * SIDE * index
                line_ref[start : start + SIDE, :] = freq[place : place + SIDE]
                line_ref[start + SIDE + half : start + span, :] = freq[
                    place + SIDE : place + 2 * SIDE
                ]
    skip = (span - WINDOW) // 2
    for row in range(rows):
        for column in range(BLOCK):
            value = line_ref[pl.ds(row * span + skip + column, SUB, stride=BLOCK), :]
            out_ref[row * BLOCK + column] = value
            if row < FAR:
                low_ref[row * BLOCK + column] = value
            if row >= rows - FAR:
                high_ref[(row - (rows - FAR)) * BLOCK + column] = value
    for ref in (out_ref, low_ref, high_ref):
        first = ref.shape[0] - 3
        for plane in range(3):
            ref[first + plane] = local_ref[plane * rows : (plane + 1) * rows, :]


def weight_lines(rows, refs, scratch_ref):
    planes = []
    for plane in range(3):
        blocks = [ref[ref.shape[0] - 3 + plane] for ref in refs]
        blocks[0] = blocks[0][rows - FAR :]
        blocks[-1] = blocks[-1][:FAR]
        planes.append(jnp.concatenate(blocks, axis=0))
    east = 1.0 + 0.125 * (planes[1] + jnp.concatenate([planes[1][1:], planes[1][:1]], axis=0))
    north = 1.0 + 0.125 * (planes[2] + pltpu.roll(planes[2], LANES - 1, 1))
    total = planes[0].shape[0]
    zero = jnp.zeros((LANES - 3 * total, LANES), jnp.float32)
    scratch_ref[...] = jnp.transpose(jnp.concatenate([planes[0], east, north, zero], axis=0))
    skip = (LANES - WINDOW) // 2
    return [scratch_ref[pl.ds(skip + column, SUB, stride=BLOCK), :] for column in range(BLOCK)]


def own_columns(column):
    place = lax.broadcasted_iota(jnp.int32, (SUB, LANES), 0) * BLOCK + column
    first = (WINDOW - LANES // 2) // 2
    return (place >= first) & (place < first + LANES // 2)


def passes(edge, own, total, source, weight, coef, step_ref, remain_ref, solved_ref, emit):
    columns = range(BLOCK)

    for turn in range(CHEB + 1):
        first, last = edge + turn + 1, total - edge - turn - 1

        def load(row, turn=turn):
            if turn == 0:
                return [coef[1] * source(row, column) for column in columns]
            return [step_ref[row, column] for column in columns]

        here = load(first - 1)
        flux = None
        for row in range(first - 1, last):
            after = load(row + 1)
            ahead = [weight(1, row, column) * (here[column] - after[column]) for column in columns]
            if row >= first:
                beside = here[1:] + [pltpu.roll(here[0], SUB - 1, 0)]
                side = [weight(2, row, column) * (here[column] - beside[column]) for column in columns]
                behind = [pltpu.roll(side[-1], 1, 0)] + side[:-1]
                inside = row in range(*own)
                results = []
                for column in columns:
                    applied = (
                        weight(0, row, column) * here[column]
                        + (ahead[column] - flux[column])
                        + (side[column] - behind[column])
                    )
                    before = source(row, column) if turn == 0 else remain_ref[row, column]
                    left = before - applied
                    if turn < CHEB:
                        remain_ref[row, column] = left
                        step_ref[row, column] = (
                            coef[2 + 2 * turn] * here[column] + coef[3 + 2 * turn] * left
                        )
                    solved = None
                    if inside:
                        place = row - own[0]
                        solved = here[column]
                        if turn > 0:
                            solved = solved_ref[place, column] + solved
                        if turn < CHEB:
                            solved_ref[place, column] = solved
                    if turn == CHEB:
                        begun = source(row, column)
                        results.append((begun, solved, begun - left))
                if turn == CHEB:
                    emit(row, *zip(*results))
            here, flux = after, ahead


def stencil_kernel(
    rows, top_far_ref, bottom_ref, field_ref, top_ref, bottom_far_ref, coef_ref,
    solved_ref, applied_ref, solved_two_ref, applied_two_ref, sums_ref,
    step_ref, remain_ref, part_ref, middle_ref, wide_ref, scratch_ref,
):
    columns = range(BLOCK)
    refs = (top_far_ref, top_ref, field_ref, bottom_ref, bottom_far_ref)
    lines = weight_lines(rows, refs, scratch_ref)
    coef = [coef_ref[index] for index in range(2 + 2 * CHEB)]
    places = [
        (ref, row) for ref in refs for row in range((ref.shape[0] - 3) // BLOCK)
    ]
    total = len(places)
    own = (FAR + rows, FAR + 2 * rows)
    made = set()

    def weight(plane, row, column):
        place = plane * BLOCK + column
        if (row, place) in made:
            return wide_ref[row, place]
        index = plane * total + row
        value = jnp.broadcast_to(lines[column][:, index : index + 1], (SUB, LANES))
        if plane == 0:
            value = value + coef[0]
        wide_ref[row, place] = value
        made.add((row, place))
        return value

    def first_source(row, column):
        ref, place = places[row]
        return ref[place * BLOCK + column]

    def second_source(row, column):
        return middle_ref[row, column]

    sums = [jnp.zeros((SUB, LANES), jnp.float32) for _ in range(4)]

    def add(index, one, two):
        for column in columns:
            product = one[column] * two[column]
            sums[index] = sums[index] + jnp.where(own_columns(column), product, 0.0)

    def emit_first(row, source, solved, applied):
        for column in columns:
            middle_ref[row, column] = applied[column]
        if row in range(*own):
            for column in columns:
                solved_ref[row - own[0], column] = solved[column]
                applied_ref[row - own[0], column] = applied[column]
            add(0, source, solved)
            add(1, solved, applied)

    def emit_second(row, source, solved, applied):
        for column in columns:
            solved_two_ref[row - own[0], column] = solved[column]
            applied_two_ref[row - own[0], column] = applied[column]
        add(2, source, solved)
        add(3, solved, applied)

    work = (weight, coef, step_ref, remain_ref, part_ref)
    passes(0, own, total, first_source, *work, emit_first)
    passes(HALO, own, total, second_source, *work, emit_second)

    lane = lane_index((1, LANES))
    line = jnp.zeros((1, LANES), jnp.float32)
    for index in range(4):
        line = jnp.where(lane == index, jnp.sum(sums[index]), line)
    sums_ref[...] = jnp.broadcast_to(line[None], sums_ref.shape)


def inverse_kernel(
    rows, times, length, cas_ref, sums_ref, one_ref, two_ref, three_ref, four_ref, out_ref, line_ref
):
    half = LANES // 2
    span = half + 2 * SIDE
    skip = (span - WINDOW) // 2
    line = jnp.sum(sums_ref[...].reshape(sums_ref.shape[0], LANES), axis=0, keepdims=True)
    gamma, curved, cross, last = (
        jnp.broadcast_to(line[:, index : index + 1], (SUB, LANES)) for index in range(4)
    )
    step = gamma / curved
    gamma_next = step * step * cross - gamma
    turn = gamma_next / gamma
    grown = 1.0 + turn
    next_curved = grown * grown * curved - 2.0 * step * grown * cross + step * step * last
    next_step = gamma_next / next_curved
    first = step + next_step * grown
    second = -next_step * step
    for row in range(rows):
        for index, (left_ref, right_ref) in enumerate(((one_ref, two_ref), (three_ref, four_ref))):
            for column in range(BLOCK):
                start = (2 * row + index) * span + skip + column
                value = first * left_ref[row, column] + second * right_ref[row, column]
                line_ref[pl.ds(start, SUB, stride=BLOCK), :] = value
    for row in range(rows):
        start = 2 * row * span + SIDE
        points = jnp.concatenate(
            [line_ref[start : start + half, :], line_ref[start + span : start + span + half, :]],
            axis=0,
        )
        back = exact_dot(cas_ref[...], points, 1, 1).reshape(length // times, times, LANES)
        out_ref[:, row * times : (row + 1) * times, :] = back


def final_kernel(rows, times, tiles, source_ref, field_ref, solution_ref, residual_ref):
    half = LANES // 2
    low = lane_index((rows, LANES)) < half
    for time in range(times):
        place = slice(time * rows, (time + 1) * rows)
        taken = pl.ds(time, rows, stride=times)
        for pair in range(tiles // 2):
            columns = slice(pair * LANES, (pair + 1) * LANES)
            left = source_ref[2 * pair, taken, :]
            right = source_ref[2 * pair + 1, taken, :]
            solution_ref[place, columns] = jnp.where(low, left, pltpu.roll(right, half, 1))
            change = jnp.where(low, pltpu.roll(left, half, 1), right)
            residual_ref[place, columns] = field_ref[place, columns] - change


def call(kernel, out_shape, scratch=()):
    shapes = [jax.ShapeDtypeStruct(shape, jnp.float32) for shape in out_shape]
    return pl.pallas_call(
        kernel,
        out_shape=shapes[0] if len(shapes) == 1 else shapes,
        scratch_shapes=[pltpu.VMEM(shape, jnp.float32) for shape in scratch],
        compiler_params=PARAMS,
    )


def shift(value, distance, spaces):
    return lax.ppermute(value, "space", [(i, (i + distance) % spaces) for i in range(spaces)])


def shards(right_side, kappa, velocity):
    tiles = lax.axis_size("tm")
    spaces = lax.axis_size("space")
    times, rows, width = right_side.shape
    length = times * tiles
    tile = width // tiles
    around = (LANES - tile) // 2
    cas_table = jnp.asarray(hartley_table(length))
    coef_table = jnp.asarray(chebyshev_table(length))

    field = right_side.reshape(times * rows, width)
    windows = call(
        functools.partial(window_kernel, rows, times, tiles),
        [(tiles, 6 * times, LANES)],
        [(width // LANES, times * rows, LANES)],
    )(field)
    gathered = lax.all_to_all(windows, "tm", 0, 0)

    squares = velocity.astype(jnp.float32) ** 2
    planes = jnp.concatenate([kappa, squares[0], squares[1]], axis=0)
    planes = jnp.concatenate([planes[:, -around:], planes, planes[:, :around]], axis=1)
    local = lax.dynamic_slice_in_dim(planes, lax.axis_index("tm") * tile, LANES, 1)
    total = 3 * rows + 2 * FAR
    tile_shape = (rows, BLOCK, SUB, LANES)
    row_shape = (rows * BLOCK + 3, SUB, LANES)
    far_shape = (FAR * BLOCK + 3, SUB, LANES)
    span = LANES // 2 + 2 * SIDE
    freq, low, high = call(
        functools.partial(forward_kernel, rows, times, length),
        [row_shape, far_shape, far_shape],
        [(rows * span, LANES)],
    )(cas_table, gathered, local)
    top, bottom = shift(freq, 1, spaces), shift(freq, -1, spaces)
    top_far, bottom_far = shift(high, 2, spaces), shift(low, -2, spaces)

    groups = [
        [i * spaces + first + j for i in range(tiles) for j in range(NEAR)]
        for first in range(0, spaces, NEAR)
    ]
    work = (total, BLOCK, SUB, LANES)
    solved, applied, solved_two, applied_two, sums = call(
        functools.partial(stencil_kernel, rows),
        [tile_shape] * 4 + [(tiles * NEAR, 1, LANES)],
        [
            work,
            work,
            tile_shape,
            work,
            (total, 3 * BLOCK, SUB, LANES),
            (LANES, LANES),
        ],
    )(top_far, bottom, freq, top, bottom_far, coef_table)
    sums = lax.all_to_all(sums, ("tm", "space"), 0, 0, axis_index_groups=groups)
    planes = spaces // NEAR
    groups = [[first + NEAR * i for i in range(planes)] for first in range(NEAR)]
    sums = jnp.broadcast_to(jnp.sum(sums, axis=0)[None], (planes, 1, LANES))
    sums = lax.all_to_all(sums, "space", 0, 0, axis_index_groups=groups)
    packed = call(
        functools.partial(inverse_kernel, rows, times, length),
        [(tiles, rows * times, LANES)],
        [(rows * 2 * span, LANES)],
    )(cas_table, sums, solved, solved_two, applied, applied_two)
    returned = lax.all_to_all(packed, "tm", 0, 0)

    solution, residual = call(
        functools.partial(final_kernel, rows, times, tiles),
        [(times * rows, width), (times * rows, width)],
    )(returned, field)
    shape = right_side.shape
    return solution.reshape(shape), residual.reshape(shape)


def solution(mesh):
    placed = (P("tm", "space", None), P("space", None), P(None, "space", None))
    return jax.shard_map(
        shards,
        mesh=mesh,
        in_specs=placed,
        out_specs=(P("tm", "space", None), P("tm", "space", None)),
        check_vma=False,
    )
```

```python
import functools
import math

import jax
import jax.numpy as jnp
import numpy as np
from jax import lax
from jax.experimental import pallas as pl
from jax.experimental.pallas import tpu as pltpu
from jax.sharding import PartitionSpec as P

CHEB = 4
COUPLING = 2.0
KAPPA_LOW = 0.05
KAPPA_HIGH = 1.0
REACH = 16.0

LANES = 128
SUB = 8
HALO = CHEB + 1
FAR = 2
SIDE = 16
BLOCK = 11
WINDOW = SUB * BLOCK
NEAR = 4
PARAMS = pltpu.CompilerParams(vmem_limit_bytes=24 * 1024 * 1024)


def hartley_table(length):
    index = np.arange(length)
    angle = (index[:, None] * index[None, :] % length) * (2.0 * math.pi / length)
    return ((np.cos(angle) + np.sin(angle)) / math.sqrt(length)).astype(np.float32)


def chebyshev_table(length):
    shift = COUPLING * (2.0 - 2.0 * np.cos(2.0 * math.pi * np.arange(length) / length))
    half = 0.5 * (KAPPA_HIGH + REACH - KAPPA_LOW)
    mid = 0.5 * (KAPPA_LOW + KAPPA_HIGH + REACH) + shift
    ratio = mid / half
    damp = 1.0 / ratio
    lines = [shift, 1.0 / mid]
    for _ in range(CHEB):
        damp_next = 1.0 / (2.0 * ratio - damp)
        lines += [damp_next * damp, 2.0 * damp_next / half]
        damp = damp_next
    return np.repeat(np.stack(lines).astype(np.float32)[:, None], SUB, 1)


def lane_index(shape):
    return lax.broadcasted_iota(jnp.int32, shape, len(shape) - 1)


def exact_dot(left, right, left_dim, right_dim):
    return lax.dot_general(
        left,
        right,
        (((left_dim,), (right_dim,)), ((), ())),
        precision=lax.Precision.HIGHEST,
        preferred_element_type=jnp.float32,
    )


def window_kernel(rows, times, tiles, source_ref, out_ref, scratch_ref):
    half = LANES // 2
    parts = source_ref.shape[1] // LANES
    for part in range(parts):
        scratch_ref[part] = source_ref[:, part * LANES : (part + 1) * LANES]
    lane = lane_index((times, LANES))
    fields = [
        [scratch_ref[part, pl.ds(row, times, stride=rows), :] for part in range(parts)]
        for row in range(rows)
    ]
    for pair in range(rows // 2):
        for part in range(parts):
            one, two = fields[2 * pair][part], fields[2 * pair + 1][part]
            place = slice(pair * times, (pair + 1) * times)
            out_ref[2 * part, place, :] = jnp.where(lane < half, one, pltpu.roll(two, half, 1))
            out_ref[2 * part + 1, place, :] = jnp.where(lane < half, pltpu.roll(one, half, 1), two)
    spread = 2 * SIDE
    group = LANES // spread
    for quad in range(rows // group):
        even = [None] * parts
        odd = [None] * parts
        for index in range(group):
            row = quad * group + index
            wide = jnp.concatenate(fields[row], axis=1)
            near = pltpu.roll(wide, spread * index + SIDE, 1)
            away = pltpu.roll(wide, (spread * index - half + SIDE) % wide.shape[1], 1)
            left = (lane >= spread * index) & (lane < spread * index + SIDE)
            right = (lane >= spread * index + SIDE) & (lane < spread * (index + 1))
            for part in range(parts):
                here = slice(part * LANES, (part + 1) * LANES)
                then = (part + 1) % parts
                then = slice(then * LANES, (then + 1) * LANES)
                if index == 0:
                    even[part] = jnp.where(left, near[:, here], away[:, here])
                    odd[part] = jnp.where(left, away[:, here], near[:, then])
                else:
                    even[part] = jnp.where(
                        left, near[:, here], jnp.where(right, away[:, here], even[part])
                    )
                    odd[part] = jnp.where(
                        left, away[:, here], jnp.where(right, near[:, then], odd[part])
                    )
        start = (rows // 2 + quad) * times
        for part in range(parts):
            out_ref[2 * part, start : start + times, :] = even[part]
            out_ref[2 * part + 1, start : start + times, :] = odd[part]


def reach(distance):
    halo = 2 * HALO - distance
    margin = 0 if halo == 0 else 4 if halo <= 4 else 8 if halo <= 8 else 12
    return SIDE - margin, SIDE + LANES // 2 + margin


def sent_places(distances, start):
    places = {}
    for distance in distances:
        places[distance] = start
        first, last = reach(distance)
        start += last - first
    return places, start


def near_places(rows):
    return sent_places(range(rows, 0, -1), 3 * rows)


def far_places(rows):
    places, end = sent_places(range(rows + 1, rows + FAR + 1), SUB)
    return places, end + SIDE


def forward_kernel(
    rows, times, length, cas_ref, field_ref, local_ref,
    out_ref, up_ref, down_ref, far_up_ref, far_down_ref, line_ref,
):
    half = LANES // 2
    span = half + 2 * SIDE
    pieces = field_ref.shape[1] // times
    group = LANES // (2 * SIDE)
    for piece in range(pieces):
        block = field_ref[:, piece * times : (piece + 1) * times, :].reshape(length, LANES)
        freq = exact_dot(block, cas_ref[...], 0, 0)
        if piece < rows // 2:
            for part in range(2):
                start = (2 * piece + part) * span + SIDE
                line_ref[start : start + half, :] = freq[part * half : (part + 1) * half]
        else:
            for index in range(group):
                start = ((piece - rows // 2) * group + index) * span
                place = 2 * SIDE * index
                line_ref[start : start + SIDE, :] = freq[place : place + SIDE]
                line_ref[start + SIDE + half : start + span, :] = freq[
                    place + SIDE : place + 2 * SIDE
                ]
    skip = (span - WINDOW) // 2
    for row in range(rows):
        for column in range(BLOCK):
            value = line_ref[pl.ds(row * span + skip + column, SUB, stride=BLOCK), :]
            out_ref[row * BLOCK + column] = value
    for plane in range(3):
        out_ref[rows * BLOCK + plane] = local_ref[plane * rows : (plane + 1) * rows, :]
    near, far = near_places(rows)[0], far_places(rows)[0]
    for ref, places, row_of in (
        (up_ref, near, lambda distance: rows - distance),
        (down_ref, near, lambda distance: distance - 1),
        (far_up_ref, far, lambda distance: 2 * rows - distance),
        (far_down_ref, far, lambda distance: distance - 1 - rows),
    ):
        for distance, place in places.items():
            first, last = reach(distance)
            start = row_of(distance) * span
            ref[place : place + last - first, :] = line_ref[start + first : start + last, :]
    up_ref[: 3 * rows, :] = local_ref[...]
    down_ref[: 3 * rows, :] = local_ref[...]
    for ref, first in ((far_up_ref, rows - FAR), (far_down_ref, 0)):
        ref[ref.shape[0] - SIDE :, :] = jnp.zeros((SIDE, LANES), jnp.float32)
        kept = [local_ref[plane * rows + first : plane * rows + first + FAR, :] for plane in range(3)]
        kept.append(jnp.zeros((SUB - 3 * FAR, LANES), jnp.float32))
        ref[:SUB, :] = jnp.concatenate(kept, axis=0)


def weight_lines(parts, scratch_ref):
    planes = [jnp.concatenate(blocks, axis=0) for blocks in zip(*parts)]
    east = 1.0 + 0.125 * (planes[1] + jnp.concatenate([planes[1][1:], planes[1][:1]], axis=0))
    north = 1.0 + 0.125 * (planes[2] + pltpu.roll(planes[2], LANES - 1, 1))
    total = planes[0].shape[0]
    zero = jnp.zeros((LANES - 3 * total, LANES), jnp.float32)
    scratch_ref[...] = jnp.transpose(jnp.concatenate([planes[0], east, north, zero], axis=0))
    skip = (LANES - WINDOW) // 2
    return [scratch_ref[pl.ds(skip + column, SUB, stride=BLOCK), :] for column in range(BLOCK)]


def own_columns(column):
    place = lax.broadcasted_iota(jnp.int32, (SUB, LANES), 0) * BLOCK + column
    first = (WINDOW - LANES // 2) // 2
    return (place >= first) & (place < first + LANES // 2)


def passes(edge, own, total, source, weight, coef, step_ref, remain_ref, solved_ref, emit):
    columns = range(BLOCK)

    for turn in range(CHEB + 1):
        first, last = edge + turn + 1, total - edge - turn - 1

        def load(row, turn=turn):
            if turn == 0:
                return [coef[1] * source(row, column) for column in columns]
            return [step_ref[row, column] for column in columns]

        here = load(first - 1)
        flux = None
        for row in range(first - 1, last):
            after = load(row + 1)
            ahead = [weight(1, row, column) * (here[column] - after[column]) for column in columns]
            if row >= first:
                beside = here[1:] + [pltpu.roll(here[0], SUB - 1, 0)]
                side = [weight(2, row, column) * (here[column] - beside[column]) for column in columns]
                behind = [pltpu.roll(side[-1], 1, 0)] + side[:-1]
                inside = row in range(*own)
                results = []
                for column in columns:
                    applied = (
                        weight(0, row, column) * here[column]
                        + (ahead[column] - flux[column])
                        + (side[column] - behind[column])
                    )
                    before = source(row, column) if turn == 0 else remain_ref[row, column]
                    left = before - applied
                    if turn < CHEB:
                        remain_ref[row, column] = left
                        step_ref[row, column] = (
                            coef[2 + 2 * turn] * here[column] + coef[3 + 2 * turn] * left
                        )
                    solved = None
                    if inside:
                        place = row - own[0]
                        solved = here[column]
                        if turn > 0:
                            solved = solved_ref[place, column] + solved
                        if turn < CHEB:
                            solved_ref[place, column] = solved
                    if turn == CHEB:
                        begun = source(row, column)
                        results.append((begun, solved, begun - left))
                if turn == CHEB:
                    emit(row, *zip(*results))
            here, flux = after, ahead


def stencil_kernel(
    rows, top_far_ref, top_ref, field_ref, bottom_ref, bottom_far_ref, coef_ref,
    solved_ref, applied_ref, solved_two_ref, applied_two_ref, sums_ref,
    step_ref, remain_ref, part_ref, middle_ref, wide_ref, scratch_ref,
):
    columns = range(BLOCK)
    parts = [
        [top_far_ref[plane * FAR : (plane + 1) * FAR, :] for plane in range(3)],
        [top_ref[plane * rows : (plane + 1) * rows, :] for plane in range(3)],
        [field_ref[rows * BLOCK + plane] for plane in range(3)],
        [bottom_ref[plane * rows : (plane + 1) * rows, :] for plane in range(3)],
        [bottom_far_ref[plane * FAR : (plane + 1) * FAR, :] for plane in range(3)],
    ]
    lines = weight_lines(parts, scratch_ref)
    coef = [coef_ref[index] for index in range(2 + 2 * CHEB)]
    total = 3 * rows + 2 * FAR
    skip = (LANES // 2 + 2 * SIDE - WINDOW) // 2
    near, far = near_places(rows)[0], far_places(rows)[0]
    own = (FAR + rows, FAR + 2 * rows)
    made = set()

    def weight(plane, row, column):
        place = plane * BLOCK + column
        if (row, place) in made:
            return wide_ref[row, place]
        index = plane * total + row
        value = jnp.broadcast_to(lines[column][:, index : index + 1], (SUB, LANES))
        if plane == 0:
            value = value + coef[0]
        wide_ref[row, place] = value
        made.add((row, place))
        return value

    def first_source(row, column):
        if row in range(*own):
            return field_ref[(row - own[0]) * BLOCK + column]
        distance = own[0] - row if row < own[0] else row - own[1] + 1
        if distance > rows:
            ref, place = (top_far_ref if row < own[0] else bottom_far_ref), far[distance]
        else:
            ref, place = (top_ref if row < own[0] else bottom_ref), near[distance]
        start = place - reach(distance)[0] + skip + column
        return ref[pl.ds(start, SUB, stride=BLOCK), :]

    def second_source(row, column):
        return middle_ref[row, column]

    sums = [jnp.zeros((SUB, LANES), jnp.float32) for _ in range(4)]

    def add(index, one, two):
        for column in columns:
            product = one[column] * two[column]
            sums[index] = sums[index] + jnp.where(own_columns(column), product, 0.0)

    def emit_first(row, source, solved, applied):
        for column in columns:
            middle_ref[row, column] = applied[column]
        if row in range(*own):
            for column in columns:
                solved_ref[row - own[0], column] = solved[column]
                applied_ref[row - own[0], column] = applied[column]
            add(0, source, solved)
            add(1, solved, applied)

    def emit_second(row, source, solved, applied):
        for column in columns:
            solved_two_ref[row - own[0], column] = solved[column]
            applied_two_ref[row - own[0], column] = applied[column]
        add(2, source, solved)
        add(3, solved, applied)

    work = (weight, coef, step_ref, remain_ref, part_ref)
    passes(0, own, total, first_source, *work, emit_first)
    passes(HALO, own, total, second_source, *work, emit_second)

    lane = lane_index((1, LANES))
    line = jnp.zeros((1, LANES), jnp.float32)
    for index in range(4):
        line = jnp.where(lane == index, jnp.sum(sums[index]), line)
    sums_ref[...] = jnp.broadcast_to(line[None], sums_ref.shape)


def inverse_kernel(
    rows, times, length, cas_ref, sums_ref, one_ref, two_ref, three_ref, four_ref, out_ref, line_ref
):
    half = LANES // 2
    span = half + 2 * SIDE
    skip = (span - WINDOW) // 2
    line = jnp.sum(sums_ref[...].reshape(sums_ref.shape[0], LANES), axis=0, keepdims=True)
    gamma, curved, cross, last = (
        jnp.broadcast_to(line[:, index : index + 1], (SUB, LANES)) for index in range(4)
    )
    step = gamma / curved
    gamma_next = step * step * cross - gamma
    turn = gamma_next / gamma
    grown = 1.0 + turn
    next_curved = grown * grown * curved - 2.0 * step * grown * cross + step * step * last
    next_step = gamma_next / next_curved
    first = step + next_step * grown
    second = -next_step * step
    for row in range(rows):
        for index, (left_ref, right_ref) in enumerate(((one_ref, two_ref), (three_ref, four_ref))):
            for column in range(BLOCK):
                start = (2 * row + index) * span + skip + column
                value = first * left_ref[row, column] + second * right_ref[row, column]
                line_ref[pl.ds(start, SUB, stride=BLOCK), :] = value
    for row in range(rows):
        start = 2 * row * span + SIDE
        points = jnp.concatenate(
            [line_ref[start : start + half, :], line_ref[start + span : start + span + half, :]],
            axis=0,
        )
        back = exact_dot(cas_ref[...], points, 1, 1).reshape(length // times, times, LANES)
        out_ref[:, row * times : (row + 1) * times, :] = back


def final_kernel(rows, times, tiles, source_ref, field_ref, solution_ref, residual_ref):
    half = LANES // 2
    low = lane_index((rows, LANES)) < half
    for time in range(times):
        place = slice(time * rows, (time + 1) * rows)
        taken = pl.ds(time, rows, stride=times)
        for pair in range(tiles // 2):
            columns = slice(pair * LANES, (pair + 1) * LANES)
            left = source_ref[2 * pair, taken, :]
            right = source_ref[2 * pair + 1, taken, :]
            solution_ref[place, columns] = jnp.where(low, left, pltpu.roll(right, half, 1))
            change = jnp.where(low, pltpu.roll(left, half, 1), right)
            residual_ref[place, columns] = field_ref[place, columns] - change


def call(kernel, out_shape, scratch=()):
    shapes = [jax.ShapeDtypeStruct(shape, jnp.float32) for shape in out_shape]
    return pl.pallas_call(
        kernel,
        out_shape=shapes[0] if len(shapes) == 1 else shapes,
        scratch_shapes=[pltpu.VMEM(shape, jnp.float32) for shape in scratch],
        compiler_params=PARAMS,
    )


def shift(value, distance, spaces):
    return lax.ppermute(value, "space", [(i, (i + distance) % spaces) for i in range(spaces)])


def shards(right_side, kappa, velocity):
    tiles = lax.axis_size("tm")
    spaces = lax.axis_size("space")
    times, rows, width = right_side.shape
    length = times * tiles
    tile = width // tiles
    around = (LANES - tile) // 2
    cas_table = jnp.asarray(hartley_table(length))
    coef_table = jnp.asarray(chebyshev_table(length))

    field = right_side.reshape(times * rows, width)
    windows = call(
        functools.partial(window_kernel, rows, times, tiles),
        [(tiles, 6 * times, LANES)],
        [(width // LANES, times * rows, LANES)],
    )(field)
    gathered = lax.all_to_all(windows, "tm", 0, 0)

    squares = velocity.astype(jnp.float32) ** 2
    planes = jnp.concatenate([kappa, squares[0], squares[1]], axis=0)
    planes = jnp.concatenate([planes[:, -around:], planes, planes[:, :around]], axis=1)
    local = lax.dynamic_slice_in_dim(planes, lax.axis_index("tm") * tile, LANES, 1)
    total = 3 * rows + 2 * FAR
    tile_shape = (rows, BLOCK, SUB, LANES)
    near_shape = (near_places(rows)[1], LANES)
    far_shape = (far_places(rows)[1], LANES)
    span = LANES // 2 + 2 * SIDE
    freq, up, down, far_up, far_down = call(
        functools.partial(forward_kernel, rows, times, length),
        [(rows * BLOCK + 3, SUB, LANES), near_shape, near_shape, far_shape, far_shape],
        [(rows * span, LANES)],
    )(cas_table, gathered, local)
    top, bottom = shift(up, 1, spaces), shift(down, -1, spaces)
    top_far, bottom_far = shift(far_up, 2, spaces), shift(far_down, -2, spaces)

    groups = [
        [i * spaces + first + j for i in range(tiles) for j in range(NEAR)]
        for first in range(0, spaces, NEAR)
    ]
    work = (total, BLOCK, SUB, LANES)
    solved, applied, solved_two, applied_two, sums = call(
        functools.partial(stencil_kernel, rows),
        [tile_shape] * 4 + [(tiles * NEAR, 1, LANES)],
        [
            work,
            work,
            tile_shape,
            work,
            (total, 3 * BLOCK, SUB, LANES),
            (LANES, LANES),
        ],
    )(top_far, top, freq, bottom, bottom_far, coef_table)
    sums = lax.all_to_all(sums, ("tm", "space"), 0, 0, axis_index_groups=groups)
    planes = spaces // NEAR
    groups = [[first + NEAR * i for i in range(planes)] for first in range(NEAR)]
    sums = jnp.broadcast_to(jnp.sum(sums, axis=0)[None], (planes, 1, LANES))
    sums = lax.all_to_all(sums, "space", 0, 0, axis_index_groups=groups)
    packed = call(
        functools.partial(inverse_kernel, rows, times, length),
        [(tiles, rows * times, LANES)],
        [(rows * 2 * span, LANES)],
    )(cas_table, sums, solved, solved_two, applied, applied_two)
    returned = lax.all_to_all(packed, "tm", 0, 0)

    solution, residual = call(
        functools.partial(final_kernel, rows, times, tiles),
        [(times * rows, width), (times * rows, width)],
    )(returned, field)
    shape = right_side.shape
    return solution.reshape(shape), residual.reshape(shape)


def solution(mesh):
    placed = (P("tm", "space", None), P("space", None), P(None, "space", None))
    return jax.shard_map(
        shards,
        mesh=mesh,
        in_specs=placed,
        out_specs=(P("tm", "space", None), P("tm", "space", None)),
        check_vma=False,
    )
```

```python
import functools
import math

import jax
import jax.numpy as jnp
import numpy as np
from jax import lax
from jax.experimental import pallas as pl
from jax.experimental.pallas import tpu as pltpu
from jax.sharding import PartitionSpec as P

CHEB = 4
COUPLING = 2.0
KAPPA_LOW = 0.05
KAPPA_HIGH = 1.0
REACH = 16.0

LANES = 128
SUB = 8
HALO = CHEB + 1
FAR = 2
SIDE = 16
BLOCK = 11
WINDOW = SUB * BLOCK
NEAR = 4
PARAMS = pltpu.CompilerParams(vmem_limit_bytes=24 * 1024 * 1024)


def hartley_table(length):
    index = np.arange(length)
    angle = (index[:, None] * index[None, :] % length) * (2.0 * math.pi / length)
    return ((np.cos(angle) + np.sin(angle)) / math.sqrt(length)).astype(np.float32)


def chebyshev_table(length):
    shift = COUPLING * (2.0 - 2.0 * np.cos(2.0 * math.pi * np.arange(length) / length))
    half = 0.5 * (KAPPA_HIGH + REACH - KAPPA_LOW)
    mid = 0.5 * (KAPPA_LOW + KAPPA_HIGH + REACH) + shift
    ratio = mid / half
    damp = 1.0 / ratio
    lines = [shift, 1.0 / mid]
    for _ in range(CHEB):
        damp_next = 1.0 / (2.0 * ratio - damp)
        lines += [damp_next * damp, 2.0 * damp_next / half]
        damp = damp_next
    return np.repeat(np.stack(lines).astype(np.float32)[:, None], SUB, 1)


def lane_index(shape):
    return lax.broadcasted_iota(jnp.int32, shape, len(shape) - 1)


def exact_dot(left, right, left_dim, right_dim):
    return lax.dot_general(
        left,
        right,
        (((left_dim,), (right_dim,)), ((), ())),
        precision=lax.Precision.HIGHEST,
        preferred_element_type=jnp.float32,
    )


def window_kernel(rows, times, tiles, source_ref, out_ref, scratch_ref, arrived):
    half = LANES // 2
    parts = source_ref.shape[1] // LANES
    copies = [
        pltpu.make_async_copy(
            source_ref.at[:, pl.ds(part * LANES, LANES)], scratch_ref.at[part], arrived.at[part]
        )
        for part in range(parts)
    ]
    for copy in copies:
        copy.start()
    for copy in copies:
        copy.wait()
    lane = lane_index((times, LANES))
    fields = [
        [scratch_ref[part, pl.ds(row, times, stride=rows), :] for part in range(parts)]
        for row in range(rows)
    ]
    for pair in range(rows // 2):
        for part in range(parts):
            one, two = fields[2 * pair][part], fields[2 * pair + 1][part]
            place = slice(pair * times, (pair + 1) * times)
            out_ref[2 * part, place, :] = jnp.where(lane < half, one, pltpu.roll(two, half, 1))
            out_ref[2 * part + 1, place, :] = jnp.where(lane < half, pltpu.roll(one, half, 1), two)
    spread = 2 * SIDE
    group = LANES // spread
    for quad in range(rows // group):
        even = [None] * parts
        odd = [None] * parts
        for index in range(group):
            row = quad * group + index
            wide = jnp.concatenate(fields[row], axis=1)
            near = pltpu.roll(wide, spread * index + SIDE, 1)
            away = pltpu.roll(wide, (spread * index - half + SIDE) % wide.shape[1], 1)
            left = (lane >= spread * index) & (lane < spread * index + SIDE)
            right = (lane >= spread * index + SIDE) & (lane < spread * (index + 1))
            for part in range(parts):
                here = slice(part * LANES, (part + 1) * LANES)
                then = (part + 1) % parts
                then = slice(then * LANES, (then + 1) * LANES)
                if index == 0:
                    even[part] = jnp.where(left, near[:, here], away[:, here])
                    odd[part] = jnp.where(left, away[:, here], near[:, then])
                else:
                    even[part] = jnp.where(
                        left, near[:, here], jnp.where(right, away[:, here], even[part])
                    )
                    odd[part] = jnp.where(
                        left, away[:, here], jnp.where(right, near[:, then], odd[part])
                    )
        start = (rows // 2 + quad) * times
        for part in range(parts):
            out_ref[2 * part, start : start + times, :] = even[part]
            out_ref[2 * part + 1, start : start + times, :] = odd[part]


def reach(distance):
    halo = 2 * HALO - distance
    margin = 0 if halo == 0 else 4 if halo <= 4 else 8 if halo <= 8 else 12
    return SIDE - margin, SIDE + LANES // 2 + margin


def sent_places(distances, start):
    places = {}
    for distance in distances:
        places[distance] = start
        first, last = reach(distance)
        start += last - first
    return places, start


def near_places(rows):
    return sent_places(range(rows, 0, -1), 3 * rows)


def far_places(rows):
    places, end = sent_places(range(rows + 1, rows + FAR + 1), SUB)
    return places, end + SIDE


def forward_kernel(
    rows, times, length, cas_ref, field_ref, local_ref,
    out_ref, up_ref, down_ref, far_up_ref, far_down_ref, line_ref,
):
    half = LANES // 2
    span = half + 2 * SIDE
    pieces = field_ref.shape[1] // times
    group = LANES // (2 * SIDE)
    for piece in range(pieces):
        block = field_ref[:, piece * times : (piece + 1) * times, :].reshape(length, LANES)
        freq = exact_dot(block, cas_ref[...], 0, 0)
        if piece < rows // 2:
            for part in range(2):
                start = (2 * piece + part) * span + SIDE
                line_ref[start : start + half, :] = freq[part * half : (part + 1) * half]
        else:
            for index in range(group):
                start = ((piece - rows // 2) * group + index) * span
                place = 2 * SIDE * index
                line_ref[start : start + SIDE, :] = freq[place : place + SIDE]
                line_ref[start + SIDE + half : start + span, :] = freq[
                    place + SIDE : place + 2 * SIDE
                ]
    skip = (span - WINDOW) // 2
    for row in range(rows):
        for column in range(BLOCK):
            value = line_ref[pl.ds(row * span + skip + column, SUB, stride=BLOCK), :]
            out_ref[row * BLOCK + column] = value
    for plane in range(3):
        out_ref[rows * BLOCK + plane] = local_ref[plane * rows : (plane + 1) * rows, :]
    near, far = near_places(rows)[0], far_places(rows)[0]
    for ref, places, row_of in (
        (up_ref, near, lambda distance: rows - distance),
        (down_ref, near, lambda distance: distance - 1),
        (far_up_ref, far, lambda distance: 2 * rows - distance),
        (far_down_ref, far, lambda distance: distance - 1 - rows),
    ):
        for distance, place in places.items():
            first, last = reach(distance)
            start = row_of(distance) * span
            ref[place : place + last - first, :] = line_ref[start + first : start + last, :]
    up_ref[: 3 * rows, :] = local_ref[...]
    down_ref[: 3 * rows, :] = local_ref[...]
    for ref, first in ((far_up_ref, rows - FAR), (far_down_ref, 0)):
        ref[ref.shape[0] - SIDE :, :] = jnp.zeros((SIDE, LANES), jnp.float32)
        kept = [local_ref[plane * rows + first : plane * rows + first + FAR, :] for plane in range(3)]
        kept.append(jnp.zeros((SUB - 3 * FAR, LANES), jnp.float32))
        ref[:SUB, :] = jnp.concatenate(kept, axis=0)


def weight_lines(parts, scratch_ref):
    planes = [jnp.concatenate(blocks, axis=0) for blocks in zip(*parts)]
    east = 1.0 + 0.125 * (planes[1] + jnp.concatenate([planes[1][1:], planes[1][:1]], axis=0))
    north = 1.0 + 0.125 * (planes[2] + pltpu.roll(planes[2], LANES - 1, 1))
    total = planes[0].shape[0]
    zero = jnp.zeros((LANES - 3 * total, LANES), jnp.float32)
    scratch_ref[...] = jnp.transpose(jnp.concatenate([planes[0], east, north, zero], axis=0))
    skip = (LANES - WINDOW) // 2
    return [scratch_ref[pl.ds(skip + column, SUB, stride=BLOCK), :] for column in range(BLOCK)]


def own_columns(column):
    place = lax.broadcasted_iota(jnp.int32, (SUB, LANES), 0) * BLOCK + column
    first = (WINDOW - LANES // 2) // 2
    return (place >= first) & (place < first + LANES // 2)


def passes(edge, own, total, source, weight, coef, step_ref, remain_ref, solved_ref, emit):
    columns = range(BLOCK)

    for turn in range(CHEB + 1):
        first, last = edge + turn + 1, total - edge - turn - 1

        def load(row, turn=turn):
            if turn == 0:
                return [coef[1] * source(row, column) for column in columns]
            return [step_ref[row, column] for column in columns]

        here = load(first - 1)
        flux = None
        for row in range(first - 1, last):
            after = load(row + 1)
            ahead = [weight(1, row, column) * (here[column] - after[column]) for column in columns]
            if row >= first:
                beside = here[1:] + [pltpu.roll(here[0], SUB - 1, 0)]
                side = [weight(2, row, column) * (here[column] - beside[column]) for column in columns]
                behind = [pltpu.roll(side[-1], 1, 0)] + side[:-1]
                inside = row in range(*own)
                results = []
                for column in columns:
                    applied = (
                        weight(0, row, column) * here[column]
                        + (ahead[column] - flux[column])
                        + (side[column] - behind[column])
                    )
                    before = source(row, column) if turn == 0 else remain_ref[row, column]
                    left = before - applied
                    if turn < CHEB:
                        remain_ref[row, column] = left
                        step_ref[row, column] = (
                            coef[2 + 2 * turn] * here[column] + coef[3 + 2 * turn] * left
                        )
                    solved = None
                    if inside:
                        place = row - own[0]
                        solved = here[column]
                        if turn > 0:
                            solved = solved_ref[place, column] + solved
                        if turn < CHEB:
                            solved_ref[place, column] = solved
                    if turn == CHEB:
                        begun = source(row, column)
                        results.append((begun, solved, begun - left))
                if turn == CHEB:
                    emit(row, *zip(*results))
            here, flux = after, ahead


def stencil_kernel(
    rows, bottom_far_ref, top_ref, field_ref, bottom_ref, top_far_ref, coef_ref,
    solved_ref, applied_ref, solved_two_ref, applied_two_ref, sums_ref,
    step_ref, remain_ref, part_ref, middle_ref, wide_ref, scratch_ref,
):
    columns = range(BLOCK)
    parts = [
        [top_far_ref[plane * FAR : (plane + 1) * FAR, :] for plane in range(3)],
        [top_ref[plane * rows : (plane + 1) * rows, :] for plane in range(3)],
        [field_ref[rows * BLOCK + plane] for plane in range(3)],
        [bottom_ref[plane * rows : (plane + 1) * rows, :] for plane in range(3)],
        [bottom_far_ref[plane * FAR : (plane + 1) * FAR, :] for plane in range(3)],
    ]
    lines = weight_lines(parts, scratch_ref)
    coef = [coef_ref[index] for index in range(2 + 2 * CHEB)]
    total = 3 * rows + 2 * FAR
    skip = (LANES // 2 + 2 * SIDE - WINDOW) // 2
    near, far = near_places(rows)[0], far_places(rows)[0]
    own = (FAR + rows, FAR + 2 * rows)
    made = set()

    def weight(plane, row, column):
        place = plane * BLOCK + column
        if (row, place) in made:
            return wide_ref[row, place]
        index = plane * total + row
        value = jnp.broadcast_to(lines[column][:, index : index + 1], (SUB, LANES))
        if plane == 0:
            value = value + coef[0]
        wide_ref[row, place] = value
        made.add((row, place))
        return value

    def first_source(row, column):
        if row in range(*own):
            return field_ref[(row - own[0]) * BLOCK + column]
        distance = own[0] - row if row < own[0] else row - own[1] + 1
        if distance > rows:
            ref, place = (top_far_ref if row < own[0] else bottom_far_ref), far[distance]
        else:
            ref, place = (top_ref if row < own[0] else bottom_ref), near[distance]
        start = place - reach(distance)[0] + skip + column
        return ref[pl.ds(start, SUB, stride=BLOCK), :]

    def second_source(row, column):
        return middle_ref[row, column]

    sums = [jnp.zeros((SUB, LANES), jnp.float32) for _ in range(4)]

    def add(index, one, two):
        for column in columns:
            product = one[column] * two[column]
            sums[index] = sums[index] + jnp.where(own_columns(column), product, 0.0)

    def emit_first(row, source, solved, applied):
        for column in columns:
            middle_ref[row, column] = applied[column]
        if row in range(*own):
            for column in columns:
                solved_ref[row - own[0], column] = solved[column]
                applied_ref[row - own[0], column] = applied[column]
            add(0, source, solved)
            add(1, solved, applied)

    def emit_second(row, source, solved, applied):
        for column in columns:
            solved_two_ref[row - own[0], column] = solved[column]
            applied_two_ref[row - own[0], column] = applied[column]
        add(2, source, solved)
        add(3, solved, applied)

    work = (weight, coef, step_ref, remain_ref, part_ref)
    passes(0, own, total, first_source, *work, emit_first)
    passes(HALO, own, total, second_source, *work, emit_second)

    lane = lane_index((1, LANES))
    line = jnp.zeros((1, LANES), jnp.float32)
    for index in range(4):
        line = jnp.where(lane == index, jnp.sum(sums[index]), line)
    sums_ref[...] = jnp.broadcast_to(line[None], sums_ref.shape)


def inverse_kernel(
    rows, times, length, cas_ref, sums_ref, one_ref, two_ref, three_ref, four_ref, out_ref, line_ref
):
    half = LANES // 2
    span = half + 2 * SIDE
    skip = (span - WINDOW) // 2
    line = jnp.sum(sums_ref[...].reshape(sums_ref.shape[0], LANES), axis=0, keepdims=True)
    gamma, curved, cross, last = (
        jnp.broadcast_to(line[:, index : index + 1], (SUB, LANES)) for index in range(4)
    )
    step = gamma / curved
    gamma_next = step * step * cross - gamma
    turn = gamma_next / gamma
    grown = 1.0 + turn
    next_curved = grown * grown * curved - 2.0 * step * grown * cross + step * step * last
    next_step = gamma_next / next_curved
    first = step + next_step * grown
    second = -next_step * step
    for row in range(rows):
        for index, (left_ref, right_ref) in enumerate(((one_ref, two_ref), (three_ref, four_ref))):
            for column in range(BLOCK):
                start = (2 * row + index) * span + skip + column
                value = first * left_ref[row, column] + second * right_ref[row, column]
                line_ref[pl.ds(start, SUB, stride=BLOCK), :] = value
    for row in range(rows):
        start = 2 * row * span + SIDE
        points = jnp.concatenate(
            [line_ref[start : start + half, :], line_ref[start + span : start + span + half, :]],
            axis=0,
        )
        back = exact_dot(cas_ref[...], points, 1, 1).reshape(length // times, times, LANES)
        out_ref[:, row * times : (row + 1) * times, :] = back


def final_kernel(rows, times, tiles, source_ref, field_ref, solution_ref, residual_ref):
    half = LANES // 2
    low = lane_index((rows, LANES)) < half
    for time in range(times):
        place = slice(time * rows, (time + 1) * rows)
        taken = pl.ds(time, rows, stride=times)
        for pair in range(tiles // 2):
            columns = slice(pair * LANES, (pair + 1) * LANES)
            left = source_ref[2 * pair, taken, :]
            right = source_ref[2 * pair + 1, taken, :]
            solution_ref[place, columns] = jnp.where(low, left, pltpu.roll(right, half, 1))
            change = jnp.where(low, pltpu.roll(left, half, 1), right)
            residual_ref[place, columns] = field_ref[place, columns] - change


def call(kernel, out_shape, scratch=()):
    shapes = [jax.ShapeDtypeStruct(shape, jnp.float32) for shape in out_shape]
    return pl.pallas_call(
        kernel,
        out_shape=shapes[0] if len(shapes) == 1 else shapes,
        scratch_shapes=[pltpu.VMEM(shape, jnp.float32) for shape in scratch],
        compiler_params=PARAMS,
    )


def shift(value, distance, spaces):
    return lax.ppermute(value, "space", [(i, (i + distance) % spaces) for i in range(spaces)])


def shards(right_side, kappa, velocity):
    tiles = lax.axis_size("tm")
    spaces = lax.axis_size("space")
    times, rows, width = right_side.shape
    length = times * tiles
    tile = width // tiles
    around = (LANES - tile) // 2
    cas_table = jnp.asarray(hartley_table(length))
    coef_table = jnp.asarray(chebyshev_table(length))

    field = right_side.reshape(times * rows, width)
    windows = pl.pallas_call(
        functools.partial(window_kernel, rows, times, tiles),
        out_shape=jax.ShapeDtypeStruct((tiles, 6 * times, LANES), jnp.float32),
        in_specs=[pl.BlockSpec(memory_space=pl.ANY)],
        scratch_shapes=[
            pltpu.VMEM((width // LANES, times * rows, LANES), jnp.float32),
            pltpu.SemaphoreType.DMA((width // LANES,)),
        ],
        compiler_params=PARAMS,
    )(field)
    gathered = lax.all_to_all(windows, "tm", 0, 0)

    squares = velocity.astype(jnp.float32) ** 2
    planes = jnp.concatenate([kappa, squares[0], squares[1]], axis=0)
    planes = jnp.concatenate([planes[:, -around:], planes, planes[:, :around]], axis=1)
    local = lax.dynamic_slice_in_dim(planes, lax.axis_index("tm") * tile, LANES, 1)
    total = 3 * rows + 2 * FAR
    tile_shape = (rows, BLOCK, SUB, LANES)
    near_shape = (near_places(rows)[1], LANES)
    far_shape = (far_places(rows)[1], LANES)
    span = LANES // 2 + 2 * SIDE
    freq, up, down, far_up, far_down = call(
        functools.partial(forward_kernel, rows, times, length),
        [(rows * BLOCK + 3, SUB, LANES), near_shape, near_shape, far_shape, far_shape],
        [(rows * span, LANES)],
    )(cas_table, gathered, local)
    top, bottom = shift(up, 1, spaces), shift(down, -1, spaces)
    top_far, bottom_far = shift(far_up, 2, spaces), shift(far_down, -2, spaces)

    groups = [
        [i * spaces + first + j for i in range(tiles) for j in range(NEAR)]
        for first in range(0, spaces, NEAR)
    ]
    work = (total, BLOCK, SUB, LANES)
    solved, applied, solved_two, applied_two, sums = call(
        functools.partial(stencil_kernel, rows),
        [tile_shape] * 4 + [(tiles * NEAR, 1, LANES)],
        [
            work,
            work,
            tile_shape,
            work,
            (total, 3 * BLOCK, SUB, LANES),
            (LANES, LANES),
        ],
    )(bottom_far, top, freq, bottom, top_far, coef_table)
    sums = lax.all_to_all(sums, ("tm", "space"), 0, 0, axis_index_groups=groups)
    planes = spaces // NEAR
    groups = [[first + NEAR * i for i in range(planes)] for first in range(NEAR)]
    sums = jnp.broadcast_to(jnp.sum(sums, axis=0)[None], (planes, 1, LANES))
    sums = lax.all_to_all(sums, "space", 0, 0, axis_index_groups=groups)
    packed = call(
        functools.partial(inverse_kernel, rows, times, length),
        [(tiles, rows * times, LANES)],
        [(rows * 2 * span, LANES)],
    )(cas_table, sums, solved, solved_two, applied, applied_two)
    returned = lax.all_to_all(packed, "tm", 0, 0)

    solution, residual = call(
        functools.partial(final_kernel, rows, times, tiles),
        [(times * rows, width), (times * rows, width)],
    )(returned, field)
    shape = right_side.shape
    return solution.reshape(shape), residual.reshape(shape)


def solution(mesh):
    placed = (P("tm", "space", None), P("space", None), P(None, "space", None))
    return jax.shard_map(
        shards,
        mesh=mesh,
        in_specs=placed,
        out_specs=(P("tm", "space", None), P("tm", "space", None)),
        check_vma=False,
    )
```

```python
import functools
import math

import jax
import jax.numpy as jnp
import numpy as np
from jax import lax
from jax.experimental import pallas as pl
from jax.experimental.pallas import tpu as pltpu
from jax.sharding import PartitionSpec as P

CHEB = 4
COUPLING = 2.0
KAPPA_LOW = 0.05
KAPPA_HIGH = 1.0
REACH = 16.0

LANES = 128
SUB = 8
HALO = CHEB + 1
FAR = 2
SIDE = 16
BLOCK = 11
WINDOW = SUB * BLOCK
NEAR = 4
PARAMS = pltpu.CompilerParams(vmem_limit_bytes=24 * 1024 * 1024)


def hartley_table(length):
    index = np.arange(length)
    angle = (index[:, None] * index[None, :] % length) * (2.0 * math.pi / length)
    return ((np.cos(angle) + np.sin(angle)) / math.sqrt(length)).astype(np.float32)


def chebyshev_table(length):
    shift = COUPLING * (2.0 - 2.0 * np.cos(2.0 * math.pi * np.arange(length) / length))
    half = 0.5 * (KAPPA_HIGH + REACH - KAPPA_LOW)
    mid = 0.5 * (KAPPA_LOW + KAPPA_HIGH + REACH) + shift
    ratio = mid / half
    damp = 1.0 / ratio
    lines = [shift, 1.0 / mid]
    for _ in range(CHEB):
        damp_next = 1.0 / (2.0 * ratio - damp)
        lines += [damp_next * damp, 2.0 * damp_next / half]
        damp = damp_next
    return np.repeat(np.stack(lines).astype(np.float32)[:, None], SUB, 1)


def lane_index(shape):
    return lax.broadcasted_iota(jnp.int32, shape, len(shape) - 1)


def exact_dot(left, right, left_dim, right_dim):
    return lax.dot_general(
        left,
        right,
        (((left_dim,), (right_dim,)), ((), ())),
        precision=lax.Precision.HIGHEST,
        preferred_element_type=jnp.float32,
    )


def window_kernel(rows, times, tiles, source_ref, out_ref, scratch_ref):
    half = LANES // 2
    parts = source_ref.shape[1] // LANES
    for part in range(parts):
        scratch_ref[part] = source_ref[:, part * LANES : (part + 1) * LANES]
    lane = lane_index((times, LANES))
    fields = [
        [scratch_ref[part, pl.ds(row, times, stride=rows), :] for part in range(parts)]
        for row in range(rows)
    ]
    for pair in range(rows // 2):
        for part in range(parts):
            one, two = fields[2 * pair][part], fields[2 * pair + 1][part]
            place = slice(pair * times, (pair + 1) * times)
            out_ref[2 * part, place, :] = jnp.where(lane < half, one, pltpu.roll(two, half, 1))
            out_ref[2 * part + 1, place, :] = jnp.where(lane < half, pltpu.roll(one, half, 1), two)
    spread = 2 * SIDE
    group = LANES // spread
    for quad in range(rows // group):
        even = [None] * parts
        odd = [None] * parts
        for index in range(group):
            row = quad * group + index
            wide = jnp.concatenate(fields[row], axis=1)
            near = pltpu.roll(wide, spread * index + SIDE, 1)
            away = pltpu.roll(wide, (spread * index - half + SIDE) % wide.shape[1], 1)
            left = (lane >= spread * index) & (lane < spread * index + SIDE)
            right = (lane >= spread * index + SIDE) & (lane < spread * (index + 1))
            for part in range(parts):
                here = slice(part * LANES, (part + 1) * LANES)
                then = (part + 1) % parts
                then = slice(then * LANES, (then + 1) * LANES)
                if index == 0:
                    even[part] = jnp.where(left, near[:, here], away[:, here])
                    odd[part] = jnp.where(left, away[:, here], near[:, then])
                else:
                    even[part] = jnp.where(
                        left, near[:, here], jnp.where(right, away[:, here], even[part])
                    )
                    odd[part] = jnp.where(
                        left, away[:, here], jnp.where(right, near[:, then], odd[part])
                    )
        start = (rows // 2 + quad) * times
        for part in range(parts):
            out_ref[2 * part, start : start + times, :] = even[part]
            out_ref[2 * part + 1, start : start + times, :] = odd[part]


def reach(distance):
    halo = 2 * HALO - distance
    margin = 0 if halo == 0 else 4 if halo <= 4 else 8 if halo <= 8 else 12
    return SIDE - margin, SIDE + LANES // 2 + margin


def sent_places(distances, start):
    places = {}
    for distance in distances:
        places[distance] = start
        first, last = reach(distance)
        start += last - first
    return places, start


def near_places(rows):
    return sent_places(range(rows, 0, -1), 3 * rows)


def far_places(rows):
    places, end = sent_places(range(rows + 1, rows + FAR + 1), SUB)
    return places, end + SIDE


def forward_kernel(
    rows, times, length, cas_ref, field_ref, local_ref,
    out_ref, up_ref, down_ref, far_up_ref, far_down_ref, line_ref,
):
    half = LANES // 2
    span = half + 2 * SIDE
    pieces = field_ref.shape[1] // times
    group = LANES // (2 * SIDE)
    for piece in range(pieces):
        block = field_ref[:, piece * times : (piece + 1) * times, :].reshape(length, LANES)
        freq = exact_dot(block, cas_ref[...], 0, 0)
        if piece < rows // 2:
            for part in range(2):
                start = (2 * piece + part) * span + SIDE
                line_ref[start : start + half, :] = freq[part * half : (part + 1) * half]
        else:
            for index in range(group):
                start = ((piece - rows // 2) * group + index) * span
                place = 2 * SIDE * index
                line_ref[start : start + SIDE, :] = freq[place : place + SIDE]
                line_ref[start + SIDE + half : start + span, :] = freq[
                    place + SIDE : place + 2 * SIDE
                ]
    skip = (span - WINDOW) // 2
    for row in range(rows):
        for column in range(BLOCK):
            value = line_ref[pl.ds(row * span + skip + column, SUB, stride=BLOCK), :]
            out_ref[row * BLOCK + column] = value
    for plane in range(3):
        out_ref[rows * BLOCK + plane] = local_ref[plane * rows : (plane + 1) * rows, :]
    near, far = near_places(rows)[0], far_places(rows)[0]
    for ref, places, row_of in (
        (up_ref, near, lambda distance: rows - distance),
        (down_ref, near, lambda distance: distance - 1),
        (far_up_ref, far, lambda distance: 2 * rows - distance),
        (far_down_ref, far, lambda distance: distance - 1 - rows),
    ):
        for distance, place in places.items():
            first, last = reach(distance)
            start = row_of(distance) * span
            ref[place : place + last - first, :] = line_ref[start + first : start + last, :]
    up_ref[: 3 * rows, :] = local_ref[...]
    down_ref[: 3 * rows, :] = local_ref[...]
    for ref, first in ((far_up_ref, rows - FAR), (far_down_ref, 0)):
        ref[ref.shape[0] - SIDE :, :] = jnp.zeros((SIDE, LANES), jnp.float32)
        kept = [local_ref[plane * rows + first : plane * rows + first + FAR, :] for plane in range(3)]
        kept.append(jnp.zeros((SUB - 3 * FAR, LANES), jnp.float32))
        ref[:SUB, :] = jnp.concatenate(kept, axis=0)


def weight_lines(parts, scratch_ref):
    planes = [jnp.concatenate(blocks, axis=0) for blocks in zip(*parts)]
    east = 1.0 + 0.125 * (planes[1] + jnp.concatenate([planes[1][1:], planes[1][:1]], axis=0))
    north = 1.0 + 0.125 * (planes[2] + pltpu.roll(planes[2], LANES - 1, 1))
    zero = jnp.zeros((LANES - 3 * planes[0].shape[0], LANES), jnp.float32)
    scratch_ref[...] = jnp.transpose(jnp.concatenate([planes[0], east, north, zero], axis=0))
    skip = (LANES - WINDOW) // 2
    return [scratch_ref[pl.ds(skip + column, SUB, stride=BLOCK), :] for column in range(BLOCK)]


def weight_part(ref, rows):
    return [ref[plane * rows : (plane + 1) * rows, :] for plane in range(3)]


def own_weight_part(field_ref, rows):
    return [field_ref[rows * BLOCK + plane] for plane in range(3)]


def received(ref, places, distance, column):
    skip = (LANES // 2 + 2 * SIDE - WINDOW) // 2
    start = places[distance] - reach(distance)[0] + skip + column
    return ref[pl.ds(start, SUB, stride=BLOCK), :]


def spread(lines, index, plane, coef):
    value = jnp.broadcast_to(lines[:, index : index + 1], (SUB, LANES))
    return value + coef[0] if plane == 0 else value


def own_columns(column):
    place = lax.broadcasted_iota(jnp.int32, (SUB, LANES), 0) * BLOCK + column
    first = (WINDOW - LANES // 2) // 2
    return (place >= first) & (place < first + LANES // 2)


def stencil(weight, row, above, here, below, flux=None):
    columns = range(BLOCK)
    if flux is None:
        flux = [weight(1, row - 1, column) * (above[column] - here[column]) for column in columns]
    ahead = [weight(1, row, column) * (here[column] - below[column]) for column in columns]
    beside = here[1:] + [pltpu.roll(here[0], SUB - 1, 0)]
    side = [weight(2, row, column) * (here[column] - beside[column]) for column in columns]
    behind = [pltpu.roll(side[-1], 1, 0)] + side[:-1]
    applied = [
        weight(0, row, column) * here[column]
        + (ahead[column] - flux[column])
        + (side[column] - behind[column])
        for column in columns
    ]
    return applied, ahead


def passes(
    edge, own, total, source, weight, coef, step_ref, remain_ref, solved_ref, emit, border=None
):
    columns = range(BLOCK)

    for turn in range(CHEB + 1):
        first, last = edge + turn + 1, total - edge - turn - 1

        def load(row, turn=turn):
            if turn == 0:
                return [coef[1] * source(row, column) for column in columns]
            return [step_ref[row, column] for column in columns]

        above, here = load(first - 1), load(first)
        flux = None
        for row in range(first, last):
            below = load(row + 1)
            if border and row == first:
                border(0, turn, here)
            if border and row == last - 1:
                border(1, turn, here)
            applied, flux = stencil(weight, row, above, here, below, flux)
            inside = row in range(*own)
            results = []
            for column in columns:
                before = source(row, column) if turn == 0 else remain_ref[row, column]
                left = before - applied[column]
                if turn < CHEB:
                    remain_ref[row, column] = left
                    step_ref[row, column] = (
                        coef[2 + 2 * turn] * here[column] + coef[3 + 2 * turn] * left
                    )
                solved = None
                if inside:
                    place = row - own[0]
                    solved = here[column]
                    if turn > 0:
                        solved = solved_ref[place, column] + solved
                    if turn < CHEB:
                        solved_ref[place, column] = solved
                if turn == CHEB:
                    begun = source(row, column)
                    results.append((begun, solved, begun - left))
            if turn == CHEB:
                emit(row, *zip(*results))
            above, here = here, below


def add_products(sums, index, one, two):
    for column in range(BLOCK):
        product = one[column] * two[column]
        sums[index] = sums[index] + jnp.where(own_columns(column), product, 0.0)


def near_kernel(
    rows, top_ref, field_ref, bottom_ref, coef_ref,
    solved_ref, middle_ref, step_ref, remain_ref, border_ref, wide_ref, early_ref,
    part_ref, scratch_ref,
):
    parts = [
        weight_part(top_ref, rows),
        own_weight_part(field_ref, rows),
        weight_part(bottom_ref, rows),
    ]
    lines = weight_lines(parts, scratch_ref)
    places = near_places(rows)[0]
    coef = [coef_ref[index] for index in range(2 + 2 * CHEB)]
    total = 3 * rows + 2 * FAR
    own = (FAR + rows, FAR + 2 * rows)
    made = set()

    def weight(plane, row, column):
        place = plane * BLOCK + column
        if (row, place) not in made:
            made.add((row, place))
            wide_ref[row, place] = spread(lines[column], plane * 3 * rows + row - FAR, plane, coef)
        return wide_ref[row, place]

    def source(row, column):
        if row < own[0]:
            return received(top_ref, places, own[0] - row, column)
        if row >= own[1]:
            return received(bottom_ref, places, row - own[1] + 1, column)
        return field_ref[(row - own[0]) * BLOCK + column]

    sums = [jnp.zeros((SUB, LANES), jnp.float32) for _ in range(2)]

    def emit(row, begun, solved, applied):
        for column in range(BLOCK):
            middle_ref[row, column] = applied[column]
        if row in range(*own):
            for column in range(BLOCK):
                solved_ref[row - own[0], column] = solved[column]
            add_products(sums, 0, begun, solved)
            add_products(sums, 1, solved, applied)

    def border(side, turn, step):
        for column in range(BLOCK):
            border_ref[side, turn, column] = step[column]

    passes(
        FAR, own, total, source, weight, coef, step_ref, remain_ref, part_ref, emit, border
    )
    early_ref[0] = sums[0]
    early_ref[1] = sums[1]


def far_kernel(
    rows, top_far_ref, top_ref, field_ref, bottom_ref, bottom_far_ref, coef_ref,
    middle_ref, frozen_step_ref, frozen_remain_ref, border_ref, wide_ref, early_ref,
    solved_ref, applied_ref, sums_ref,
    step_ref, remain_ref, part_ref, outer_ref, scratch_ref,
):
    columns = range(BLOCK)
    parts = [
        weight_part(top_far_ref, FAR),
        weight_part(top_ref, rows),
        own_weight_part(field_ref, rows),
        weight_part(bottom_ref, rows),
        weight_part(bottom_far_ref, FAR),
    ]
    lines = weight_lines(parts, scratch_ref)
    coef = [coef_ref[index] for index in range(2 + 2 * CHEB)]
    total = 3 * rows + 2 * FAR
    own = (FAR + rows, FAR + 2 * rows)
    near, far = near_places(rows)[0], far_places(rows)[0]
    made = {}

    def weight(plane, row, column):
        if FAR < row < total - FAR - 1 or (plane == 1 and row == FAR):
            return wide_ref[row, plane * BLOCK + column]
        key = (plane, row, column)
        if key not in made:
            made[key] = spread(lines[column], plane * total + row, plane, coef)
        return made[key]

    def source(row):
        distance = own[0] - row if row < own[0] else row - own[1] + 1
        if distance > rows:
            ref, places = (top_far_ref if row < own[0] else bottom_far_ref), far
        else:
            ref, places = (top_ref if row < own[0] else bottom_ref), near
        return [received(ref, places, distance, column) for column in columns]

    for side in range(2):

        def at(index, side=side):
            return total - 1 - index if side else index

        ends = [[coef[1] * value for value in source(at(index))] for index in range(FAR)]
        rest = source(at(1))
        for turn in range(CHEB + 1):
            edge_row = at(turn + 2)
            if turn == 0:
                inner = [coef[1] * value for value in source(edge_row)]
                inner_rest = source(edge_row)
            else:
                inner = [frozen_step_ref[edge_row, column] for column in columns]
                inner_rest = [frozen_remain_ref[edge_row, column] for column in columns]
            steps = ends + [inner, [border_ref[side, turn, column] for column in columns]]
            new_ends, new_rest = [], []
            for index, before in ((1, rest), (2, inner_rest)):
                row = at(turn + index)
                outside, inside = steps[index - 1], steps[index + 1]
                above, below = (inside, outside) if side else (outside, inside)
                here = steps[index]
                applied, _ = stencil(weight, row, above, here, below)
                left = [before[column] - applied[column] for column in columns]
                new_rest.append(left)
                if turn < CHEB:
                    new_ends.append(
                        [
                            coef[2 + 2 * turn] * here[column] + coef[3 + 2 * turn] * left[column]
                            for column in columns
                        ]
                    )
                else:
                    begun = source(row)
                    for column in columns:
                        outer_ref[side * FAR + index - 1, column] = begun[column] - left[column]
            ends, rest = new_ends, new_rest[1]

    def middle(row, column):
        index = min(row, total - 1 - row)
        if index < HALO + FAR:
            return outer_ref[FAR * (row > index) + index - HALO, column]
        return middle_ref[row, column]

    sums = [early_ref[0], early_ref[1]] + [jnp.zeros((SUB, LANES), jnp.float32) for _ in range(2)]

    def emit(row, begun, solved, applied):
        for column in columns:
            solved_ref[row - own[0], column] = solved[column]
            applied_ref[row - own[0], column] = applied[column]
        add_products(sums, 2, begun, solved)
        add_products(sums, 3, solved, applied)

    passes(HALO, own, total, middle, weight, coef, step_ref, remain_ref, part_ref, emit)

    lane = lane_index((1, LANES))
    line = jnp.zeros((1, LANES), jnp.float32)
    for index in range(4):
        line = jnp.where(lane == index, jnp.sum(sums[index]), line)
    sums_ref[...] = jnp.broadcast_to(line[None], sums_ref.shape)


def inverse_kernel(
    rows, times, length, cas_ref, sums_ref, one_ref, two_ref, three_ref, four_ref, out_ref, line_ref
):
    half = LANES // 2
    span = half + 2 * SIDE
    skip = (span - WINDOW) // 2
    line = jnp.sum(sums_ref[...].reshape(sums_ref.shape[0], LANES), axis=0, keepdims=True)
    gamma, curved, cross, last = (
        jnp.broadcast_to(line[:, index : index + 1], (SUB, LANES)) for index in range(4)
    )
    step = gamma / curved
    gamma_next = step * step * cross - gamma
    turn = gamma_next / gamma
    grown = 1.0 + turn
    next_curved = grown * grown * curved - 2.0 * step * grown * cross + step * step * last
    next_step = gamma_next / next_curved
    first = step + next_step * grown
    second = -next_step * step
    for row in range(rows):
        for index, (left_ref, right_ref) in enumerate(((one_ref, two_ref), (three_ref, four_ref))):
            offset = left_ref.shape[0] // 2 - rows // 2
            for column in range(BLOCK):
                start = (2 * row + index) * span + skip + column
                value = first * left_ref[offset + row, column] + second * right_ref[row, column]
                line_ref[pl.ds(start, SUB, stride=BLOCK), :] = value
    for row in range(rows):
        start = 2 * row * span + SIDE
        points = jnp.concatenate(
            [line_ref[start : start + half, :], line_ref[start + span : start + span + half, :]],
            axis=0,
        )
        back = exact_dot(cas_ref[...], points, 1, 1).reshape(length // times, times, LANES)
        out_ref[:, row * times : (row + 1) * times, :] = back


def final_kernel(rows, times, tiles, source_ref, field_ref, solution_ref, residual_ref):
    half = LANES // 2
    low = lane_index((rows, LANES)) < half
    for time in range(times):
        place = slice(time * rows, (time + 1) * rows)
        taken = pl.ds(time, rows, stride=times)
        for pair in range(tiles // 2):
            columns = slice(pair * LANES, (pair + 1) * LANES)
            left = source_ref[2 * pair, taken, :]
            right = source_ref[2 * pair + 1, taken, :]
            solution_ref[place, columns] = jnp.where(low, left, pltpu.roll(right, half, 1))
            change = jnp.where(low, pltpu.roll(left, half, 1), right)
            residual_ref[place, columns] = field_ref[place, columns] - change


def call(kernel, out_shape, scratch=()):
    shapes = [jax.ShapeDtypeStruct(shape, jnp.float32) for shape in out_shape]
    return pl.pallas_call(
        kernel,
        out_shape=shapes[0] if len(shapes) == 1 else shapes,
        scratch_shapes=[pltpu.VMEM(shape, jnp.float32) for shape in scratch],
        compiler_params=PARAMS,
    )


def shift(value, distance, spaces):
    return lax.ppermute(value, "space", [(i, (i + distance) % spaces) for i in range(spaces)])


def shards(right_side, kappa, velocity):
    tiles = lax.axis_size("tm")
    spaces = lax.axis_size("space")
    times, rows, width = right_side.shape
    length = times * tiles
    tile = width // tiles
    around = (LANES - tile) // 2
    cas_table = jnp.asarray(hartley_table(length))
    coef_table = jnp.asarray(chebyshev_table(length))

    field = right_side.reshape(times * rows, width)
    windows = call(
        functools.partial(window_kernel, rows, times, tiles),
        [(tiles, 6 * times, LANES)],
        [(width // LANES, times * rows, LANES)],
    )(field)
    gathered = lax.all_to_all(windows, "tm", 0, 0)

    squares = velocity.astype(jnp.float32) ** 2
    planes = jnp.concatenate([kappa, squares[0], squares[1]], axis=0)
    planes = jnp.concatenate([planes[:, -around:], planes, planes[:, :around]], axis=1)
    local = lax.dynamic_slice_in_dim(planes, lax.axis_index("tm") * tile, LANES, 1)
    total = 3 * rows + 2 * FAR
    tile_shape = (rows, BLOCK, SUB, LANES)
    near_shape = (near_places(rows)[1], LANES)
    far_shape = (far_places(rows)[1], LANES)
    span = LANES // 2 + 2 * SIDE
    freq, up, down, far_up, far_down = call(
        functools.partial(forward_kernel, rows, times, length),
        [(rows * BLOCK + 3, SUB, LANES), near_shape, near_shape, far_shape, far_shape],
        [(rows * span, LANES)],
    )(cas_table, gathered, local)
    top, bottom = shift(up, 1, spaces), shift(down, -1, spaces)
    top_far, bottom_far = shift(far_up, 2, spaces), shift(far_down, -2, spaces)

    groups = [
        [i * spaces + first + j for i in range(tiles) for j in range(NEAR)]
        for first in range(0, spaces, NEAR)
    ]
    work = (total, BLOCK, SUB, LANES)
    solved, middle, step, remain, border, wide, early = call(
        functools.partial(near_kernel, rows),
        [
            tile_shape,
            work,
            work,
            work,
            (2, CHEB + 1, BLOCK, SUB, LANES),
            (total, 3 * BLOCK, SUB, LANES),
            (2, SUB, LANES),
        ],
        [tile_shape, (LANES, LANES)],
    )(top, freq, bottom, coef_table)
    solved_two, applied_two, sums = call(
        functools.partial(far_kernel, rows),
        [tile_shape, tile_shape, (tiles * NEAR, 1, LANES)],
        [work, work, tile_shape, (2 * FAR, BLOCK, SUB, LANES), (LANES, LANES)],
    )(
        top_far, top, freq, bottom, bottom_far, coef_table, middle, step, remain, border, wide, early
    )
    sums = lax.all_to_all(sums, ("tm", "space"), 0, 0, axis_index_groups=groups)
    planes = spaces // NEAR
    groups = [[first + NEAR * i for i in range(planes)] for first in range(NEAR)]
    sums = jnp.broadcast_to(jnp.sum(sums, axis=0)[None], (planes, 1, LANES))
    sums = lax.all_to_all(sums, "space", 0, 0, axis_index_groups=groups)
    packed = call(
        functools.partial(inverse_kernel, rows, times, length),
        [(tiles, rows * times, LANES)],
        [(rows * 2 * span, LANES)],
    )(cas_table, sums, solved, solved_two, middle, applied_two)
    returned = lax.all_to_all(packed, "tm", 0, 0)

    solution, residual = call(
        functools.partial(final_kernel, rows, times, tiles),
        [(times * rows, width), (times * rows, width)],
    )(returned, field)
    shape = right_side.shape
    return solution.reshape(shape), residual.reshape(shape)


def solution(mesh):
    placed = (P("tm", "space", None), P("space", None), P(None, "space", None))
    return jax.shard_map(
        shards,
        mesh=mesh,
        in_specs=placed,
        out_specs=(P("tm", "space", None), P("tm", "space", None)),
        check_vma=False,
    )
```

```python
import functools
import math

import jax
import jax.numpy as jnp
import numpy as np
from jax import lax
from jax.experimental import pallas as pl
from jax.experimental.pallas import tpu as pltpu
from jax.sharding import PartitionSpec as P

CHEB = 4
COUPLING = 2.0
KAPPA_LOW = 0.05
KAPPA_HIGH = 1.0
REACH = 16.0

LANES = 128
SUB = 8
HALO = CHEB + 1
FAR = 2
SIDE = 16
BLOCK = 11
WINDOW = SUB * BLOCK
NEAR = 4
PARAMS = pltpu.CompilerParams(vmem_limit_bytes=24 * 1024 * 1024)


def hartley_table(length):
    index = np.arange(length)
    angle = (index[:, None] * index[None, :] % length) * (2.0 * math.pi / length)
    return ((np.cos(angle) + np.sin(angle)) / math.sqrt(length)).astype(np.float32)


def chebyshev_table(length):
    shift = COUPLING * (2.0 - 2.0 * np.cos(2.0 * math.pi * np.arange(length) / length))
    half = 0.5 * (KAPPA_HIGH + REACH - KAPPA_LOW)
    mid = 0.5 * (KAPPA_LOW + KAPPA_HIGH + REACH) + shift
    ratio = mid / half
    damp = 1.0 / ratio
    lines = [shift, 1.0 / mid]
    for _ in range(CHEB):
        damp_next = 1.0 / (2.0 * ratio - damp)
        lines += [damp_next * damp, 2.0 * damp_next / half]
        damp = damp_next
    return np.repeat(np.stack(lines).astype(np.float32)[:, None], SUB, 1)


def lane_index(shape):
    return lax.broadcasted_iota(jnp.int32, shape, len(shape) - 1)


def exact_dot(left, right, left_dim, right_dim):
    return lax.dot_general(
        left,
        right,
        (((left_dim,), (right_dim,)), ((), ())),
        precision=lax.Precision.HIGHEST,
        preferred_element_type=jnp.float32,
    )


def window_kernel(rows, times, tiles, source_ref, out_ref, scratch_ref):
    half = LANES // 2
    parts = source_ref.shape[1] // LANES
    for part in range(parts):
        scratch_ref[part] = source_ref[:, part * LANES : (part + 1) * LANES]
    lane = lane_index((times, LANES))
    fields = [
        [scratch_ref[part, pl.ds(row, times, stride=rows), :] for part in range(parts)]
        for row in range(rows)
    ]
    for pair in range(rows // 2):
        for part in range(parts):
            one, two = fields[2 * pair][part], fields[2 * pair + 1][part]
            place = slice(pair * times, (pair + 1) * times)
            out_ref[2 * part, place, :] = jnp.where(lane < half, one, pltpu.roll(two, half, 1))
            out_ref[2 * part + 1, place, :] = jnp.where(lane < half, pltpu.roll(one, half, 1), two)
    spread = 2 * SIDE
    group = LANES // spread
    for quad in range(rows // group):
        even = [None] * parts
        odd = [None] * parts
        for index in range(group):
            row = quad * group + index
            wide = jnp.concatenate(fields[row], axis=1)
            near = pltpu.roll(wide, spread * index + SIDE, 1)
            away = pltpu.roll(wide, (spread * index - half + SIDE) % wide.shape[1], 1)
            left = (lane >= spread * index) & (lane < spread * index + SIDE)
            right = (lane >= spread * index + SIDE) & (lane < spread * (index + 1))
            for part in range(parts):
                here = slice(part * LANES, (part + 1) * LANES)
                then = (part + 1) % parts
                then = slice(then * LANES, (then + 1) * LANES)
                if index == 0:
                    even[part] = jnp.where(left, near[:, here], away[:, here])
                    odd[part] = jnp.where(left, away[:, here], near[:, then])
                else:
                    even[part] = jnp.where(
                        left, near[:, here], jnp.where(right, away[:, here], even[part])
                    )
                    odd[part] = jnp.where(
                        left, away[:, here], jnp.where(right, near[:, then], odd[part])
                    )
        start = (rows // 2 + quad) * times
        for part in range(parts):
            out_ref[2 * part, start : start + times, :] = even[part]
            out_ref[2 * part + 1, start : start + times, :] = odd[part]


def reach(distance):
    halo = 2 * HALO - distance
    margin = 0 if halo == 0 else 4 if halo <= 4 else 8 if halo <= 8 else 12
    return SIDE - margin, SIDE + LANES // 2 + margin


def sent_places(distances, start):
    places = {}
    for distance in distances:
        places[distance] = start
        first, last = reach(distance)
        start += last - first
    return places, start


def near_places(rows):
    return sent_places(range(rows, 0, -1), 3 * rows)


def far_places(rows):
    places, end = sent_places(range(rows + 1, rows + FAR + 1), SUB)
    return places, end + SIDE


def forward_kernel(
    rows, times, length, cas_ref, field_ref, local_ref,
    out_ref, up_ref, down_ref, far_up_ref, far_down_ref, line_ref,
):
    half = LANES // 2
    span = half + 2 * SIDE
    pieces = field_ref.shape[1] // times
    group = LANES // (2 * SIDE)
    for piece in range(pieces):
        block = field_ref[:, piece * times : (piece + 1) * times, :].reshape(length, LANES)
        freq = exact_dot(block, cas_ref[...], 0, 0)
        if piece < rows // 2:
            for part in range(2):
                start = (2 * piece + part) * span + SIDE
                line_ref[start : start + half, :] = freq[part * half : (part + 1) * half]
        else:
            for index in range(group):
                start = ((piece - rows // 2) * group + index) * span
                place = 2 * SIDE * index
                line_ref[start : start + SIDE, :] = freq[place : place + SIDE]
                line_ref[start + SIDE + half : start + span, :] = freq[
                    place + SIDE : place + 2 * SIDE
                ]
    skip = (span - WINDOW) // 2
    for row in range(rows):
        for column in range(BLOCK):
            value = line_ref[pl.ds(row * span + skip + column, SUB, stride=BLOCK), :]
            out_ref[row * BLOCK + column] = value
    for plane in range(3):
        out_ref[rows * BLOCK + plane] = local_ref[plane * rows : (plane + 1) * rows, :]
    near, far = near_places(rows)[0], far_places(rows)[0]
    for ref, places, row_of in (
        (up_ref, near, lambda distance: rows - distance),
        (down_ref, near, lambda distance: distance - 1),
        (far_up_ref, far, lambda distance: 2 * rows - distance),
        (far_down_ref, far, lambda distance: distance - 1 - rows),
    ):
        for distance, place in places.items():
            first, last = reach(distance)
            start = row_of(distance) * span
            ref[place : place + last - first, :] = line_ref[start + first : start + last, :]
    up_ref[: 3 * rows, :] = local_ref[...]
    down_ref[: 3 * rows, :] = local_ref[...]
    for ref, first in ((far_up_ref, rows - FAR), (far_down_ref, 0)):
        ref[ref.shape[0] - SIDE :, :] = jnp.zeros((SIDE, LANES), jnp.float32)
        kept = [local_ref[plane * rows + first : plane * rows + first + FAR, :] for plane in range(3)]
        kept.append(jnp.zeros((SUB - 3 * FAR, LANES), jnp.float32))
        ref[:SUB, :] = jnp.concatenate(kept, axis=0)


def weight_lines(parts, scratch_ref):
    planes = [jnp.concatenate(blocks, axis=0) for blocks in zip(*parts)]
    east = 1.0 + 0.125 * (planes[1] + jnp.concatenate([planes[1][1:], planes[1][:1]], axis=0))
    north = 1.0 + 0.125 * (planes[2] + pltpu.roll(planes[2], LANES - 1, 1))
    zero = jnp.zeros((LANES - 3 * planes[0].shape[0], LANES), jnp.float32)
    scratch_ref[...] = jnp.transpose(jnp.concatenate([planes[0], east, north, zero], axis=0))
    skip = (LANES - WINDOW) // 2
    return [scratch_ref[pl.ds(skip + column, SUB, stride=BLOCK), :] for column in range(BLOCK)]


def weight_part(ref, rows):
    return [ref[plane * rows : (plane + 1) * rows, :] for plane in range(3)]


def own_weight_part(field_ref, rows):
    return [field_ref[rows * BLOCK + plane] for plane in range(3)]


def received(ref, places, distance, column):
    skip = (LANES // 2 + 2 * SIDE - WINDOW) // 2
    start = places[distance] - reach(distance)[0] + skip + column
    return ref[pl.ds(start, SUB, stride=BLOCK), :]


def spread(lines, index, plane, coef):
    value = jnp.broadcast_to(lines[:, index : index + 1], (SUB, LANES))
    return value + coef[0] if plane == 0 else value


def own_columns(column):
    place = lax.broadcasted_iota(jnp.int32, (SUB, LANES), 0) * BLOCK + column
    first = (WINDOW - LANES // 2) // 2
    return (place >= first) & (place < first + LANES // 2)


def stencil(weight, row, above, here, below, flux=None):
    columns = range(BLOCK)
    if flux is None:
        flux = [weight(1, row - 1, column) * (above[column] - here[column]) for column in columns]
    ahead = [weight(1, row, column) * (here[column] - below[column]) for column in columns]
    beside = here[1:] + [pltpu.roll(here[0], SUB - 1, 0)]
    side = [weight(2, row, column) * (here[column] - beside[column]) for column in columns]
    behind = [pltpu.roll(side[-1], 1, 0)] + side[:-1]
    applied = [
        weight(0, row, column) * here[column]
        + (ahead[column] - flux[column])
        + (side[column] - behind[column])
        for column in columns
    ]
    return applied, ahead


def passes(
    edge, own, total, source, weight, coef, step_ref, remain_ref, solved_ref, emit, border=None
):
    columns = range(BLOCK)

    for turn in range(CHEB + 1):
        first, last = edge + turn + 1, total - edge - turn - 1

        def load(row, turn=turn):
            if turn == 0:
                return [coef[1] * source(row, column) for column in columns]
            return [step_ref[row, column] for column in columns]

        above, here = load(first - 1), load(first)
        flux = None
        for row in range(first, last):
            below = load(row + 1)
            if border and row == first:
                border(0, turn, here)
            if border and row == last - 1:
                border(1, turn, here)
            applied, flux = stencil(weight, row, above, here, below, flux)
            inside = row in range(*own)
            results = []
            for column in columns:
                before = source(row, column) if turn == 0 else remain_ref[row, column]
                left = before - applied[column]
                if turn < CHEB:
                    remain_ref[row, column] = left
                    step_ref[row, column] = (
                        coef[2 + 2 * turn] * here[column] + coef[3 + 2 * turn] * left
                    )
                solved = None
                if inside:
                    place = row - own[0]
                    solved = here[column]
                    if turn > 0:
                        solved = solved_ref[place, column] + solved
                    if turn < CHEB:
                        solved_ref[place, column] = solved
                if turn == CHEB:
                    begun = source(row, column)
                    results.append((begun, solved, begun - left))
            if turn == CHEB:
                emit(row, *zip(*results))
            above, here = here, below


def add_products(sums, index, one, two):
    for column in range(BLOCK):
        product = one[column] * two[column]
        sums[index] = sums[index] + jnp.where(own_columns(column), product, 0.0)


def near_kernel(
    rows, top_ref, field_ref, bottom_ref, coef_ref,
    solved_ref, middle_ref, step_ref, remain_ref, border_ref, wide_ref, early_ref,
    part_ref, scratch_ref,
):
    parts = [
        weight_part(top_ref, rows),
        own_weight_part(field_ref, rows),
        weight_part(bottom_ref, rows),
    ]
    lines = weight_lines(parts, scratch_ref)
    places = near_places(rows)[0]
    coef = [coef_ref[index] for index in range(2 + 2 * CHEB)]
    total = 3 * rows + 2 * FAR
    own = (FAR + rows, FAR + 2 * rows)
    made = set()

    def weight(plane, row, column):
        place = plane * BLOCK + column
        if (row, place) not in made:
            made.add((row, place))
            wide_ref[row, place] = spread(lines[column], plane * 3 * rows + row - FAR, plane, coef)
        return wide_ref[row, place]

    def source(row, column):
        if row < own[0]:
            return received(top_ref, places, own[0] - row, column)
        if row >= own[1]:
            return received(bottom_ref, places, row - own[1] + 1, column)
        return field_ref[(row - own[0]) * BLOCK + column]

    sums = [jnp.zeros((SUB, LANES), jnp.float32) for _ in range(2)]

    def emit(row, begun, solved, applied):
        for column in range(BLOCK):
            middle_ref[row, column] = applied[column]
        if row in range(*own):
            for column in range(BLOCK):
                solved_ref[row - own[0], column] = solved[column]
            add_products(sums, 0, begun, solved)
            add_products(sums, 1, solved, applied)

    def border(side, turn, step):
        for column in range(BLOCK):
            border_ref[side, turn, column] = step[column]

    passes(
        FAR, own, total, source, weight, coef, step_ref, remain_ref, part_ref, emit, border
    )
    early_ref[0] = sums[0]
    early_ref[1] = sums[1]


def far_kernel(
    rows, top_far_ref, top_ref, field_ref, bottom_ref, bottom_far_ref, coef_ref,
    middle_ref, frozen_step_ref, frozen_remain_ref, border_ref, wide_ref, early_ref,
    solved_ref, applied_ref, sums_ref,
    step_ref, remain_ref, part_ref, outer_ref, scratch_ref,
):
    columns = range(BLOCK)
    parts = [
        weight_part(top_far_ref, FAR),
        weight_part(top_ref, rows),
        own_weight_part(field_ref, rows),
        weight_part(bottom_ref, rows),
        weight_part(bottom_far_ref, FAR),
    ]
    lines = weight_lines(parts, scratch_ref)
    coef = [coef_ref[index] for index in range(2 + 2 * CHEB)]
    total = 3 * rows + 2 * FAR
    own = (FAR + rows, FAR + 2 * rows)
    near, far = near_places(rows)[0], far_places(rows)[0]
    made = {}

    def weight(plane, row, column):
        if FAR < row < total - FAR - 1 or (plane == 1 and row == FAR):
            return wide_ref[row, plane * BLOCK + column]
        key = (plane, row, column)
        if key not in made:
            made[key] = spread(lines[column], plane * total + row, plane, coef)
        return made[key]

    def source(row):
        distance = own[0] - row if row < own[0] else row - own[1] + 1
        if distance > rows:
            ref, places = (top_far_ref if row < own[0] else bottom_far_ref), far
        else:
            ref, places = (top_ref if row < own[0] else bottom_ref), near
        return [received(ref, places, distance, column) for column in columns]

    for side in range(2):

        def at(index, side=side):
            return total - 1 - index if side else index

        ends = [[coef[1] * value for value in source(at(index))] for index in range(FAR)]
        rest = source(at(1))
        for turn in range(CHEB + 1):
            edge_row = at(turn + 2)
            if turn == 0:
                inner = [coef[1] * value for value in source(edge_row)]
                inner_rest = source(edge_row)
            else:
                inner = [frozen_step_ref[edge_row, column] for column in columns]
                inner_rest = [frozen_remain_ref[edge_row, column] for column in columns]
            steps = ends + [inner, [border_ref[side, turn, column] for column in columns]]
            new_ends, new_rest = [], []
            for index, before in ((1, rest), (2, inner_rest)):
                row = at(turn + index)
                outside, inside = steps[index - 1], steps[index + 1]
                above, below = (inside, outside) if side else (outside, inside)
                here = steps[index]
                applied, _ = stencil(weight, row, above, here, below)
                left = [before[column] - applied[column] for column in columns]
                new_rest.append(left)
                if turn < CHEB:
                    new_ends.append(
                        [
                            coef[2 + 2 * turn] * here[column] + coef[3 + 2 * turn] * left[column]
                            for column in columns
                        ]
                    )
                else:
                    begun = source(row)
                    for column in columns:
                        outer_ref[side * FAR + index - 1, column] = begun[column] - left[column]
            ends, rest = new_ends, new_rest[1]

    def middle(row, column):
        index = min(row, total - 1 - row)
        if index < HALO + FAR:
            return outer_ref[FAR * (row > index) + index - HALO, column]
        return middle_ref[row, column]

    sums = [early_ref[0], early_ref[1]] + [jnp.zeros((SUB, LANES), jnp.float32) for _ in range(2)]

    def emit(row, begun, solved, applied):
        for column in columns:
            solved_ref[row - own[0], column] = solved[column]
            applied_ref[row - own[0], column] = applied[column]
        add_products(sums, 2, begun, solved)
        add_products(sums, 3, solved, applied)

    passes(HALO, own, total, middle, weight, coef, step_ref, remain_ref, part_ref, emit)

    lane = lane_index((1, LANES))
    line = jnp.zeros((1, LANES), jnp.float32)
    for index in range(4):
        line = jnp.where(lane == index, jnp.sum(sums[index]), line)
    sums_ref[...] = jnp.broadcast_to(line[None], sums_ref.shape)


def inverse_kernel(
    rows, times, length, cas_ref, sums_ref, one_ref, two_ref, three_ref, four_ref, out_ref, line_ref
):
    half = LANES // 2
    span = half + 2 * SIDE
    skip = (span - WINDOW) // 2
    line = jnp.sum(sums_ref[...].reshape(sums_ref.shape[0], LANES), axis=0, keepdims=True)
    gamma, curved, cross, last = (
        jnp.broadcast_to(line[:, index : index + 1], (SUB, LANES)) for index in range(4)
    )
    step = gamma / curved
    gamma_next = step * step * cross - gamma
    turn = gamma_next / gamma
    grown = 1.0 + turn
    next_curved = grown * grown * curved - 2.0 * step * grown * cross + step * step * last
    next_step = gamma_next / next_curved
    first = step + next_step * grown
    second = -next_step * step
    for row in range(rows):
        for index, (left_ref, right_ref) in enumerate(((one_ref, two_ref), (three_ref, four_ref))):
            offset = left_ref.shape[0] // 2 - rows // 2
            for column in range(BLOCK):
                start = (2 * row + index) * span + skip + column
                value = first * left_ref[offset + row, column] + second * right_ref[row, column]
                line_ref[pl.ds(start, SUB, stride=BLOCK), :] = value
    points = jnp.concatenate(
        [
            line_ref[index * span + SIDE : index * span + SIDE + half, :]
            for index in range(2 * rows)
        ],
        axis=0,
    )
    back = exact_dot(cas_ref[...], points, 1, 1)
    for row in range(rows):
        piece = back[:, row * LANES : (row + 1) * LANES].reshape(length // times, times, LANES)
        out_ref[:, row * times : (row + 1) * times, :] = piece


def final_kernel(rows, times, tiles, source_ref, field_ref, solution_ref, residual_ref):
    half = LANES // 2
    low = lane_index((rows, LANES)) < half
    for time in range(times):
        place = slice(time * rows, (time + 1) * rows)
        taken = pl.ds(time, rows, stride=times)
        for pair in range(tiles // 2):
            columns = slice(pair * LANES, (pair + 1) * LANES)
            left = source_ref[2 * pair, taken, :]
            right = source_ref[2 * pair + 1, taken, :]
            solution_ref[place, columns] = jnp.where(low, left, pltpu.roll(right, half, 1))
            change = jnp.where(low, pltpu.roll(left, half, 1), right)
            residual_ref[place, columns] = field_ref[place, columns] - change


def call(kernel, out_shape, scratch=()):
    shapes = [jax.ShapeDtypeStruct(shape, jnp.float32) for shape in out_shape]
    return pl.pallas_call(
        kernel,
        out_shape=shapes[0] if len(shapes) == 1 else shapes,
        scratch_shapes=[pltpu.VMEM(shape, jnp.float32) for shape in scratch],
        compiler_params=PARAMS,
    )


def shift(value, distance, spaces):
    return lax.ppermute(value, "space", [(i, (i + distance) % spaces) for i in range(spaces)])


def shards(right_side, kappa, velocity):
    tiles = lax.axis_size("tm")
    spaces = lax.axis_size("space")
    times, rows, width = right_side.shape
    length = times * tiles
    tile = width // tiles
    around = (LANES - tile) // 2
    cas_table = jnp.asarray(hartley_table(length))
    coef_table = jnp.asarray(chebyshev_table(length))

    field = right_side.reshape(times * rows, width)
    windows = call(
        functools.partial(window_kernel, rows, times, tiles),
        [(tiles, 6 * times, LANES)],
        [(width // LANES, times * rows, LANES)],
    )(field)
    gathered = lax.all_to_all(windows, "tm", 0, 0)

    squares = velocity.astype(jnp.float32) ** 2
    planes = jnp.concatenate([kappa, squares[0], squares[1]], axis=0)
    planes = jnp.concatenate([planes[:, -around:], planes, planes[:, :around]], axis=1)
    local = lax.dynamic_slice_in_dim(planes, lax.axis_index("tm") * tile, LANES, 1)
    total = 3 * rows + 2 * FAR
    tile_shape = (rows, BLOCK, SUB, LANES)
    near_shape = (near_places(rows)[1], LANES)
    far_shape = (far_places(rows)[1], LANES)
    span = LANES // 2 + 2 * SIDE
    freq, up, down, far_up, far_down = call(
        functools.partial(forward_kernel, rows, times, length),
        [(rows * BLOCK + 3, SUB, LANES), near_shape, near_shape, far_shape, far_shape],
        [(rows * span, LANES)],
    )(cas_table, gathered, local)
    top, bottom = shift(up, 1, spaces), shift(down, -1, spaces)
    top_far, bottom_far = shift(far_up, 2, spaces), shift(far_down, -2, spaces)

    groups = [
        [i * spaces + first + j for i in range(tiles) for j in range(NEAR)]
        for first in range(0, spaces, NEAR)
    ]
    work = (total, BLOCK, SUB, LANES)
    solved, middle, step, remain, border, wide, early = call(
        functools.partial(near_kernel, rows),
        [
            tile_shape,
            work,
            work,
            work,
            (2, CHEB + 1, BLOCK, SUB, LANES),
            (total, 3 * BLOCK, SUB, LANES),
            (2, SUB, LANES),
        ],
        [tile_shape, (LANES, LANES)],
    )(top, freq, bottom, coef_table)
    solved_two, applied_two, sums = call(
        functools.partial(far_kernel, rows),
        [tile_shape, tile_shape, (tiles * NEAR, 1, LANES)],
        [work, work, tile_shape, (2 * FAR, BLOCK, SUB, LANES), (LANES, LANES)],
    )(
        top_far, top, freq, bottom, bottom_far, coef_table, middle, step, remain, border, wide, early
    )
    sums = lax.all_to_all(sums, ("tm", "space"), 0, 0, axis_index_groups=groups)
    planes = spaces // NEAR
    groups = [[first + NEAR * i for i in range(planes)] for first in range(NEAR)]
    sums = jnp.broadcast_to(jnp.sum(sums, axis=0)[None], (planes, 1, LANES))
    sums = lax.all_to_all(sums, "space", 0, 0, axis_index_groups=groups)
    packed = call(
        functools.partial(inverse_kernel, rows, times, length),
        [(tiles, rows * times, LANES)],
        [(rows * 2 * span, LANES)],
    )(cas_table, sums, solved, solved_two, middle, applied_two)
    returned = lax.all_to_all(packed, "tm", 0, 0)

    solution, residual = call(
        functools.partial(final_kernel, rows, times, tiles),
        [(times * rows, width), (times * rows, width)],
    )(returned, field)
    shape = right_side.shape
    return solution.reshape(shape), residual.reshape(shape)


def solution(mesh):
    placed = (P("tm", "space", None), P("space", None), P(None, "space", None))
    return jax.shard_map(
        shards,
        mesh=mesh,
        in_specs=placed,
        out_specs=(P("tm", "space", None), P("tm", "space", None)),
        check_vma=False,
    )
```

```python
import functools
import math

import jax
import jax.numpy as jnp
import numpy as np
from jax import lax
from jax.experimental import pallas as pl
from jax.experimental.pallas import tpu as pltpu
from jax.sharding import PartitionSpec as P

CHEB = 4
COUPLING = 2.0
KAPPA_LOW = 0.05
KAPPA_HIGH = 1.0
REACH = 16.0

LANES = 128
SUB = 8
HALO = CHEB + 1
FAR = 2
SIDE = 16
BLOCK = 11
WINDOW = SUB * BLOCK
NEAR = 4
PARAMS = pltpu.CompilerParams(vmem_limit_bytes=24 * 1024 * 1024)


def hartley_table(length):
    index = np.arange(length)
    angle = (index[:, None] * index[None, :] % length) * (2.0 * math.pi / length)
    return ((np.cos(angle) + np.sin(angle)) / math.sqrt(length)).astype(np.float32)


def chebyshev_table(length):
    shift = COUPLING * (2.0 - 2.0 * np.cos(2.0 * math.pi * np.arange(length) / length))
    half = 0.5 * (KAPPA_HIGH + REACH - KAPPA_LOW)
    mid = 0.5 * (KAPPA_LOW + KAPPA_HIGH + REACH) + shift
    ratio = mid / half
    damp = 1.0 / ratio
    lines = [shift, 1.0 / mid]
    for _ in range(CHEB):
        damp_next = 1.0 / (2.0 * ratio - damp)
        lines += [damp_next * damp, 2.0 * damp_next / half]
        damp = damp_next
    return np.repeat(np.stack(lines).astype(np.float32)[:, None], SUB, 1)


def lane_index(shape):
    return lax.broadcasted_iota(jnp.int32, shape, len(shape) - 1)


def exact_dot(left, right, left_dim, right_dim):
    return lax.dot_general(
        left,
        right,
        (((left_dim,), (right_dim,)), ((), ())),
        precision=lax.Precision.HIGHEST,
        preferred_element_type=jnp.float32,
    )


def window_kernel(rows, times, tiles, source_ref, out_ref, scratch_ref):
    half = LANES // 2
    parts = source_ref.shape[1] // LANES
    for part in range(parts):
        scratch_ref[part] = source_ref[:, part * LANES : (part + 1) * LANES]
    lane = lane_index((times, LANES))
    fields = [
        [scratch_ref[part, pl.ds(row, times, stride=rows), :] for part in range(parts)]
        for row in range(rows)
    ]
    for pair in range(rows // 2):
        for part in range(parts):
            one, two = fields[2 * pair][part], fields[2 * pair + 1][part]
            place = slice(pair * times, (pair + 1) * times)
            out_ref[2 * part, place, :] = jnp.where(lane < half, one, pltpu.roll(two, half, 1))
            out_ref[2 * part + 1, place, :] = jnp.where(lane < half, pltpu.roll(one, half, 1), two)
    spread = 2 * SIDE
    group = LANES // spread
    for quad in range(rows // group):
        even = [None] * parts
        odd = [None] * parts
        for index in range(group):
            row = quad * group + index
            wide = jnp.concatenate(fields[row], axis=1)
            near = pltpu.roll(wide, spread * index + SIDE, 1)
            away = pltpu.roll(wide, (spread * index - half + SIDE) % wide.shape[1], 1)
            left = (lane >= spread * index) & (lane < spread * index + SIDE)
            right = (lane >= spread * index + SIDE) & (lane < spread * (index + 1))
            for part in range(parts):
                here = slice(part * LANES, (part + 1) * LANES)
                then = (part + 1) % parts
                then = slice(then * LANES, (then + 1) * LANES)
                if index == 0:
                    even[part] = jnp.where(left, near[:, here], away[:, here])
                    odd[part] = jnp.where(left, away[:, here], near[:, then])
                else:
                    even[part] = jnp.where(
                        left, near[:, here], jnp.where(right, away[:, here], even[part])
                    )
                    odd[part] = jnp.where(
                        left, away[:, here], jnp.where(right, near[:, then], odd[part])
                    )
        start = (rows // 2 + quad) * times
        for part in range(parts):
            out_ref[2 * part, start : start + times, :] = even[part]
            out_ref[2 * part + 1, start : start + times, :] = odd[part]


def reach(distance):
    halo = 2 * HALO - distance
    margin = 0 if halo == 0 else 4 if halo <= 4 else 8 if halo <= 8 else 12
    return SIDE - margin, SIDE + LANES // 2 + margin


def sent_places(distances, start):
    places = {}
    for distance in distances:
        places[distance] = start
        first, last = reach(distance)
        start += last - first
    return places, start


def near_places(rows):
    return sent_places(range(rows, 0, -1), 3 * rows)


def far_places(rows):
    places, end = sent_places(range(rows + 1, rows + FAR + 1), SUB)
    return places, end + SIDE


def forward_kernel(
    rows, times, length, cas_ref, field_ref, local_ref,
    out_ref, up_ref, down_ref, far_up_ref, far_down_ref, line_ref,
):
    half = LANES // 2
    span = half + 2 * SIDE
    pieces = field_ref.shape[1] // times
    group = LANES // (2 * SIDE)
    for piece in range(pieces):
        block = field_ref[:, piece * times : (piece + 1) * times, :].reshape(length, LANES)
        freq = exact_dot(block, cas_ref[...], 0, 0)
        if piece < rows // 2:
            for part in range(2):
                start = (2 * piece + part) * span + SIDE
                line_ref[start : start + half, :] = freq[part * half : (part + 1) * half]
        else:
            for index in range(group):
                start = ((piece - rows // 2) * group + index) * span
                place = 2 * SIDE * index
                line_ref[start : start + SIDE, :] = freq[place : place + SIDE]
                line_ref[start + SIDE + half : start + span, :] = freq[
                    place + SIDE : place + 2 * SIDE
                ]
    skip = (span - WINDOW) // 2
    for row in range(rows):
        for column in range(BLOCK):
            value = line_ref[pl.ds(row * span + skip + column, SUB, stride=BLOCK), :]
            out_ref[row * BLOCK + column] = value
    for plane in range(3):
        out_ref[rows * BLOCK + plane] = local_ref[plane * rows : (plane + 1) * rows, :]
    near, far = near_places(rows)[0], far_places(rows)[0]
    for ref, places, row_of in (
        (up_ref, near, lambda distance: rows - distance),
        (down_ref, near, lambda distance: distance - 1),
        (far_up_ref, far, lambda distance: 2 * rows - distance),
        (far_down_ref, far, lambda distance: distance - 1 - rows),
    ):
        for distance, place in places.items():
            first, last = reach(distance)
            start = row_of(distance) * span
            ref[place : place + last - first, :] = line_ref[start + first : start + last, :]
    up_ref[: 3 * rows, :] = local_ref[...]
    down_ref[: 3 * rows, :] = local_ref[...]
    for ref, first in ((far_up_ref, rows - FAR), (far_down_ref, 0)):
        ref[ref.shape[0] - SIDE :, :] = jnp.zeros((SIDE, LANES), jnp.float32)
        kept = [local_ref[plane * rows + first : plane * rows + first + FAR, :] for plane in range(3)]
        kept.append(jnp.zeros((SUB - 3 * FAR, LANES), jnp.float32))
        ref[:SUB, :] = jnp.concatenate(kept, axis=0)


def weight_lines(parts, scratch_ref):
    planes = [jnp.concatenate(blocks, axis=0) for blocks in zip(*parts)]
    east = 1.0 + 0.125 * (planes[1] + jnp.concatenate([planes[1][1:], planes[1][:1]], axis=0))
    north = 1.0 + 0.125 * (planes[2] + pltpu.roll(planes[2], LANES - 1, 1))
    zero = jnp.zeros((LANES - 3 * planes[0].shape[0], LANES), jnp.float32)
    scratch_ref[...] = jnp.transpose(jnp.concatenate([planes[0], east, north, zero], axis=0))
    skip = (LANES - WINDOW) // 2
    return [scratch_ref[pl.ds(skip + column, SUB, stride=BLOCK), :] for column in range(BLOCK)]


def weight_part(ref, rows):
    return [ref[plane * rows : (plane + 1) * rows, :] for plane in range(3)]


def own_weight_part(field_ref, rows):
    return [field_ref[rows * BLOCK + plane] for plane in range(3)]


def received(ref, places, distance, column):
    skip = (LANES // 2 + 2 * SIDE - WINDOW) // 2
    start = places[distance] - reach(distance)[0] + skip + column
    return ref[pl.ds(start, SUB, stride=BLOCK), :]


def spread(lines, index, plane, coef):
    value = jnp.broadcast_to(lines[:, index : index + 1], (SUB, LANES))
    return value + coef[0] if plane == 0 else value


def own_columns(column):
    place = lax.broadcasted_iota(jnp.int32, (SUB, LANES), 0) * BLOCK + column
    first = (WINDOW - LANES // 2) // 2
    return (place >= first) & (place < first + LANES // 2)


def stencil(weight, row, above, here, below, flux=None):
    columns = range(BLOCK)
    if flux is None:
        flux = [weight(1, row - 1, column) * (above[column] - here[column]) for column in columns]
    ahead = [weight(1, row, column) * (here[column] - below[column]) for column in columns]
    beside = here[1:] + [pltpu.roll(here[0], SUB - 1, 0)]
    side = [weight(2, row, column) * (here[column] - beside[column]) for column in columns]
    behind = [pltpu.roll(side[-1], 1, 0)] + side[:-1]
    applied = [
        weight(0, row, column) * here[column]
        + (ahead[column] - flux[column])
        + (side[column] - behind[column])
        for column in columns
    ]
    return applied, ahead


def passes(
    edge, own, total, source, weight, coef, step_ref, remain_ref, solved_ref, emit, border=None
):
    columns = range(BLOCK)

    for turn in range(CHEB + 1):
        first, last = edge + turn + 1, total - edge - turn - 1

        def load(row, turn=turn):
            if turn == 0:
                return [coef[1] * source(row, column) for column in columns]
            return [step_ref[row, column] for column in columns]

        above, here = load(first - 1), load(first)
        flux = None
        for row in range(first, last):
            below = load(row + 1)
            if border and row == first:
                border(0, turn, here)
            if border and row == last - 1:
                border(1, turn, here)
            applied, flux = stencil(weight, row, above, here, below, flux)
            inside = row in range(*own)
            results = []
            for column in columns:
                before = source(row, column) if turn == 0 else remain_ref[row, column]
                left = before - applied[column]
                if turn < CHEB:
                    remain_ref[row, column] = left
                    step_ref[row, column] = (
                        coef[2 + 2 * turn] * here[column] + coef[3 + 2 * turn] * left
                    )
                solved = None
                if inside:
                    place = row - own[0]
                    solved = here[column]
                    if turn > 0:
                        solved = solved_ref[place, column] + solved
                    if turn < CHEB:
                        solved_ref[place, column] = solved
                if turn == CHEB:
                    begun = source(row, column)
                    results.append((begun, solved, begun - left))
            if turn == CHEB:
                emit(row, *zip(*results))
            above, here = here, below


def add_products(sums, index, one, two):
    for column in range(BLOCK):
        product = one[column] * two[column]
        sums[index] = sums[index] + jnp.where(own_columns(column), product, 0.0)


def own_kernel(rows, local_ref, coef_ref, wide_ref, scratch_ref):
    lines = weight_lines([weight_part(local_ref, rows)], scratch_ref)
    coef = [coef_ref[0]]
    for row in range(rows):
        for plane in range(3):
            for column in range(BLOCK):
                value = jnp.zeros((SUB, LANES), jnp.float32)
                if plane != 1 or row < rows - 1:
                    value = spread(lines[column], plane * rows + row, plane, coef)
                wide_ref[row, plane * BLOCK + column] = value


def near_kernel(
    rows, top_ref, field_ref, bottom_ref, coef_ref, own_wide_ref,
    solved_ref, middle_ref, step_ref, remain_ref, border_ref, wide_ref, early_ref,
    part_ref, scratch_ref,
):
    parts = [
        weight_part(top_ref, rows),
        own_weight_part(field_ref, rows),
        weight_part(bottom_ref, rows),
    ]
    lines = weight_lines(parts, scratch_ref)
    places = near_places(rows)[0]
    coef = [coef_ref[index] for index in range(2 + 2 * CHEB)]
    total = 3 * rows + 2 * FAR
    own = (FAR + rows, FAR + 2 * rows)
    made = set()

    def weight(plane, row, column):
        place = plane * BLOCK + column
        if own[0] <= row < own[1] - (plane == 1):
            return own_wide_ref[row - own[0], place]
        if (row, place) not in made:
            made.add((row, place))
            wide_ref[row, place] = spread(lines[column], plane * 3 * rows + row - FAR, plane, coef)
        return wide_ref[row, place]

    def source(row, column):
        if row < own[0]:
            return received(top_ref, places, own[0] - row, column)
        if row >= own[1]:
            return received(bottom_ref, places, row - own[1] + 1, column)
        return field_ref[(row - own[0]) * BLOCK + column]

    sums = [jnp.zeros((SUB, LANES), jnp.float32) for _ in range(2)]

    def emit(row, begun, solved, applied):
        for column in range(BLOCK):
            middle_ref[row, column] = applied[column]
        if row in range(*own):
            for column in range(BLOCK):
                solved_ref[row - own[0], column] = solved[column]
            add_products(sums, 0, begun, solved)
            add_products(sums, 1, solved, applied)

    def border(side, turn, step):
        for column in range(BLOCK):
            border_ref[side, turn, column] = step[column]

    passes(
        FAR, own, total, source, weight, coef, step_ref, remain_ref, part_ref, emit, border
    )
    early_ref[0] = sums[0]
    early_ref[1] = sums[1]


def far_kernel(
    rows, top_far_ref, top_ref, field_ref, bottom_ref, bottom_far_ref, coef_ref,
    middle_ref, frozen_step_ref, frozen_remain_ref, border_ref, wide_ref, own_wide_ref, early_ref,
    solved_ref, applied_ref, sums_ref,
    step_ref, remain_ref, part_ref, outer_ref, scratch_ref,
):
    columns = range(BLOCK)
    parts = [
        weight_part(top_far_ref, FAR),
        weight_part(top_ref, rows),
        own_weight_part(field_ref, rows),
        weight_part(bottom_ref, rows),
        weight_part(bottom_far_ref, FAR),
    ]
    lines = weight_lines(parts, scratch_ref)
    coef = [coef_ref[index] for index in range(2 + 2 * CHEB)]
    total = 3 * rows + 2 * FAR
    own = (FAR + rows, FAR + 2 * rows)
    near, far = near_places(rows)[0], far_places(rows)[0]
    made = {}

    def weight(plane, row, column):
        if own[0] <= row < own[1] - (plane == 1):
            return own_wide_ref[row - own[0], plane * BLOCK + column]
        if FAR < row < total - FAR - 1 or (plane == 1 and row == FAR):
            return wide_ref[row, plane * BLOCK + column]
        key = (plane, row, column)
        if key not in made:
            made[key] = spread(lines[column], plane * total + row, plane, coef)
        return made[key]

    def source(row):
        distance = own[0] - row if row < own[0] else row - own[1] + 1
        if distance > rows:
            ref, places = (top_far_ref if row < own[0] else bottom_far_ref), far
        else:
            ref, places = (top_ref if row < own[0] else bottom_ref), near
        return [received(ref, places, distance, column) for column in columns]

    for side in range(2):

        def at(index, side=side):
            return total - 1 - index if side else index

        ends = [[coef[1] * value for value in source(at(index))] for index in range(FAR)]
        rest = source(at(1))
        for turn in range(CHEB + 1):
            edge_row = at(turn + 2)
            if turn == 0:
                inner = [coef[1] * value for value in source(edge_row)]
                inner_rest = source(edge_row)
            else:
                inner = [frozen_step_ref[edge_row, column] for column in columns]
                inner_rest = [frozen_remain_ref[edge_row, column] for column in columns]
            steps = ends + [inner, [border_ref[side, turn, column] for column in columns]]
            new_ends, new_rest = [], []
            for index, before in ((1, rest), (2, inner_rest)):
                row = at(turn + index)
                outside, inside = steps[index - 1], steps[index + 1]
                above, below = (inside, outside) if side else (outside, inside)
                here = steps[index]
                applied, _ = stencil(weight, row, above, here, below)
                left = [before[column] - applied[column] for column in columns]
                new_rest.append(left)
                if turn < CHEB:
                    new_ends.append(
                        [
                            coef[2 + 2 * turn] * here[column] + coef[3 + 2 * turn] * left[column]
                            for column in columns
                        ]
                    )
                else:
                    begun = source(row)
                    for column in columns:
                        outer_ref[side * FAR + index - 1, column] = begun[column] - left[column]
            ends, rest = new_ends, new_rest[1]

    def middle(row, column):
        index = min(row, total - 1 - row)
        if index < HALO + FAR:
            return outer_ref[FAR * (row > index) + index - HALO, column]
        return middle_ref[row, column]

    sums = [early_ref[0], early_ref[1]] + [jnp.zeros((SUB, LANES), jnp.float32) for _ in range(2)]

    def emit(row, begun, solved, applied):
        for column in columns:
            solved_ref[row - own[0], column] = solved[column]
            applied_ref[row - own[0], column] = applied[column]
        add_products(sums, 2, begun, solved)
        add_products(sums, 3, solved, applied)

    passes(HALO, own, total, middle, weight, coef, step_ref, remain_ref, part_ref, emit)

    lane = lane_index((1, LANES))
    line = jnp.zeros((1, LANES), jnp.float32)
    for index in range(4):
        line = jnp.where(lane == index, jnp.sum(sums[index]), line)
    sums_ref[...] = jnp.broadcast_to(line[None], sums_ref.shape)


def inverse_kernel(
    rows, times, length, cas_ref, sums_ref, one_ref, two_ref, three_ref, four_ref, out_ref, line_ref
):
    half = LANES // 2
    span = half + 2 * SIDE
    skip = (span - WINDOW) // 2
    line = jnp.sum(sums_ref[...].reshape(sums_ref.shape[0], LANES), axis=0, keepdims=True)
    gamma, curved, cross, last = (
        jnp.broadcast_to(line[:, index : index + 1], (SUB, LANES)) for index in range(4)
    )
    step = gamma / curved
    gamma_next = step * step * cross - gamma
    turn = gamma_next / gamma
    grown = 1.0 + turn
    next_curved = grown * grown * curved - 2.0 * step * grown * cross + step * step * last
    next_step = gamma_next / next_curved
    first = step + next_step * grown
    second = -next_step * step
    for row in range(rows):
        for index, (left_ref, right_ref) in enumerate(((one_ref, two_ref), (three_ref, four_ref))):
            offset = left_ref.shape[0] // 2 - rows // 2
            for column in range(BLOCK):
                start = (2 * row + index) * span + skip + column
                value = first * left_ref[offset + row, column] + second * right_ref[row, column]
                line_ref[pl.ds(start, SUB, stride=BLOCK), :] = value
    points = jnp.concatenate(
        [
            line_ref[index * span + SIDE : index * span + SIDE + half, :]
            for index in range(2 * rows)
        ],
        axis=0,
    )
    back = exact_dot(cas_ref[...], points, 1, 1)
    for row in range(rows):
        piece = back[:, row * LANES : (row + 1) * LANES].reshape(length // times, times, LANES)
        out_ref[:, row * times : (row + 1) * times, :] = piece


def final_kernel(rows, times, tiles, source_ref, field_ref, solution_ref, residual_ref):
    half = LANES // 2
    low = lane_index((rows, LANES)) < half
    for time in range(times):
        place = slice(time * rows, (time + 1) * rows)
        taken = pl.ds(time, rows, stride=times)
        for pair in range(tiles // 2):
            columns = slice(pair * LANES, (pair + 1) * LANES)
            left = source_ref[2 * pair, taken, :]
            right = source_ref[2 * pair + 1, taken, :]
            solution_ref[place, columns] = jnp.where(low, left, pltpu.roll(right, half, 1))
            change = jnp.where(low, pltpu.roll(left, half, 1), right)
            residual_ref[place, columns] = field_ref[place, columns] - change


def call(kernel, out_shape, scratch=()):
    shapes = [jax.ShapeDtypeStruct(shape, jnp.float32) for shape in out_shape]
    return pl.pallas_call(
        kernel,
        out_shape=shapes[0] if len(shapes) == 1 else shapes,
        scratch_shapes=[pltpu.VMEM(shape, jnp.float32) for shape in scratch],
        compiler_params=PARAMS,
    )


def shift(value, distance, spaces):
    return lax.ppermute(value, "space", [(i, (i + distance) % spaces) for i in range(spaces)])


def shards(right_side, kappa, velocity):
    tiles = lax.axis_size("tm")
    spaces = lax.axis_size("space")
    times, rows, width = right_side.shape
    length = times * tiles
    tile = width // tiles
    around = (LANES - tile) // 2
    cas_table = jnp.asarray(hartley_table(length))
    coef_table = jnp.asarray(chebyshev_table(length))

    field = right_side.reshape(times * rows, width)
    windows = call(
        functools.partial(window_kernel, rows, times, tiles),
        [(tiles, 6 * times, LANES)],
        [(width // LANES, times * rows, LANES)],
    )(field)
    gathered = lax.all_to_all(windows, "tm", 0, 0)

    squares = velocity.astype(jnp.float32) ** 2
    planes = jnp.concatenate([kappa, squares[0], squares[1]], axis=0)
    planes = jnp.concatenate([planes[:, -around:], planes, planes[:, :around]], axis=1)
    local = lax.dynamic_slice_in_dim(planes, lax.axis_index("tm") * tile, LANES, 1)
    own_wide = call(
        functools.partial(own_kernel, rows),
        [(rows, 3 * BLOCK, SUB, LANES)],
        [(LANES, LANES)],
    )(local, coef_table)

    total = 3 * rows + 2 * FAR
    tile_shape = (rows, BLOCK, SUB, LANES)
    near_shape = (near_places(rows)[1], LANES)
    far_shape = (far_places(rows)[1], LANES)
    span = LANES // 2 + 2 * SIDE
    freq, up, down, far_up, far_down = call(
        functools.partial(forward_kernel, rows, times, length),
        [(rows * BLOCK + 3, SUB, LANES), near_shape, near_shape, far_shape, far_shape],
        [(rows * span, LANES)],
    )(cas_table, gathered, local)
    top, bottom = shift(up, 1, spaces), shift(down, -1, spaces)
    top_far, bottom_far = shift(far_up, 2, spaces), shift(far_down, -2, spaces)

    groups = [
        [i * spaces + first + j for i in range(tiles) for j in range(NEAR)]
        for first in range(0, spaces, NEAR)
    ]
    work = (total, BLOCK, SUB, LANES)
    solved, middle, step, remain, border, wide, early = call(
        functools.partial(near_kernel, rows),
        [
            tile_shape,
            work,
            work,
            work,
            (2, CHEB + 1, BLOCK, SUB, LANES),
            (total, 3 * BLOCK, SUB, LANES),
            (2, SUB, LANES),
        ],
        [tile_shape, (LANES, LANES)],
    )(top, freq, bottom, coef_table, own_wide)
    solved_two, applied_two, sums = call(
        functools.partial(far_kernel, rows),
        [tile_shape, tile_shape, (tiles * NEAR, 1, LANES)],
        [work, work, tile_shape, (2 * FAR, BLOCK, SUB, LANES), (LANES, LANES)],
    )(
        top_far, top, freq, bottom, bottom_far, coef_table, middle, step, remain, border, wide,
        own_wide, early,
    )
    sums = lax.all_to_all(sums, ("tm", "space"), 0, 0, axis_index_groups=groups)
    planes = spaces // NEAR
    groups = [[first + NEAR * i for i in range(planes)] for first in range(NEAR)]
    sums = jnp.broadcast_to(jnp.sum(sums, axis=0)[None], (planes, 1, LANES))
    sums = lax.all_to_all(sums, "space", 0, 0, axis_index_groups=groups)
    packed = call(
        functools.partial(inverse_kernel, rows, times, length),
        [(tiles, rows * times, LANES)],
        [(rows * 2 * span, LANES)],
    )(cas_table, sums, solved, solved_two, middle, applied_two)
    returned = lax.all_to_all(packed, "tm", 0, 0)

    solution, residual = call(
        functools.partial(final_kernel, rows, times, tiles),
        [(times * rows, width), (times * rows, width)],
    )(returned, field)
    shape = right_side.shape
    return solution.reshape(shape), residual.reshape(shape)


def solution(mesh):
    placed = (P("tm", "space", None), P("space", None), P(None, "space", None))
    return jax.shard_map(
        shards,
        mesh=mesh,
        in_specs=placed,
        out_specs=(P("tm", "space", None), P("tm", "space", None)),
        check_vma=False,
    )
```

```python
import functools
import math

import jax
import jax.numpy as jnp
import numpy as np
from jax import lax
from jax.experimental import pallas as pl
from jax.experimental.pallas import tpu as pltpu
from jax.sharding import PartitionSpec as P

CHEB = 4
COUPLING = 2.0
KAPPA_LOW = 0.05
KAPPA_HIGH = 1.0
REACH = 16.0

LANES = 128
SUB = 8
HALO = CHEB + 1
FAR = 2
SIDE = 16
BLOCK = 11
WINDOW = SUB * BLOCK
NEAR = 4
PARAMS = pltpu.CompilerParams(vmem_limit_bytes=24 * 1024 * 1024)


def hartley_table(length):
    index = np.arange(length)
    angle = (index[:, None] * index[None, :] % length) * (2.0 * math.pi / length)
    return ((np.cos(angle) + np.sin(angle)) / math.sqrt(length)).astype(np.float32)


def chebyshev_table(length):
    shift = COUPLING * (2.0 - 2.0 * np.cos(2.0 * math.pi * np.arange(length) / length))
    half = 0.5 * (KAPPA_HIGH + REACH - KAPPA_LOW)
    mid = 0.5 * (KAPPA_LOW + KAPPA_HIGH + REACH) + shift
    ratio = mid / half
    damp = 1.0 / ratio
    lines = [shift, 1.0 / mid]
    for _ in range(CHEB):
        damp_next = 1.0 / (2.0 * ratio - damp)
        lines += [damp_next * damp, 2.0 * damp_next / half]
        damp = damp_next
    return np.repeat(np.stack(lines).astype(np.float32)[:, None], SUB, 1)


def lane_index(shape):
    return lax.broadcasted_iota(jnp.int32, shape, len(shape) - 1)


def exact_dot(left, right, left_dim, right_dim):
    return lax.dot_general(
        left,
        right,
        (((left_dim,), (right_dim,)), ((), ())),
        precision=lax.Precision.HIGHEST,
        preferred_element_type=jnp.float32,
    )


def window_kernel(rows, times, tiles, source_ref, out_ref, scratch_ref):
    half = LANES // 2
    parts = source_ref.shape[1] // LANES
    for part in range(parts):
        scratch_ref[part] = source_ref[:, part * LANES : (part + 1) * LANES]
    lane = lane_index((times, LANES))
    fields = [
        [scratch_ref[part, pl.ds(row, times, stride=rows), :] for part in range(parts)]
        for row in range(rows)
    ]
    for pair in range(rows // 2):
        for part in range(parts):
            one, two = fields[2 * pair][part], fields[2 * pair + 1][part]
            place = slice(pair * times, (pair + 1) * times)
            out_ref[2 * part, place, :] = jnp.where(lane < half, one, pltpu.roll(two, half, 1))
            out_ref[2 * part + 1, place, :] = jnp.where(lane < half, pltpu.roll(one, half, 1), two)
    spread = 2 * SIDE
    group = LANES // spread
    for quad in range(rows // group):
        even = [None] * parts
        odd = [None] * parts
        for index in range(group):
            row = quad * group + index
            wide = jnp.concatenate(fields[row], axis=1)
            near = pltpu.roll(wide, spread * index + SIDE, 1)
            away = pltpu.roll(wide, (spread * index - half + SIDE) % wide.shape[1], 1)
            left = (lane >= spread * index) & (lane < spread * index + SIDE)
            right = (lane >= spread * index + SIDE) & (lane < spread * (index + 1))
            for part in range(parts):
                here = slice(part * LANES, (part + 1) * LANES)
                then = (part + 1) % parts
                then = slice(then * LANES, (then + 1) * LANES)
                if index == 0:
                    even[part] = jnp.where(left, near[:, here], away[:, here])
                    odd[part] = jnp.where(left, away[:, here], near[:, then])
                else:
                    even[part] = jnp.where(
                        left, near[:, here], jnp.where(right, away[:, here], even[part])
                    )
                    odd[part] = jnp.where(
                        left, away[:, here], jnp.where(right, near[:, then], odd[part])
                    )
        start = (rows // 2 + quad) * times
        for part in range(parts):
            out_ref[2 * part, start : start + times, :] = even[part]
            out_ref[2 * part + 1, start : start + times, :] = odd[part]


def reach(distance):
    halo = 2 * HALO - distance
    margin = 0 if halo == 0 else 4 if halo <= 4 else 8 if halo <= 8 else 12
    return SIDE - margin, SIDE + LANES // 2 + margin


def sent_places(distances, start):
    places = {}
    for distance in distances:
        places[distance] = start
        first, last = reach(distance)
        start += last - first
    return places, start


def near_places(rows):
    return sent_places(range(rows, 0, -1), 3 * rows)


def far_places(rows):
    places, end = sent_places(range(rows + 1, rows + FAR + 1), SUB)
    return places, end + SIDE


def forward_kernel(
    rows, times, length, cas_ref, field_ref, local_ref,
    out_ref, up_ref, down_ref, far_up_ref, far_down_ref, line_ref,
):
    half = LANES // 2
    span = half + 2 * SIDE
    pieces = field_ref.shape[1] // times
    group = LANES // (2 * SIDE)
    for piece in range(pieces):
        block = field_ref[:, piece * times : (piece + 1) * times, :].reshape(length, LANES)
        freq = exact_dot(block, cas_ref[...], 0, 0)
        if piece < rows // 2:
            for part in range(2):
                start = (2 * piece + part) * span + SIDE
                line_ref[start : start + half, :] = freq[part * half : (part + 1) * half]
        else:
            for index in range(group):
                start = ((piece - rows // 2) * group + index) * span
                place = 2 * SIDE * index
                line_ref[start : start + SIDE, :] = freq[place : place + SIDE]
                line_ref[start + SIDE + half : start + span, :] = freq[
                    place + SIDE : place + 2 * SIDE
                ]
    skip = (span - WINDOW) // 2
    for row in range(rows):
        for column in range(BLOCK):
            value = line_ref[pl.ds(row * span + skip + column, SUB, stride=BLOCK), :]
            out_ref[row * BLOCK + column] = value
    for plane in range(3):
        out_ref[rows * BLOCK + plane] = local_ref[plane * rows : (plane + 1) * rows, :]
    near, far = near_places(rows)[0], far_places(rows)[0]
    for ref, places, row_of in (
        (up_ref, near, lambda distance: rows - distance),
        (down_ref, near, lambda distance: distance - 1),
        (far_up_ref, far, lambda distance: 2 * rows - distance),
        (far_down_ref, far, lambda distance: distance - 1 - rows),
    ):
        for distance, place in places.items():
            first, last = reach(distance)
            start = row_of(distance) * span
            ref[place : place + last - first, :] = line_ref[start + first : start + last, :]
    up_ref[: 3 * rows, :] = local_ref[...]
    down_ref[: 3 * rows, :] = local_ref[...]
    for ref, first in ((far_up_ref, rows - FAR), (far_down_ref, 0)):
        ref[ref.shape[0] - SIDE :, :] = jnp.zeros((SIDE, LANES), jnp.float32)
        kept = [local_ref[plane * rows + first : plane * rows + first + FAR, :] for plane in range(3)]
        kept.append(jnp.zeros((SUB - 3 * FAR, LANES), jnp.float32))
        ref[:SUB, :] = jnp.concatenate(kept, axis=0)


def weight_lines(parts, scratch_ref):
    planes = [jnp.concatenate(blocks, axis=0) for blocks in zip(*parts)]
    east = 1.0 + 0.125 * (planes[1] + jnp.concatenate([planes[1][1:], planes[1][:1]], axis=0))
    north = 1.0 + 0.125 * (planes[2] + pltpu.roll(planes[2], LANES - 1, 1))
    zero = jnp.zeros((LANES - 3 * planes[0].shape[0], LANES), jnp.float32)
    scratch_ref[...] = jnp.transpose(jnp.concatenate([planes[0], east, north, zero], axis=0))
    skip = (LANES - WINDOW) // 2
    return [scratch_ref[pl.ds(skip + column, SUB, stride=BLOCK), :] for column in range(BLOCK)]


def weight_part(ref, rows):
    return [ref[plane * rows : (plane + 1) * rows, :] for plane in range(3)]


def own_weight_part(field_ref, rows):
    return [field_ref[rows * BLOCK + plane] for plane in range(3)]


def received(ref, places, distance, column):
    skip = (LANES // 2 + 2 * SIDE - WINDOW) // 2
    start = places[distance] - reach(distance)[0] + skip + column
    return ref[pl.ds(start, SUB, stride=BLOCK), :]


def spread(lines, index, plane, coef):
    value = jnp.broadcast_to(lines[:, index : index + 1], (SUB, LANES))
    return value + coef[0] if plane == 0 else value


def own_columns(column):
    place = lax.broadcasted_iota(jnp.int32, (SUB, LANES), 0) * BLOCK + column
    first = (WINDOW - LANES // 2) // 2
    return (place >= first) & (place < first + LANES // 2)


def stencil(weight, row, above, here, below, flux=None):
    columns = range(BLOCK)
    if flux is None:
        flux = [weight(1, row - 1, column) * (above[column] - here[column]) for column in columns]
    ahead = [weight(1, row, column) * (here[column] - below[column]) for column in columns]
    beside = here[1:] + [pltpu.roll(here[0], SUB - 1, 0)]
    side = [weight(2, row, column) * (here[column] - beside[column]) for column in columns]
    behind = [pltpu.roll(side[-1], 1, 0)] + side[:-1]
    applied = [
        weight(0, row, column) * here[column]
        + (ahead[column] - flux[column])
        + (side[column] - behind[column])
        for column in columns
    ]
    return applied, ahead


def passes(
    edge, own, total, source, weight, coef, step_ref, remain_ref, solved_ref, emit, border=None
):
    columns = range(BLOCK)

    for turn in range(CHEB + 1):
        first, last = edge + turn + 1, total - edge - turn - 1

        def load(row, turn=turn):
            if turn == 0:
                return [coef[1] * source(row, column) for column in columns]
            return [step_ref[row, column] for column in columns]

        above, here = load(first - 1), load(first)
        flux = None
        for row in range(first, last):
            below = load(row + 1)
            if border and row == first:
                border(0, turn, here)
            if border and row == last - 1:
                border(1, turn, here)
            applied, flux = stencil(weight, row, above, here, below, flux)
            inside = row in range(*own)
            results = []
            for column in columns:
                before = source(row, column) if turn == 0 else remain_ref[row, column]
                left = before - applied[column]
                if turn < CHEB:
                    remain_ref[row, column] = left
                    step_ref[row, column] = (
                        coef[2 + 2 * turn] * here[column] + coef[3 + 2 * turn] * left
                    )
                solved = None
                if inside:
                    place = row - own[0]
                    solved = here[column]
                    if turn > 0:
                        solved = solved_ref[place, column] + solved
                    if turn < CHEB:
                        solved_ref[place, column] = solved
                if turn == CHEB:
                    begun = source(row, column)
                    results.append((begun, solved, begun - left))
            if turn == CHEB:
                emit(row, *zip(*results))
            above, here = here, below


def add_products(sums, index, one, two):
    for column in range(BLOCK):
        product = one[column] * two[column]
        sums[index] = sums[index] + jnp.where(own_columns(column), product, 0.0)


def own_kernel(rows, local_ref, coef_ref, wide_ref, scratch_ref):
    lines = weight_lines([weight_part(local_ref, rows)], scratch_ref)
    coef = [coef_ref[0]]
    for row in range(rows):
        for plane in range(3):
            for column in range(BLOCK):
                value = jnp.zeros((SUB, LANES), jnp.float32)
                if plane != 1 or row < rows - 1:
                    value = spread(lines[column], plane * rows + row, plane, coef)
                wide_ref[row, plane * BLOCK + column] = value


def near_kernel(
    rows, top_ref, field_ref, bottom_ref, coef_ref, own_wide_ref,
    solved_ref, middle_ref, step_ref, remain_ref, border_ref, wide_ref, early_ref,
    part_ref, scratch_ref,
):
    parts = [
        weight_part(top_ref, rows),
        own_weight_part(field_ref, rows),
        weight_part(bottom_ref, rows),
    ]
    lines = weight_lines(parts, scratch_ref)
    places = near_places(rows)[0]
    coef = [coef_ref[index] for index in range(2 + 2 * CHEB)]
    total = 3 * rows + 2 * FAR
    own = (FAR + rows, FAR + 2 * rows)
    made = set()

    def weight(plane, row, column):
        place = plane * BLOCK + column
        if own[0] <= row < own[1] - (plane == 1):
            return own_wide_ref[row - own[0], place]
        if (row, place) not in made:
            made.add((row, place))
            wide_ref[row, place] = spread(lines[column], plane * 3 * rows + row - FAR, plane, coef)
        return wide_ref[row, place]

    def source(row, column):
        if row < own[0]:
            return received(top_ref, places, own[0] - row, column)
        if row >= own[1]:
            return received(bottom_ref, places, row - own[1] + 1, column)
        return field_ref[(row - own[0]) * BLOCK + column]

    sums = [jnp.zeros((SUB, LANES), jnp.float32) for _ in range(2)]

    def emit(row, begun, solved, applied):
        for column in range(BLOCK):
            middle_ref[row, column] = applied[column]
        if row in range(*own):
            for column in range(BLOCK):
                solved_ref[row - own[0], column] = solved[column]
            add_products(sums, 0, begun, solved)
            add_products(sums, 1, solved, applied)

    def border(side, turn, step):
        for column in range(BLOCK):
            border_ref[side, turn, column] = step[column]

    passes(
        FAR, own, total, source, weight, coef, step_ref, remain_ref, part_ref, emit, border
    )
    early_ref[0] = sums[0]
    early_ref[1] = sums[1]


def far_kernel(
    rows, top_far_ref, top_ref, field_ref, bottom_ref, bottom_far_ref, coef_ref,
    middle_ref, frozen_step_ref, frozen_remain_ref, border_ref, wide_ref, own_wide_ref, early_ref,
    solved_ref, applied_ref, sums_ref,
    step_ref, remain_ref, part_ref, outer_ref, scratch_ref,
):
    columns = range(BLOCK)
    parts = [
        weight_part(top_far_ref, FAR),
        weight_part(top_ref, rows),
        own_weight_part(field_ref, rows),
        weight_part(bottom_ref, rows),
        weight_part(bottom_far_ref, FAR),
    ]
    lines = weight_lines(parts, scratch_ref)
    coef = [coef_ref[index] for index in range(2 + 2 * CHEB)]
    total = 3 * rows + 2 * FAR
    own = (FAR + rows, FAR + 2 * rows)
    near, far = near_places(rows)[0], far_places(rows)[0]
    made = {}

    def weight(plane, row, column):
        if own[0] <= row < own[1] - (plane == 1):
            return own_wide_ref[row - own[0], plane * BLOCK + column]
        if FAR < row < total - FAR - 1 or (plane == 1 and row == FAR):
            return wide_ref[row, plane * BLOCK + column]
        key = (plane, row, column)
        if key not in made:
            made[key] = spread(lines[column], plane * total + row, plane, coef)
        return made[key]

    def source(row):
        distance = own[0] - row if row < own[0] else row - own[1] + 1
        if distance > rows:
            ref, places = (top_far_ref if row < own[0] else bottom_far_ref), far
        else:
            ref, places = (top_ref if row < own[0] else bottom_ref), near
        return [received(ref, places, distance, column) for column in columns]

    for side in range(2):

        def at(index, side=side):
            return total - 1 - index if side else index

        ends = [[coef[1] * value for value in source(at(index))] for index in range(FAR)]
        rest = source(at(1))
        for turn in range(CHEB + 1):
            edge_row = at(turn + 2)
            if turn == 0:
                inner = [coef[1] * value for value in source(edge_row)]
                inner_rest = source(edge_row)
            else:
                inner = [frozen_step_ref[edge_row, column] for column in columns]
                inner_rest = [frozen_remain_ref[edge_row, column] for column in columns]
            steps = ends + [inner, [border_ref[side, turn, column] for column in columns]]
            new_ends, new_rest = [], []
            for index, before in ((1, rest), (2, inner_rest)):
                row = at(turn + index)
                outside, inside = steps[index - 1], steps[index + 1]
                above, below = (inside, outside) if side else (outside, inside)
                here = steps[index]
                applied, _ = stencil(weight, row, above, here, below)
                left = [before[column] - applied[column] for column in columns]
                new_rest.append(left)
                if turn < CHEB:
                    new_ends.append(
                        [
                            coef[2 + 2 * turn] * here[column] + coef[3 + 2 * turn] * left[column]
                            for column in columns
                        ]
                    )
                else:
                    begun = source(row)
                    for column in columns:
                        outer_ref[side * FAR + index - 1, column] = begun[column] - left[column]
            ends, rest = new_ends, new_rest[1]

    def middle(row, column):
        index = min(row, total - 1 - row)
        if index < HALO + FAR:
            return outer_ref[FAR * (row > index) + index - HALO, column]
        return middle_ref[row, column]

    sums = [early_ref[0], early_ref[1]] + [jnp.zeros((SUB, LANES), jnp.float32) for _ in range(2)]

    def emit(row, begun, solved, applied):
        for column in columns:
            solved_ref[row - own[0], column] = solved[column]
            applied_ref[row - own[0], column] = applied[column]
        add_products(sums, 2, begun, solved)
        add_products(sums, 3, solved, applied)

    passes(HALO, own, total, middle, weight, coef, step_ref, remain_ref, part_ref, emit)

    lane = lane_index((1, LANES))
    line = jnp.zeros((1, LANES), jnp.float32)
    for index in range(4):
        line = jnp.where(lane == index, jnp.sum(sums[index]), line)
    sums_ref[...] = jnp.broadcast_to(line[None], sums_ref.shape)


def inverse_kernel(
    rows, times, length, cas_ref, sums_ref, one_ref, two_ref, three_ref, four_ref, out_ref, line_ref
):
    half = LANES // 2
    span = half + 2 * SIDE
    skip = (span - WINDOW) // 2
    line = jnp.sum(sums_ref[...].reshape(sums_ref.shape[0], LANES), axis=0, keepdims=True)
    gamma, curved, cross, last = (
        jnp.broadcast_to(line[:, index : index + 1], (SUB, LANES)) for index in range(4)
    )
    step = gamma / curved
    gamma_next = step * step * cross - gamma
    turn = gamma_next / gamma
    grown = 1.0 + turn
    next_curved = grown * grown * curved - 2.0 * step * grown * cross + step * step * last
    next_step = gamma_next / next_curved
    first = step + next_step * grown
    second = -next_step * step
    for row in range(rows):
        for index, (left_ref, right_ref) in enumerate(((one_ref, two_ref), (three_ref, four_ref))):
            offset = left_ref.shape[0] // 2 - rows // 2
            for column in range(BLOCK):
                start = (2 * row + index) * span + skip + column
                value = first * left_ref[offset + row, column] + second * right_ref[row, column]
                line_ref[pl.ds(start, SUB, stride=BLOCK), :] = value
    points = jnp.concatenate(
        [
            line_ref[index * span + SIDE : index * span + SIDE + half, :]
            for index in range(2 * rows)
        ],
        axis=0,
    )
    back = exact_dot(cas_ref[...], points, 1, 1)
    for row in range(rows):
        piece = back[:, row * LANES : (row + 1) * LANES].reshape(length // times, times, LANES)
        out_ref[:, row * times : (row + 1) * times, :] = piece


def final_kernel(
    rows, times, tiles, source_ref, field_ref, solution_ref, residual_ref,
    solution_part, residual_part, sent,
):
    half = LANES // 2
    low = lane_index((rows, LANES)) < half
    copies = []
    for time in range(times):
        place = slice(time * rows, (time + 1) * rows)
        taken = pl.ds(time, rows, stride=times)
        for pair in range(tiles // 2):
            columns = slice(pair * LANES, (pair + 1) * LANES)
            left = source_ref[2 * pair, taken, :]
            right = source_ref[2 * pair + 1, taken, :]
            solution_part[place, columns] = jnp.where(low, left, pltpu.roll(right, half, 1))
            change = jnp.where(low, pltpu.roll(left, half, 1), right)
            residual_part[place, columns] = field_ref[place, columns] - change
        for index, (part_ref, whole_ref) in enumerate(
            ((solution_part, solution_ref), (residual_part, residual_ref))
        ):
            span = pl.ds(time * rows, rows)
            copies.append(
                pltpu.make_async_copy(part_ref.at[span], whole_ref.at[span], sent.at[index, time])
            )
            copies[-1].start()
    for copy in copies:
        copy.wait()


def call(kernel, out_shape, scratch=()):
    shapes = [jax.ShapeDtypeStruct(shape, jnp.float32) for shape in out_shape]
    return pl.pallas_call(
        kernel,
        out_shape=shapes[0] if len(shapes) == 1 else shapes,
        scratch_shapes=[pltpu.VMEM(shape, jnp.float32) for shape in scratch],
        compiler_params=PARAMS,
    )


def shift(value, distance, spaces):
    return lax.ppermute(value, "space", [(i, (i + distance) % spaces) for i in range(spaces)])


def shards(right_side, kappa, velocity):
    tiles = lax.axis_size("tm")
    spaces = lax.axis_size("space")
    times, rows, width = right_side.shape
    length = times * tiles
    tile = width // tiles
    around = (LANES - tile) // 2
    cas_table = jnp.asarray(hartley_table(length))
    coef_table = jnp.asarray(chebyshev_table(length))

    field = right_side.reshape(times * rows, width)
    windows = call(
        functools.partial(window_kernel, rows, times, tiles),
        [(tiles, 6 * times, LANES)],
        [(width // LANES, times * rows, LANES)],
    )(field)
    gathered = lax.all_to_all(windows, "tm", 0, 0)

    squares = velocity.astype(jnp.float32) ** 2
    planes = jnp.concatenate([kappa, squares[0], squares[1]], axis=0)
    planes = jnp.concatenate([planes[:, -around:], planes, planes[:, :around]], axis=1)
    local = lax.dynamic_slice_in_dim(planes, lax.axis_index("tm") * tile, LANES, 1)
    own_wide = call(
        functools.partial(own_kernel, rows),
        [(rows, 3 * BLOCK, SUB, LANES)],
        [(LANES, LANES)],
    )(local, coef_table)

    total = 3 * rows + 2 * FAR
    tile_shape = (rows, BLOCK, SUB, LANES)
    near_shape = (near_places(rows)[1], LANES)
    far_shape = (far_places(rows)[1], LANES)
    span = LANES // 2 + 2 * SIDE
    freq, up, down, far_up, far_down = call(
        functools.partial(forward_kernel, rows, times, length),
        [(rows * BLOCK + 3, SUB, LANES), near_shape, near_shape, far_shape, far_shape],
        [(rows * span, LANES)],
    )(cas_table, gathered, local)
    top, bottom = shift(up, 1, spaces), shift(down, -1, spaces)
    top_far, bottom_far = shift(far_up, 2, spaces), shift(far_down, -2, spaces)

    groups = [
        [i * spaces + first + j for i in range(tiles) for j in range(NEAR)]
        for first in range(0, spaces, NEAR)
    ]
    work = (total, BLOCK, SUB, LANES)
    solved, middle, step, remain, border, wide, early = call(
        functools.partial(near_kernel, rows),
        [
            tile_shape,
            work,
            work,
            work,
            (2, CHEB + 1, BLOCK, SUB, LANES),
            (total, 3 * BLOCK, SUB, LANES),
            (2, SUB, LANES),
        ],
        [tile_shape, (LANES, LANES)],
    )(top, freq, bottom, coef_table, own_wide)
    solved_two, applied_two, sums = call(
        functools.partial(far_kernel, rows),
        [tile_shape, tile_shape, (tiles * NEAR, 1, LANES)],
        [work, work, tile_shape, (2 * FAR, BLOCK, SUB, LANES), (LANES, LANES)],
    )(
        top_far, top, freq, bottom, bottom_far, coef_table, middle, step, remain, border, wide,
        own_wide, early,
    )
    sums = lax.all_to_all(sums, ("tm", "space"), 0, 0, axis_index_groups=groups)
    planes = spaces // NEAR
    groups = [[first + NEAR * i for i in range(planes)] for first in range(NEAR)]
    sums = jnp.broadcast_to(jnp.sum(sums, axis=0)[None], (planes, 1, LANES))
    sums = lax.all_to_all(sums, "space", 0, 0, axis_index_groups=groups)
    packed = call(
        functools.partial(inverse_kernel, rows, times, length),
        [(tiles, rows * times, LANES)],
        [(rows * 2 * span, LANES)],
    )(cas_table, sums, solved, solved_two, middle, applied_two)
    returned = lax.all_to_all(packed, "tm", 0, 0)

    whole = jax.ShapeDtypeStruct((times * rows, width), jnp.float32)
    solution, residual = pl.pallas_call(
        functools.partial(final_kernel, rows, times, tiles),
        out_shape=[whole, whole],
        out_specs=[pl.BlockSpec(memory_space=pl.ANY)] * 2,
        scratch_shapes=[
            pltpu.VMEM(whole.shape, jnp.float32),
            pltpu.VMEM(whole.shape, jnp.float32),
            pltpu.SemaphoreType.DMA((2, times)),
        ],
        compiler_params=PARAMS,
    )(returned, field)
    shape = right_side.shape
    return solution.reshape(shape), residual.reshape(shape)


def solution(mesh):
    placed = (P("tm", "space", None), P("space", None), P(None, "space", None))
    return jax.shard_map(
        shards,
        mesh=mesh,
        in_specs=placed,
        out_specs=(P("tm", "space", None), P("tm", "space", None)),
        check_vma=False,
    )
```

```python
import functools
import math

import jax
import jax.numpy as jnp
import numpy as np
from jax import lax
from jax.experimental import pallas as pl
from jax.experimental.pallas import tpu as pltpu
from jax.sharding import PartitionSpec as P

CHEB = 4
COUPLING = 2.0
KAPPA_LOW = 0.05
KAPPA_HIGH = 1.0
REACH = 16.0

LANES = 128
SUB = 8
HALO = CHEB + 1
FAR = 2
SIDE = 16
BLOCK = 11
WINDOW = SUB * BLOCK
PARAMS = pltpu.CompilerParams(vmem_limit_bytes=24 * 1024 * 1024)


def hartley_table(length):
    index = np.arange(length)
    angle = (index[:, None] * index[None, :] % length) * (2.0 * math.pi / length)
    return ((np.cos(angle) + np.sin(angle)) / math.sqrt(length)).astype(np.float32)


def chebyshev_table(length):
    shift = COUPLING * (2.0 - 2.0 * np.cos(2.0 * math.pi * np.arange(length) / length))
    half = 0.5 * (KAPPA_HIGH + REACH - KAPPA_LOW)
    mid = 0.5 * (KAPPA_LOW + KAPPA_HIGH + REACH) + shift
    ratio = mid / half
    damp = 1.0 / ratio
    lines = [shift, 1.0 / mid]
    for _ in range(CHEB):
        damp_next = 1.0 / (2.0 * ratio - damp)
        lines += [damp_next * damp, 2.0 * damp_next / half]
        damp = damp_next
    return np.repeat(np.stack(lines).astype(np.float32)[:, None], SUB, 1)


def lane_index(shape):
    return lax.broadcasted_iota(jnp.int32, shape, len(shape) - 1)


def exact_dot(left, right, left_dim, right_dim):
    return lax.dot_general(
        left,
        right,
        (((left_dim,), (right_dim,)), ((), ())),
        precision=lax.Precision.HIGHEST,
        preferred_element_type=jnp.float32,
    )


def window_kernel(rows, times, tiles, source_ref, out_ref, scratch_ref):
    half = LANES // 2
    parts = source_ref.shape[1] // LANES
    for part in range(parts):
        scratch_ref[part] = source_ref[:, part * LANES : (part + 1) * LANES]
    lane = lane_index((times, LANES))
    fields = [
        [scratch_ref[part, pl.ds(row, times, stride=rows), :] for part in range(parts)]
        for row in range(rows)
    ]
    for pair in range(rows // 2):
        for part in range(parts):
            one, two = fields[2 * pair][part], fields[2 * pair + 1][part]
            place = slice(pair * times, (pair + 1) * times)
            out_ref[2 * part, place, :] = jnp.where(lane < half, one, pltpu.roll(two, half, 1))
            out_ref[2 * part + 1, place, :] = jnp.where(lane < half, pltpu.roll(one, half, 1), two)
    spread = 2 * SIDE
    group = LANES // spread
    for quad in range(rows // group):
        even = [None] * parts
        odd = [None] * parts
        for index in range(group):
            row = quad * group + index
            wide = jnp.concatenate(fields[row], axis=1)
            near = pltpu.roll(wide, spread * index + SIDE, 1)
            away = pltpu.roll(wide, (spread * index - half + SIDE) % wide.shape[1], 1)
            left = (lane >= spread * index) & (lane < spread * index + SIDE)
            right = (lane >= spread * index + SIDE) & (lane < spread * (index + 1))
            for part in range(parts):
                here = slice(part * LANES, (part + 1) * LANES)
                then = (part + 1) % parts
                then = slice(then * LANES, (then + 1) * LANES)
                if index == 0:
                    even[part] = jnp.where(left, near[:, here], away[:, here])
                    odd[part] = jnp.where(left, away[:, here], near[:, then])
                else:
                    even[part] = jnp.where(
                        left, near[:, here], jnp.where(right, away[:, here], even[part])
                    )
                    odd[part] = jnp.where(
                        left, away[:, here], jnp.where(right, near[:, then], odd[part])
                    )
        start = (rows // 2 + quad) * times
        for part in range(parts):
            out_ref[2 * part, start : start + times, :] = even[part]
            out_ref[2 * part + 1, start : start + times, :] = odd[part]


def reach(distance):
    halo = 2 * HALO - distance
    margin = 0 if halo == 0 else 4 if halo <= 4 else 8 if halo <= 8 else 12
    return SIDE - margin, SIDE + LANES // 2 + margin


def sent_places(distances, start):
    places = {}
    for distance in distances:
        places[distance] = start
        first, last = reach(distance)
        start += last - first
    return places, start


def near_places(rows):
    return sent_places(range(rows, 0, -1), 3 * rows)


def far_places(rows):
    places, end = sent_places(range(rows + 1, rows + FAR + 1), SUB)
    return places, end + SIDE


def forward_kernel(
    rows, times, length, cas_ref, field_ref, local_ref,
    out_ref, up_ref, down_ref, far_up_ref, far_down_ref, line_ref,
):
    half = LANES // 2
    span = half + 2 * SIDE
    pieces = field_ref.shape[1] // times
    group = LANES // (2 * SIDE)
    for piece in range(pieces):
        block = field_ref[:, piece * times : (piece + 1) * times, :].reshape(length, LANES)
        freq = exact_dot(block, cas_ref[...], 0, 0)
        if piece < rows // 2:
            for part in range(2):
                start = (2 * piece + part) * span + SIDE
                line_ref[start : start + half, :] = freq[part * half : (part + 1) * half]
        else:
            for index in range(group):
                start = ((piece - rows // 2) * group + index) * span
                place = 2 * SIDE * index
                line_ref[start : start + SIDE, :] = freq[place : place + SIDE]
                line_ref[start + SIDE + half : start + span, :] = freq[
                    place + SIDE : place + 2 * SIDE
                ]
    skip = (span - WINDOW) // 2
    for row in range(rows):
        for column in range(BLOCK):
            value = line_ref[pl.ds(row * span + skip + column, SUB, stride=BLOCK), :]
            out_ref[row * BLOCK + column] = value
    for plane in range(3):
        out_ref[rows * BLOCK + plane] = local_ref[plane * rows : (plane + 1) * rows, :]
    near, far = near_places(rows)[0], far_places(rows)[0]
    for ref, places, row_of in (
        (up_ref, near, lambda distance: rows - distance),
        (down_ref, near, lambda distance: distance - 1),
        (far_up_ref, far, lambda distance: 2 * rows - distance),
        (far_down_ref, far, lambda distance: distance - 1 - rows),
    ):
        for distance, place in places.items():
            first, last = reach(distance)
            start = row_of(distance) * span
            ref[place : place + last - first, :] = line_ref[start + first : start + last, :]
    up_ref[: 3 * rows, :] = local_ref[...]
    down_ref[: 3 * rows, :] = local_ref[...]
    for ref, first in ((far_up_ref, rows - FAR), (far_down_ref, 0)):
        ref[ref.shape[0] - SIDE :, :] = jnp.zeros((SIDE, LANES), jnp.float32)
        kept = [local_ref[plane * rows + first : plane * rows + first + FAR, :] for plane in range(3)]
        kept.append(jnp.zeros((SUB - 3 * FAR, LANES), jnp.float32))
        ref[:SUB, :] = jnp.concatenate(kept, axis=0)


def weight_lines(parts, scratch_ref):
    planes = [jnp.concatenate(blocks, axis=0) for blocks in zip(*parts)]
    east = 1.0 + 0.125 * (planes[1] + jnp.concatenate([planes[1][1:], planes[1][:1]], axis=0))
    north = 1.0 + 0.125 * (planes[2] + pltpu.roll(planes[2], LANES - 1, 1))
    zero = jnp.zeros((LANES - 3 * planes[0].shape[0], LANES), jnp.float32)
    scratch_ref[...] = jnp.transpose(jnp.concatenate([planes[0], east, north, zero], axis=0))
    skip = (LANES - WINDOW) // 2
    return [scratch_ref[pl.ds(skip + column, SUB, stride=BLOCK), :] for column in range(BLOCK)]


def weight_part(ref, rows):
    return [ref[plane * rows : (plane + 1) * rows, :] for plane in range(3)]


def own_weight_part(field_ref, rows):
    return [field_ref[rows * BLOCK + plane] for plane in range(3)]


def received(ref, places, distance, column):
    skip = (LANES // 2 + 2 * SIDE - WINDOW) // 2
    start = places[distance] - reach(distance)[0] + skip + column
    return ref[pl.ds(start, SUB, stride=BLOCK), :]


def spread(lines, index, plane, coef):
    value = jnp.broadcast_to(lines[:, index : index + 1], (SUB, LANES))
    return value + coef[0] if plane == 0 else value


def own_columns(column):
    place = lax.broadcasted_iota(jnp.int32, (SUB, LANES), 0) * BLOCK + column
    first = (WINDOW - LANES // 2) // 2
    return (place >= first) & (place < first + LANES // 2)


def stencil(weight, row, above, here, below, flux=None):
    columns = range(BLOCK)
    if flux is None:
        flux = [weight(1, row - 1, column) * (above[column] - here[column]) for column in columns]
    ahead = [weight(1, row, column) * (here[column] - below[column]) for column in columns]
    beside = here[1:] + [pltpu.roll(here[0], SUB - 1, 0)]
    side = [weight(2, row, column) * (here[column] - beside[column]) for column in columns]
    behind = [pltpu.roll(side[-1], 1, 0)] + side[:-1]
    applied = [
        weight(0, row, column) * here[column]
        + (ahead[column] - flux[column])
        + (side[column] - behind[column])
        for column in columns
    ]
    return applied, ahead


def passes(
    edge, own, total, source, weight, coef, step_ref, remain_ref, solved_ref, emit, border=None
):
    columns = range(BLOCK)

    for turn in range(CHEB + 1):
        first, last = edge + turn + 1, total - edge - turn - 1

        def load(row, turn=turn):
            if turn == 0:
                return [coef[1] * source(row, column) for column in columns]
            return [step_ref[row, column] for column in columns]

        above, here = load(first - 1), load(first)
        flux = None
        for row in range(first, last):
            below = load(row + 1)
            if border and row == first:
                border(0, turn, here)
            if border and row == last - 1:
                border(1, turn, here)
            applied, flux = stencil(weight, row, above, here, below, flux)
            inside = row in range(*own)
            results = []
            for column in columns:
                before = source(row, column) if turn == 0 else remain_ref[row, column]
                left = before - applied[column]
                if turn < CHEB:
                    remain_ref[row, column] = left
                    step_ref[row, column] = (
                        coef[2 + 2 * turn] * here[column] + coef[3 + 2 * turn] * left
                    )
                solved = None
                if inside:
                    place = row - own[0]
                    solved = here[column]
                    if turn > 0:
                        solved = solved_ref[place, column] + solved
                    if turn < CHEB:
                        solved_ref[place, column] = solved
                if turn == CHEB:
                    begun = source(row, column)
                    results.append((begun, solved, begun - left))
            if turn == CHEB:
                emit(row, *zip(*results))
            above, here = here, below


def add_products(sums, index, one, two):
    for column in range(BLOCK):
        product = one[column] * two[column]
        sums[index] = sums[index] + jnp.where(own_columns(column), product, 0.0)


def own_kernel(rows, local_ref, coef_ref, wide_ref, scratch_ref):
    lines = weight_lines([weight_part(local_ref, rows)], scratch_ref)
    coef = [coef_ref[0]]
    for row in range(rows):
        for plane in range(3):
            for column in range(BLOCK):
                value = jnp.zeros((SUB, LANES), jnp.float32)
                if plane != 1 or row < rows - 1:
                    value = spread(lines[column], plane * rows + row, plane, coef)
                wide_ref[row, plane * BLOCK + column] = value


def near_kernel(
    rows, top_ref, field_ref, bottom_ref, coef_ref, own_wide_ref,
    solved_ref, middle_ref, step_ref, remain_ref, border_ref, wide_ref, early_ref,
    part_ref, scratch_ref,
):
    parts = [
        weight_part(top_ref, rows),
        own_weight_part(field_ref, rows),
        weight_part(bottom_ref, rows),
    ]
    lines = weight_lines(parts, scratch_ref)
    places = near_places(rows)[0]
    coef = [coef_ref[index] for index in range(2 + 2 * CHEB)]
    total = 3 * rows + 2 * FAR
    own = (FAR + rows, FAR + 2 * rows)
    made = set()

    def weight(plane, row, column):
        place = plane * BLOCK + column
        if own[0] <= row < own[1] - (plane == 1):
            return own_wide_ref[row - own[0], place]
        if (row, place) not in made:
            made.add((row, place))
            wide_ref[row, place] = spread(lines[column], plane * 3 * rows + row - FAR, plane, coef)
        return wide_ref[row, place]

    def source(row, column):
        if row < own[0]:
            return received(top_ref, places, own[0] - row, column)
        if row >= own[1]:
            return received(bottom_ref, places, row - own[1] + 1, column)
        return field_ref[(row - own[0]) * BLOCK + column]

    sums = [jnp.zeros((SUB, LANES), jnp.float32) for _ in range(2)]

    def emit(row, begun, solved, applied):
        for column in range(BLOCK):
            middle_ref[row, column] = applied[column]
        if row in range(*own):
            for column in range(BLOCK):
                solved_ref[row - own[0], column] = solved[column]
            add_products(sums, 0, begun, solved)
            add_products(sums, 1, solved, applied)

    def border(side, turn, step):
        for column in range(BLOCK):
            border_ref[side, turn, column] = step[column]

    passes(
        FAR, own, total, source, weight, coef, step_ref, remain_ref, part_ref, emit, border
    )
    early_ref[0] = sums[0]
    early_ref[1] = sums[1]


def far_kernel(
    rows, top_far_ref, top_ref, field_ref, bottom_ref, bottom_far_ref, coef_ref,
    middle_ref, frozen_step_ref, frozen_remain_ref, border_ref, wide_ref, own_wide_ref, early_ref,
    solved_ref, applied_ref, sums_ref,
    step_ref, remain_ref, part_ref, outer_ref, scratch_ref,
):
    columns = range(BLOCK)
    parts = [
        weight_part(top_far_ref, FAR),
        weight_part(top_ref, rows),
        own_weight_part(field_ref, rows),
        weight_part(bottom_ref, rows),
        weight_part(bottom_far_ref, FAR),
    ]
    lines = weight_lines(parts, scratch_ref)
    coef = [coef_ref[index] for index in range(2 + 2 * CHEB)]
    total = 3 * rows + 2 * FAR
    own = (FAR + rows, FAR + 2 * rows)
    near, far = near_places(rows)[0], far_places(rows)[0]
    made = {}

    def weight(plane, row, column):
        if own[0] <= row < own[1] - (plane == 1):
            return own_wide_ref[row - own[0], plane * BLOCK + column]
        if FAR < row < total - FAR - 1 or (plane == 1 and row == FAR):
            return wide_ref[row, plane * BLOCK + column]
        key = (plane, row, column)
        if key not in made:
            made[key] = spread(lines[column], plane * total + row, plane, coef)
        return made[key]

    def source(row):
        distance = own[0] - row if row < own[0] else row - own[1] + 1
        if distance > rows:
            ref, places = (top_far_ref if row < own[0] else bottom_far_ref), far
        else:
            ref, places = (top_ref if row < own[0] else bottom_ref), near
        return [received(ref, places, distance, column) for column in columns]

    for side in range(2):

        def at(index, side=side):
            return total - 1 - index if side else index

        ends = [[coef[1] * value for value in source(at(index))] for index in range(FAR)]
        rest = source(at(1))
        for turn in range(CHEB + 1):
            edge_row = at(turn + 2)
            if turn == 0:
                inner = [coef[1] * value for value in source(edge_row)]
                inner_rest = source(edge_row)
            else:
                inner = [frozen_step_ref[edge_row, column] for column in columns]
                inner_rest = [frozen_remain_ref[edge_row, column] for column in columns]
            steps = ends + [inner, [border_ref[side, turn, column] for column in columns]]
            new_ends, new_rest = [], []
            for index, before in ((1, rest), (2, inner_rest)):
                row = at(turn + index)
                outside, inside = steps[index - 1], steps[index + 1]
                above, below = (inside, outside) if side else (outside, inside)
                here = steps[index]
                applied, _ = stencil(weight, row, above, here, below)
                left = [before[column] - applied[column] for column in columns]
                new_rest.append(left)
                if turn < CHEB:
                    new_ends.append(
                        [
                            coef[2 + 2 * turn] * here[column] + coef[3 + 2 * turn] * left[column]
                            for column in columns
                        ]
                    )
                else:
                    begun = source(row)
                    for column in columns:
                        outer_ref[side * FAR + index - 1, column] = begun[column] - left[column]
            ends, rest = new_ends, new_rest[1]

    def middle(row, column):
        index = min(row, total - 1 - row)
        if index < HALO + FAR:
            return outer_ref[FAR * (row > index) + index - HALO, column]
        return middle_ref[row, column]

    sums = [early_ref[0], early_ref[1]] + [jnp.zeros((SUB, LANES), jnp.float32) for _ in range(2)]

    def emit(row, begun, solved, applied):
        for column in columns:
            solved_ref[row - own[0], column] = solved[column]
            applied_ref[row - own[0], column] = applied[column]
        add_products(sums, 2, begun, solved)
        add_products(sums, 3, solved, applied)

    passes(HALO, own, total, middle, weight, coef, step_ref, remain_ref, part_ref, emit)

    lane = lane_index((1, LANES))
    line = jnp.zeros((1, LANES), jnp.float32)
    for index in range(4):
        line = jnp.where(lane == index, jnp.sum(sums[index]), line)
    sums_ref[...] = jnp.broadcast_to(line[None], sums_ref.shape)


def inverse_kernel(
    rows, times, length, cas_ref, sums_ref, one_ref, two_ref, three_ref, four_ref, out_ref, line_ref
):
    half = LANES // 2
    span = half + 2 * SIDE
    skip = (span - WINDOW) // 2
    line = jnp.sum(sums_ref[...].reshape(sums_ref.shape[0], LANES), axis=0, keepdims=True)
    gamma, curved, cross, last = (
        jnp.broadcast_to(line[:, index : index + 1], (SUB, LANES)) for index in range(4)
    )
    step = gamma / curved
    gamma_next = step * step * cross - gamma
    turn = gamma_next / gamma
    grown = 1.0 + turn
    next_curved = grown * grown * curved - 2.0 * step * grown * cross + step * step * last
    next_step = gamma_next / next_curved
    first = step + next_step * grown
    second = -next_step * step
    for row in range(rows):
        for index, (left_ref, right_ref) in enumerate(((one_ref, two_ref), (three_ref, four_ref))):
            offset = left_ref.shape[0] // 2 - rows // 2
            for column in range(BLOCK):
                start = (2 * row + index) * span + skip + column
                value = first * left_ref[offset + row, column] + second * right_ref[row, column]
                line_ref[pl.ds(start, SUB, stride=BLOCK), :] = value
    points = jnp.concatenate(
        [
            line_ref[index * span + SIDE : index * span + SIDE + half, :]
            for index in range(2 * rows)
        ],
        axis=0,
    )
    back = exact_dot(cas_ref[...], points, 1, 1)
    for row in range(rows):
        piece = back[:, row * LANES : (row + 1) * LANES].reshape(length // times, times, LANES)
        out_ref[:, row * times : (row + 1) * times, :] = piece


def final_kernel(rows, times, tiles, source_ref, field_ref, solution_ref, residual_ref):
    half = LANES // 2
    low = lane_index((rows, LANES)) < half
    for time in range(times):
        place = slice(time * rows, (time + 1) * rows)
        taken = pl.ds(time, rows, stride=times)
        for pair in range(tiles // 2):
            columns = slice(pair * LANES, (pair + 1) * LANES)
            left = source_ref[2 * pair, taken, :]
            right = source_ref[2 * pair + 1, taken, :]
            solution_ref[place, columns] = jnp.where(low, left, pltpu.roll(right, half, 1))
            change = jnp.where(low, pltpu.roll(left, half, 1), right)
            residual_ref[place, columns] = field_ref[place, columns] - change


def call(kernel, out_shape, scratch=()):
    shapes = [jax.ShapeDtypeStruct(shape, jnp.float32) for shape in out_shape]
    return pl.pallas_call(
        kernel,
        out_shape=shapes[0] if len(shapes) == 1 else shapes,
        scratch_shapes=[pltpu.VMEM(shape, jnp.float32) for shape in scratch],
        compiler_params=PARAMS,
    )


def shift(value, distance, spaces):
    return lax.ppermute(value, "space", [(i, (i + distance) % spaces) for i in range(spaces)])


def shards(right_side, kappa, velocity):
    tiles = lax.axis_size("tm")
    spaces = lax.axis_size("space")
    times, rows, width = right_side.shape
    length = times * tiles
    tile = width // tiles
    around = (LANES - tile) // 2
    cas_table = jnp.asarray(hartley_table(length))
    coef_table = jnp.asarray(chebyshev_table(length))

    field = right_side.reshape(times * rows, width)
    windows = call(
        functools.partial(window_kernel, rows, times, tiles),
        [(tiles, 6 * times, LANES)],
        [(width // LANES, times * rows, LANES)],
    )(field)
    gathered = lax.all_to_all(windows, "tm", 0, 0)

    squares = velocity.astype(jnp.float32) ** 2
    planes = jnp.concatenate([kappa, squares[0], squares[1]], axis=0)
    planes = jnp.concatenate([planes[:, -around:], planes, planes[:, :around]], axis=1)
    local = lax.dynamic_slice_in_dim(planes, lax.axis_index("tm") * tile, LANES, 1)
    own_wide = call(
        functools.partial(own_kernel, rows),
        [(rows, 3 * BLOCK, SUB, LANES)],
        [(LANES, LANES)],
    )(local, coef_table)

    total = 3 * rows + 2 * FAR
    tile_shape = (rows, BLOCK, SUB, LANES)
    near_shape = (near_places(rows)[1], LANES)
    far_shape = (far_places(rows)[1], LANES)
    span = LANES // 2 + 2 * SIDE
    freq, up, down, far_up, far_down = call(
        functools.partial(forward_kernel, rows, times, length),
        [(rows * BLOCK + 3, SUB, LANES), near_shape, near_shape, far_shape, far_shape],
        [(rows * span, LANES)],
    )(cas_table, gathered, local)
    top, bottom = shift(up, 1, spaces), shift(down, -1, spaces)
    top_far, bottom_far = shift(far_up, 2, spaces), shift(far_down, -2, spaces)

    work = (total, BLOCK, SUB, LANES)
    solved, middle, step, remain, border, wide, early = call(
        functools.partial(near_kernel, rows),
        [
            tile_shape,
            work,
            work,
            work,
            (2, CHEB + 1, BLOCK, SUB, LANES),
            (total, 3 * BLOCK, SUB, LANES),
            (2, SUB, LANES),
        ],
        [tile_shape, (LANES, LANES)],
    )(top, freq, bottom, coef_table, own_wide)
    solved_two, applied_two, sums = call(
        functools.partial(far_kernel, rows),
        [tile_shape, tile_shape, (tiles, 1, LANES)],
        [work, work, tile_shape, (2 * FAR, BLOCK, SUB, LANES), (LANES, LANES)],
    )(
        top_far, top, freq, bottom, bottom_far, coef_table, middle, step, remain, border, wide,
        own_wide, early,
    )
    sums = jnp.sum(lax.all_to_all(sums, "tm", 0, 0), axis=0)
    sums = lax.all_to_all(jnp.broadcast_to(sums[None], (spaces, 1, LANES)), "space", 0, 0)
    packed = call(
        functools.partial(inverse_kernel, rows, times, length),
        [(tiles, rows * times, LANES)],
        [(rows * 2 * span, LANES)],
    )(cas_table, sums, solved, solved_two, middle, applied_two)
    returned = lax.all_to_all(packed, "tm", 0, 0)

    solution, residual = call(
        functools.partial(final_kernel, rows, times, tiles),
        [(times * rows, width), (times * rows, width)],
    )(returned, field)
    shape = right_side.shape
    return solution.reshape(shape), residual.reshape(shape)


def solution(mesh):
    placed = (P("tm", "space", None), P("space", None), P(None, "space", None))
    return jax.shard_map(
        shards,
        mesh=mesh,
        in_specs=placed,
        out_specs=(P("tm", "space", None), P("tm", "space", None)),
        check_vma=False,
    )
```
